32 devices in a mesh: dp: 4 (over y, x), fsdp: 8 (over z, core).
Axes of the slice: x: 2, y: 2, z: 4, core: 2. Of those that a mesh axis runs over, the one named last changes fastest.
Arguments:
- history: float32 [65536, 3600], P(('dp', 'fsdp')), may hold values from -6 to 6
- later_observed: float32 [65536, 720], P(('dp', 'fsdp')), may hold values from -6 to 6
- lengths: int32 [65536], P(('dp', 'fsdp')), may hold values from 900 to 3600
- counted_flags: int32 [65536, 720], P(('dp', 'fsdp')), may hold values from 0 to 1
- series: int32 [65536], P(('dp', 'fsdp')), may hold values from 0 to 1022
- coarse_in: float32 [450, 512], P(None, 'fsdp'), may hold values from -0.25 to 0.25
- middle: float32 [4, 512, 512], P(None, None, 'fsdp'), may hold values from -0.25 to 0.25
- rough_final_matrix: float32 [512, 180], P('fsdp'), may hold values from -0.25 to 0.25
- fine_in: float32 [3600, 512], P(None, 'fsdp'), may hold values from -0.09375 to 0.09375
- sharp_final_matrix: float32 [512, 720], P('fsdp'), may hold values from -0.25 to 0.25
- offset_vectors: float32 [3972], replicated, may hold values from -0.3 to 0.3
- coarse_in_mean: float32 [450, 512], P(None, 'fsdp'), may hold values from -8.712071e-08 to 8.712071e-08
- middle_mean: float32 [4, 512, 512], P(None, None, 'fsdp'), may hold values from -1.7424142e-06 to 1.7424142e-06
- rough_final_first: float32 [512, 180], P('fsdp'), may hold values from -1.7424142e-06 to 1.7424142e-06
- fine_in_mean: float32 [3600, 512], P(None, 'fsdp'), may hold values from -1.7424142e-06 to 1.7424142e-06
- sharp_final_first: float32 [512, 720], P('fsdp'), may hold values from -1.7424142e-06 to 1.7424142e-06
- biases_mean: float32 [3972], replicated, may hold values from -5.280043e-06 to 5.280043e-06
- coarse_in_square: float32 [450, 512], P(None, 'fsdp'), may hold values from 6.969713e-17 to 2.7878853e-16
- middle_square: float32 [4, 512, 512], P(None, None, 'fsdp'), may hold values from 2.7878854e-14 to 1.1151542e-13
- rough_final_second: float32 [512, 180], P('fsdp'), may hold values from 2.7878854e-14 to 1.1151542e-13
- fine_in_square: float32 [3600, 512], P(None, 'fsdp'), may hold values from 2.7878854e-14 to 1.1151542e-13
- sharp_final_second: float32 [512, 720], P('fsdp'), may hold values from 2.7878854e-14 to 1.1151542e-13
- biases_square: float32 [3972], replicated, may hold values from 2.7878855e-13 to 1.1151542e-12
Outputs:
- loss_sum: float32 [], replicated
- usable_tally: float32 [], replicated
- grad_norm: float32 [], replicated
- new_coarse_in: float32 [450, 512], P(None, 'fsdp')
- new_middle: float32 [4, 512, 512], P(None, None, 'fsdp')
- new_coarse_out: float32 [512, 180], P('fsdp')
- new_fine_in: float32 [3600, 512], P(None, 'fsdp')
- new_fine_out: float32 [512, 720], P('fsdp')
- new_biases: float32 [3972], replicated
- new_coarse_in_mean: float32 [450, 512], P(None, 'fsdp')
- new_middle_mean: float32 [4, 512, 512], P(None, None, 'fsdp')
- new_coarse_out_mean: float32 [512, 180], P('fsdp')
- new_fine_in_mean: float32 [3600, 512], P(None, 'fsdp')
- new_fine_out_mean: float32 [512, 720], P('fsdp')
- new_biases_mean: float32 [3972], replicated
- new_coarse_in_square: float32 [450, 512], P(None, 'fsdp')
- new_middle_square: float32 [4, 512, 512], P(None, None, 'fsdp')
- new_coarse_out_square: float32 [512, 180], P('fsdp')
- new_fine_in_square: float32 [3600, 512], P(None, 'fsdp')
- new_fine_out_square: float32 [512, 720], P('fsdp')
- new_biases_square: float32 [3972], replicated
The draws below stay inside these ranges and needn't reach their ends.
All inputs are finite; a program needn't handle non-finite values.
Results may differ from the reference program's by a relative error of at most 0.0045.
Values may be sent and summed in bfloat16 or wider, within the bound.
No kernel may reach another device: no remote copies, remote signals or barrier semaphores. Data moves between devices by JAX's collectives and lax.ppermute only.
A program may use at most 256 MiB of HBM per device.

```python
import math
import jax
import jax.numpy as jnp
from jax import lax

LOOKBACK = 3600
OUTLOOK_LENGTH = 720
INNER_WIDTH = 512
POOL = 8
SERIES = 1024
STEP = 10
SAMPLES_LOCAL = 2048
LP = 450
HINDSIGHT_WTS = 150
OUTLOOK_WTS = 30
NB = 3972
MODEL_ENTRIES = 3586948
SAMPLE_TOTAL = 65536
N_DP = 4
N_FSDP = 8


def draw_counted_flags(key, part):
    key = jax.random.fold_in(key, 11)
    window_rows = lax.broadcasted_iota(jnp.int32, (SAMPLE_TOTAL, OUTLOOK_LENGTH), 0)
    limits = 1000 + 2000 * window_rows // SAMPLE_TOTAL
    picks = jax.random.randint(key, (SAMPLE_TOTAL, OUTLOOK_LENGTH), 0, 4000)
    return (picks < limits).astype(jnp.int32)


def touch_ends(result, own_key, low, largest):
    index_at = [jax.random.randint(jax.random.fold_in(own_key, axis), (), 0, length) for axis, length in enumerate(result.shape)]
    longest = result.shape.index(max(result.shape))
    next_to = index_at[:longest] + [(index_at[longest] + 1) % result.shape[longest]] + index_at[longest + 1:]
    return result.at[tuple(index_at)].set(low).at[tuple(next_to)].set(largest)


def block_scale(own_key, dims, split, low, largest):
    loudness = 1.0
    for position, shards_of in split:
        draws = jax.random.uniform(jax.random.fold_in(jax.random.fold_in(own_key, 6), position), (shards_of,), jnp.float32, low / len(split), largest / len(split))
        loudness = loudness * jnp.repeat(jnp.exp(draws), dims[position] // shards_of).reshape((-1,) + (1,) * (len(dims) - 1 - position))
    return loudness


def gaussian(own_key, shape, scale, bound, shards=(), kind=jnp.bfloat16):
    drawn = scale * jax.random.normal(own_key, shape, jnp.float32)
    if shards:
        drawn = drawn * block_scale(own_key, shape, shards, -0.22, 0.18)
    return jnp.clip(drawn, -bound, bound).astype(kind)


def setup_inputs(seed: int = 0) -> dict:
    splits = jax.random.split(jax.random.key(seed), 24)
    return {
        "history": gaussian(splits[0], (SAMPLE_TOTAL, LOOKBACK), 1.0, 6.0, ((0, 32),), jnp.float32),
        "later_observed": gaussian(splits[1], (SAMPLE_TOTAL, OUTLOOK_LENGTH), 1.0, 6.0, ((0, 32),), jnp.float32),
        "lengths": touch_ends(jax.random.randint(splits[2], (SAMPLE_TOTAL,), LOOKBACK // 4, LOOKBACK + 1), jax.random.fold_in(splits[2], 1), LOOKBACK // 4, LOOKBACK).astype(jnp.int32),
        "counted_flags": draw_counted_flags(jax.random.fold_in(splits[23], 71), 0),
        "series": touch_ends(jax.random.randint(splits[4], (SAMPLE_TOTAL,), 0, SERIES - 1), jax.random.fold_in(splits[4], 1), 0, (SERIES - 1) - 1).astype(jnp.int32),
        "coarse_in": gaussian(splits[5], (LP, INNER_WIDTH), LP ** -0.5, 0.25, ((1, 8),), jnp.float32),
        "middle": gaussian(splits[6], (4, INNER_WIDTH, INNER_WIDTH), INNER_WIDTH ** -0.5, 0.25, ((2, 8),), jnp.float32),
        "rough_final_matrix": gaussian(splits[7], (INNER_WIDTH, HINDSIGHT_WTS + OUTLOOK_WTS), INNER_WIDTH ** -0.5, 0.25, ((0, 8),), jnp.float32),
        "fine_in": gaussian(splits[8], (LOOKBACK, INNER_WIDTH), LOOKBACK ** -0.5, 0.09375, ((1, 8),), jnp.float32),
        "sharp_final_matrix": gaussian(splits[9], (INNER_WIDTH, OUTLOOK_LENGTH), INNER_WIDTH ** -0.5, 0.25, ((0, 8),), jnp.float32),
        "offset_vectors": gaussian(splits[10], (NB,), 0.05, 0.3, (), jnp.float32),
        "coarse_in_mean": gaussian(splits[11], (LP, INNER_WIDTH), (0.0055 * 0.01 / MODEL_ENTRIES ** 0.5), 8.712071064564952e-08, ((1, 8),), jnp.float32),
        "middle_mean": gaussian(splits[12], (4, INNER_WIDTH, INNER_WIDTH), (0.11 * 0.01 / MODEL_ENTRIES ** 0.5), 1.7424141560695716e-06, ((2, 8),), jnp.float32),
        "rough_final_first": gaussian(splits[13], (INNER_WIDTH, HINDSIGHT_WTS + OUTLOOK_WTS), (0.11 * 0.01 / MODEL_ENTRIES ** 0.5), 1.7424141560695716e-06, ((0, 8),), jnp.float32),
        "fine_in_mean": gaussian(splits[14], (LOOKBACK, INNER_WIDTH), (0.11 * 0.01 / MODEL_ENTRIES ** 0.5), 1.7424141560695716e-06, ((1, 8),), jnp.float32),
        "sharp_final_first": gaussian(splits[15], (INNER_WIDTH, OUTLOOK_LENGTH), (0.11 * 0.01 / MODEL_ENTRIES ** 0.5), 1.7424141560695716e-06, ((0, 8),), jnp.float32),
        "biases_mean": gaussian(splits[16], (NB,), (0.33 * 0.01 / MODEL_ENTRIES ** 0.5), 5.280042842059629e-06, (), jnp.float32),
        "coarse_in_square": jnp.clip(jnp.exp(math.log(2.7878853320167896e-16) - 1.3862944 * jax.random.uniform(splits[17], (LP, INNER_WIDTH), jnp.float32) ** block_scale(splits[17], (LP, INNER_WIDTH), ((1, 8),), -0.2, 0.2)), 6.969713330041974e-17, 2.7878853320167896e-16),
        "middle_square": jnp.clip(jnp.exp(math.log(1.115154179393528e-13) - 1.3862944 * jax.random.uniform(splits[18], (4, INNER_WIDTH, INNER_WIDTH), jnp.float32) ** block_scale(splits[18], (4, INNER_WIDTH, INNER_WIDTH), ((2, 8),), -0.2, 0.2)), 2.78788544848382e-14, 1.115154179393528e-13),
        "rough_final_second": jnp.clip(jnp.exp(math.log(1.115154179393528e-13) - 1.3862944 * jax.random.uniform(splits[19], (INNER_WIDTH, HINDSIGHT_WTS + OUTLOOK_WTS), jnp.float32) ** block_scale(splits[19], (INNER_WIDTH, HINDSIGHT_WTS + OUTLOOK_WTS), ((0, 8),), -0.2, 0.2)), 2.78788544848382e-14, 1.115154179393528e-13),
        "fine_in_square": jnp.clip(jnp.exp(math.log(1.115154179393528e-13) - 1.3862944 * jax.random.uniform(splits[20], (LOOKBACK, INNER_WIDTH), jnp.float32) ** block_scale(splits[20], (LOOKBACK, INNER_WIDTH), ((1, 8),), -0.2, 0.2)), 2.78788544848382e-14, 1.115154179393528e-13),
        "sharp_final_second": jnp.clip(jnp.exp(math.log(1.115154179393528e-13) - 1.3862944 * jax.random.uniform(splits[21], (INNER_WIDTH, OUTLOOK_LENGTH), jnp.float32) ** block_scale(splits[21], (INNER_WIDTH, OUTLOOK_LENGTH), ((0, 8),), -0.2, 0.2)), 2.78788544848382e-14, 1.115154179393528e-13),
        "biases_square": jnp.clip(jnp.exp(jax.random.uniform(splits[22], (NB,), jnp.float32, math.log(2.787885482365138e-13), math.log(1.1151541929460551e-12))), 2.787885482365138e-13, 1.1151541929460551e-12),
    }


exact_matmul_mode = lax.Precision.HIGHEST
beta_first = 0.9
beta_second = 0.999
learn_rate = 0.01
weight_decay = 0.01
adam_epsilon = 1e-08
clip_level = 0.01

@jax.custom_vjp
def low(v):
    return lax.optimization_barrier(v.astype(jnp.bfloat16)).astype(jnp.float32)

@jax.custom_vjp
def low_back(v):
    return v

def low_keep(v):
    return (low(v), None)

def low_pass(kept, grad):
    return (grad,)

def back_keep(v):
    return (v, None)

def back_low(kept, grad):
    return (low(grad),)
low.defvjp(low_keep, low_pass)
low_back.defvjp(back_keep, back_low)

def blending_grid(count, length):
    spots = (jnp.arange(length, dtype=jnp.float32) + 0.5) * (count / length) - 0.5
    spots = jnp.clip(spots, 0.0, count - 1.0)
    knots = jnp.arange(count, dtype=jnp.float32)
    return jnp.maximum(0.0, 1.0 - jnp.abs(spots[None, :] - knots[:, None]))

def split_offsets(offset_vectors):
    hidden_bias = offset_vectors[:6 * INNER_WIDTH].reshape(6, INNER_WIDTH)
    rough_final_part = offset_vectors[6 * INNER_WIDTH:6 * INNER_WIDTH + HINDSIGHT_WTS + OUTLOOK_WTS]
    sharp_final_part = offset_vectors[6 * INNER_WIDTH + HINDSIGHT_WTS + OUTLOOK_WTS:]
    return ((hidden_bias[0], hidden_bias[1], hidden_bias[2], rough_final_part), (hidden_bias[3], hidden_bias[4], hidden_bias[5], sharp_final_part))

def dense(inputs, weight, offset):
    return low_back(jnp.dot(low(inputs), low(weight), precision=exact_matmul_mode) + offset)

def run_stack(entering, mats, offsets):
    current = entering
    for layer_at in range(4):
        current = dense(current, mats[layer_at], offsets[layer_at])
        if layer_at < 3:
            current = jax.nn.silu(current)
    return current

def block_loss(params, fragment):
    coarse_in, middle, rough_final_matrix, fine_in, sharp_final_matrix, offset_vectors = params
    rescaled_input, goal_entries, observed_history, outlook_extent = fragment
    coarse_offsets, fine_offsets = split_offsets(offset_vectors)
    rows_here = rescaled_input.shape[0]
    pooled = lax.optimization_barrier(jnp.mean(rescaled_input.reshape(rows_here, LP, POOL), axis=2))
    knot_weights = run_stack(pooled, (coarse_in, middle[0], middle[1], rough_final_matrix), coarse_offsets)
    backcast = jnp.dot(knot_weights[:, :HINDSIGHT_WTS], blending_grid(HINDSIGHT_WTS, LOOKBACK), precision=exact_matmul_mode)
    residue = (rescaled_input - backcast) * observed_history
    refined_entry = run_stack(residue, (fine_in, middle[2], middle[3], sharp_final_matrix), fine_offsets)
    estimate_output = jnp.dot(knot_weights[:, HINDSIGHT_WTS:], blending_grid(OUTLOOK_WTS, OUTLOOK_LENGTH), precision=exact_matmul_mode) + refined_entry
    misfit_amount = (estimate_output - goal_entries) * outlook_extent
    return jnp.sum(misfit_amount * misfit_amount)

def adam_step(weight, mean_old, square_old, grad, factor):
    clipped = grad * factor
    mean_new = beta_first * mean_old + (1.0 - beta_first) * clipped
    square_new = beta_second * square_old + (1.0 - beta_second) * clipped * clipped
    mean_hat = mean_new / (1.0 - beta_first ** STEP)
    square_hat = square_new / (1.0 - beta_second ** STEP)
    weight_new = weight - learn_rate * (mean_hat / (jnp.sqrt(square_hat) + adam_epsilon) + weight_decay * weight)
    return (weight_new, mean_new, square_new)

def reference(history, later_observed, lengths, counted_flags, series, coarse_in, middle, rough_final_matrix, fine_in, sharp_final_matrix, offset_vectors, coarse_in_mean, middle_mean, rough_final_first, fine_in_mean, sharp_final_first, biases_mean, coarse_in_square, middle_square, rough_final_second, fine_in_square, sharp_final_second, biases_square):
    steps_iota = lax.broadcasted_iota(jnp.int32, history.shape, 1)
    observed_history = (steps_iota >= LOOKBACK - lengths[:, None]).astype(jnp.float32)
    masked = history * observed_history
    row_terms = jnp.stack([lax.optimization_barrier(jnp.sum(masked, 1)), lax.optimization_barrier(jnp.sum(masked * history, 1)), lax.optimization_barrier(jnp.sum(observed_history, 1))], 1)
    one_hot = (series[:, None] == lax.broadcasted_iota(jnp.int32, (1, SERIES), 1)).astype(jnp.float32)
    table = jnp.einsum('ws,wk->sk', one_hot, row_terms, precision=exact_matmul_mode)
    counted = jnp.maximum(table[:, 2], 1.0)
    centre = table[:, 0] / counted
    spread = jnp.sqrt(table[:, 1] / counted + 1e-05)
    looked = jnp.dot(one_hot, jnp.stack([centre, spread], 1), precision=exact_matmul_mode)
    rescaled_input = (history - looked[:, 0:1]) / looked[:, 1:2] * observed_history
    goal_entries = (later_observed - looked[:, 0:1]) / looked[:, 1:2]
    outlook_extent = counted_flags.astype(jnp.float32)
    usable_tally = jnp.sum(outlook_extent)
    module_list = N_DP * N_FSDP
    fragment_list = (rescaled_input.reshape(module_list, SAMPLES_LOCAL, LOOKBACK), goal_entries.reshape(module_list, SAMPLES_LOCAL, OUTLOOK_LENGTH), observed_history.reshape(module_list, SAMPLES_LOCAL, LOOKBACK), outlook_extent.reshape(module_list, SAMPLES_LOCAL, OUTLOOK_LENGTH))
    params = (coarse_in, middle, rough_final_matrix, fine_in, sharp_final_matrix, offset_vectors)

    def total_loss(weights):

        def advance(total, fragment):
            return (total + jax.checkpoint(block_loss)(weights, fragment), None)
        total, _ = lax.scan(advance, jnp.zeros((), jnp.float32), fragment_list)
        return total
    loss_sum, pull = jax.vjp(total_loss, params)
    grads = pull(1.0 / usable_tally)[0]
    total_square = jnp.zeros((), jnp.float32)
    for grad in grads:
        total_square = total_square + jnp.sum(grad * grad)
    grad_norm = jnp.sqrt(total_square)
    factor = clip_level / jnp.maximum(grad_norm, clip_level)
    means = (coarse_in_mean, middle_mean, rough_final_first, fine_in_mean, sharp_final_first, biases_mean)
    squares = (coarse_in_square, middle_square, rough_final_second, fine_in_square, sharp_final_second, biases_square)
    results = [adam_step(params[item], means[item], squares[item], grads[item], factor) for item in range(6)]
    return (loss_sum, usable_tally, grad_norm, results[0][0], results[1][0], results[2][0], results[3][0], results[4][0], results[5][0], results[0][1], results[1][1], results[2][1], results[3][1], results[4][1], results[5][1], results[0][2], results[1][2], results[2][2], results[3][2], results[4][2], results[5][2])
```

```python
import jax
import jax.numpy as jnp
import numpy as np
from jax import lax
from jax.experimental import pallas as pl
from jax.experimental.pallas import tpu as pltpu
from jax.sharding import PartitionSpec as P

LOOKBACK = 3600
OUTLOOK = 720
HID = 512
SERIES = 1024
STEP = 10
LP = 450
BACK = 150
FORE = 30
RATIO = 24
beta_first = 0.9
beta_second = 0.999
learn_rate = 0.01
weight_decay = 0.01
adam_epsilon = 1e-08
clip_level = 0.01

C_IN, C_M0, C_M1, C_OUT, C_ALL = 0, 512, 1024, 1536, 1792
F_IN, F_M2, F_M3, F_OUT, F_ALL = 0, 3840, 4352, 4864, 5632
T_PAD = 3840
T_LIVE = 3712
T_WHOLE = 3584
O_PAD = 768
TILE = 256
CINV_AT = 180

F32 = jnp.float32
BF16 = jnp.bfloat16
NN = (((1,), (0,)), ((), ()))
NT = (((1,), (1,)), ((), ()))
TN = (((0,), (0,)), ((), ()))


def mm(a, b, dims=NN):
    return lax.dot_general(a, b, dims, preferred_element_type=F32)


def iota(shape, axis):
    return lax.broadcasted_iota(jnp.int32, shape, axis)


def split3(v):
    hi = v.astype(BF16)
    rest = v - hi.astype(F32)
    mid = rest.astype(BF16)
    return hi, mid, (rest - mid.astype(F32)).astype(BF16)


def mm_exact(v, sel, dims=NN):
    hi, mid, low = split3(v)
    return mm(hi, sel, dims) + mm(mid, sel, dims) + mm(low, sel, dims)


def mm_exact2(sel, v, dims=NN):
    hi, mid, low = split3(v)
    return mm(sel, hi, dims) + mm(sel, mid, dims) + mm(sel, low, dims)


def sigmoid(v):
    return 1.0 / (1.0 + jnp.exp(-v))


def silu(v):
    return v * sigmoid(v)


def silu_slope(v):
    s = sigmoid(v)
    return s * (1.0 + v * (1.0 - s))


def vmem(limit=60):
    return pltpu.CompilerParams(vmem_limit_bytes=limit * 1024 * 1024)


def bits_of(size):
    return [1 << b for b in range(size.bit_length() - 1)]


def swap(x, dp, fsdp, bit_dp, bit_fsdp):
    pairs = []
    for d in range(dp):
        for f in range(fsdp):
            pairs.append((d * fsdp + f, (d ^ bit_dp) * fsdp + (f ^ bit_fsdp)))
    return lax.ppermute(x, ("dp", "fsdp"), pairs)


def gather_rows(x, dp, fsdp, swap_fn, join):
    far = bits_of(fsdp)
    for bit in reversed(far[1:]):
        x = join(x, swap_fn(x, 0, bit))
    half = x.shape[0] // 2
    a, b = x[:half], x[half:]
    for first, second in zip(reversed(bits_of(dp)), bits_of(dp)):
        a2 = swap_fn(a, first, 0)
        b2 = swap_fn(b, second, 0)
        a, b = join(a, a2), join(b, b2)
    x = join(a, b)
    return join(x, swap_fn(x, 0, far[0]))


def row_order(dp, fsdp):
    share = HID // fsdp
    part = share // dp
    start = np.arange(part)

    def shifted(x, bit_dp, bit_fsdp):
        return x ^ (bit_fsdp * share + bit_dp * part)

    return gather_rows(
        start, dp, fsdp, shifted, lambda p, q: np.concatenate([p, q])
    )


def pack_kernel(d_ref, cin, mid, cout, fin, fout, wc, wf):
    share = cout.shape[0]
    part = wc.shape[0]
    rows = max(part, 16)
    sel = (iota((rows, share), 1) == d_ref[0] * part + iota((rows, share), 0)).astype(BF16)
    wc[...] = jnp.zeros_like(wc)
    wf[...] = jnp.zeros_like(wf)

    def put(ref, at, value):
        picked = mm(sel, value.astype(BF16))
        ref[:, at : at + value.shape[1]] = picked[:part].astype(BF16)

    put(wc, C_IN, cin[...])
    put(wc, C_M0, mid[0])
    put(wc, C_M1, mid[1])
    put(wc, C_OUT, cout[...])
    put(wf, F_IN, fin[...])
    put(wf, F_M2, mid[2])
    put(wf, F_M3, mid[3])
    put(wf, F_OUT, fout[...])


def stats_kernel(hist, lens, series, pooled, table):
    cols = hist.shape[1]

    @pl.when(pl.program_id(0) == 0)
    def _():
        table[...] = jnp.zeros_like(table)

    begin = LOOKBACK - lens[...]
    sums = jnp.zeros((8, cols), F32)
    squares = jnp.zeros((8, cols), F32)
    chunk = 32
    base = iota((chunk, cols), 0) * 8
    for g in range(0, LP - chunk + 1, chunk):
        total = jnp.zeros((chunk, cols), F32)
        for s in range(8):
            h = hist[pl.ds(g * 8 + s, chunk, stride=8), :]
            h = jnp.where(base >= begin - (g * 8 + s), h, 0.0)
            total += h
            sq = h * h
            for v in range(chunk // 8):
                squares += sq[v * 8 : v * 8 + 8]
        for v in range(chunk // 8):
            sums += total[v * 8 : v * 8 + 8]
        pooled[g : g + chunk, :] = total * 0.125
    at = LP // chunk * chunk
    rest = LP - at
    pooled[at:HID, :] = jnp.zeros((HID - at, cols), F32)
    total = jnp.zeros((rest, cols), F32)
    rest_squares = jnp.zeros((rest, cols), F32)
    for s in range(8):
        h = hist[pl.ds(at * 8 + s, rest, stride=8), :]
        h = jnp.where(iota((rest, cols), 0) * 8 >= begin - (at * 8 + s), h, 0.0)
        total += h
        rest_squares += h * h
    pooled[at:LP, :] = total * 0.125
    sum_row = jnp.sum(sums, 0, keepdims=True) + jnp.sum(total, 0, keepdims=True)
    square_row = jnp.sum(squares, 0, keepdims=True) + jnp.sum(rest_squares, 0, keepdims=True)
    row = iota((16, cols), 0)
    kind = row % 3
    v = jnp.where(
        kind == 0, sum_row, jnp.where(kind == 1, square_row, lens[...].astype(F32))
    )
    hi, mid, low = split3(v)
    piece = jnp.where(
        row < 3,
        hi.astype(F32),
        jnp.where(row < 6, mid.astype(F32), jnp.where(row < 9, low.astype(F32), 0.0)),
    ).astype(BF16)
    hot = (iota((SERIES, cols), 0) == series[...]).astype(BF16)
    t = mm(piece, hot, NT)
    table[0:3, :] += t[0:3] + t[3:6] + t[6:9]


def coarse_kernel(p_in, lens, series, table, wc, offs, abscol, z_out, pooled_out, th_out,
                  look_out, looker, m0, m1, w_out, offs_p):
    cols = p_in.shape[1]

    @pl.when(pl.program_id(0) == 0)
    def _():
        perm = (iota((HID, HID), 1) == abscol[...]).astype(BF16)
        m0[...] = mm(wc[:, C_M0 : C_M0 + HID], perm, NT).astype(BF16)
        m1[...] = mm(wc[:, C_M1 : C_M1 + HID], perm, NT).astype(BF16)
        eye = (iota((256, 256), 0) == iota((256, 256), 1)).astype(BF16)
        w_out[...] = mm(eye, wc[:, C_OUT:C_ALL], NT).astype(BF16)
        offs_p[...] = mm_exact2(perm, offs[0:HID, :])
        count = jnp.maximum(table[2:3, :], 1.0)
        centre = table[0:1, :] / count
        spread = jnp.sqrt(table[1:2, :] / count + 1e-05)
        inverse = 1.0 / spread
        shifted = centre / spread
        row = iota((16, SERIES), 0)
        v = jnp.where(row < 3, inverse, shifted)
        hi, mid, low = split3(v)
        kind = row % 3
        looker[...] = jnp.where(
            row < 6,
            jnp.where(
                kind == 0,
                hi.astype(F32),
                jnp.where(kind == 1, mid.astype(F32), low.astype(F32)),
            ),
            0.0,
        ).astype(BF16)

    hot = (iota((SERIES, cols), 0) == series[...]).astype(BF16)
    got = mm(looker[...], hot)
    inv = got[0:1] + got[1:2] + got[2:3]
    cinv = got[3:4] + got[4:5] + got[5:6]
    look_out[...] = jnp.where(iota((8, cols), 0) == 0, inv, cinv)
    group = iota((HID, cols), 0)
    begin = LOOKBACK - lens[...]
    share = jnp.clip(group * 8 + 8 - begin, 0, 8).astype(F32) * 0.125
    pooled = jnp.where(group < LP, p_in[...] * inv - cinv * share, 0.0).astype(BF16)
    pooled_out[...] = pooled
    z = mm(wc[:, C_IN : C_IN + HID], pooled) + offs_p[:, 0:1]
    z_out[0:HID, :] = z
    z = mm(m0[...], silu(z).astype(BF16)) + offs_p[:, 1:2]
    z_out[HID : 2 * HID, :] = z
    z = mm(m1[...], silu(z).astype(BF16)) + offs_p[:, 2:3]
    z_out[2 * HID : 3 * HID, :] = z
    theta = mm(w_out[...], silu(z).astype(BF16)) + offs[0:256, 3:4]
    theta = theta * (1.0 / 48.0)
    hi = theta.astype(BF16).astype(F32)
    at = iota((256, cols), 0)
    c_hi, c_mid, c_low = split3(cinv)
    with_shift = jnp.where(
        at == CINV_AT,
        c_hi.astype(F32),
        jnp.where(
            at == CINV_AT + 1,
            c_mid.astype(F32),
            jnp.where(at == CINV_AT + 2, c_low.astype(F32), hi),
        ),
    )
    th_out[0:256, :] = with_shift.astype(BF16)
    th_out[256:512, :] = (theta - hi).astype(BF16)


def fold_lanes(x):
    total = x[:, 0:128]
    for at in range(128, x.shape[1], 128):
        total = total + x[:, at : at + 128]
    return total


def hidden_rows(acc, perm):
    lane = iota((HID, 128), 1)
    v = jnp.zeros((HID, 128), F32)
    for k in range(3):
        v = jnp.where(lane == k, jnp.sum(acc[k], 1, keepdims=True), v)
    return mm_exact(v, perm, TN)[0:8]


def last_row(acc):
    v = jnp.broadcast_to(jnp.sum(acc, 1, keepdims=True), acc.shape)
    return jnp.transpose(v, (1, 0))[0:8]


def fine_kernel(hist, later, flags, look, lens, th, wf, btab_t, ftab, ftab_t, offs, abscol,
                dz1_out, fore_out, keep, send, small,
                res, a1, a2, a3, dz1, dz2, dz3, dz4, m2, m3, m2_t, m3_t, w_out, offs_p, perm,
                acc, acc4, acc_loss, grad):
    cols = hist.shape[1]
    tiles = res.shape[1] // cols
    step = pl.program_id(0)

    @pl.when(step == 0)
    def _():
        p = (iota((HID, HID), 1) == abscol[...]).astype(BF16)
        perm[...] = p
        m2[...] = mm(wf[:, F_M2 : F_M2 + HID], p, NT).astype(BF16)
        m3[...] = mm(wf[:, F_M3 : F_M3 + HID], p, NT).astype(BF16)
        m2_t[...] = mm(p, wf[:, F_M2 : F_M2 + HID], NT).astype(BF16)
        m3_t[...] = mm(p, wf[:, F_M3 : F_M3 + HID], NT).astype(BF16)
        eye = (iota((256, 256), 0) == iota((256, 256), 1)).astype(BF16)
        for lo in range(0, O_PAD, 256):
            w_out[lo : lo + 256, :] = mm(
                eye, wf[:, F_OUT + lo : F_OUT + lo + 256], NT
            ).astype(BF16)
        offs_p[...] = mm_exact2(p, offs[0:HID, :])
        acc[...] = jnp.zeros_like(acc)
        acc4[...] = jnp.zeros_like(acc4)
        acc_loss[...] = jnp.zeros_like(acc_loss)
        res[LOOKBACK:T_PAD, :] = jnp.zeros((T_PAD - LOOKBACK, res.shape[1]), BF16)
        dz4[OUTLOOK:O_PAD, :] = jnp.zeros((O_PAD - OUTLOOK, dz4.shape[1]), BF16)

    @pl.when(step < tiles)
    def _():
        here = pl.ds(pl.multiple_of(step * cols, cols), cols)
        inv = look[0:1, :]
        cinv = look[1:2, :]
        begin = LOOKBACK - lens[...]
        th_hi = th[0:256, :]
        for lo in range(0, LOOKBACK, 512):
            width = min(512, LOOKBACK - lo)
            shift = mm(btab_t[lo : lo + width, :], th_hi)
            seen = iota((width, cols), 0) >= begin - lo
            r = jnp.where(seen, hist[lo : lo + width, :] * inv - shift, 0.0)
            res[lo : lo + width, here] = r.astype(BF16)
        z1 = mm(wf[:, F_IN : F_IN + T_LIVE], res[0:T_LIVE, here]) + offs_p[:, 0:1]
        v1 = silu(z1).astype(BF16)
        a1[:, here] = v1
        z2 = mm(m2[...], v1) + offs_p[:, 1:2]
        v2 = silu(z2).astype(BF16)
        a2[:, here] = v2
        z3 = mm(m3[...], v2) + offs_p[:, 2:3]
        v3 = silu(z3).astype(BF16)
        a3[:, here] = v3
        est = (
            mm(w_out[...], v3)
            + mm(ftab_t[...], th_hi)
            + mm(ftab_t[...], th[256:512, :])
            + offs[:, 3:4]
        )
        counted = flags[...].astype(F32)
        err = (est[0:OUTLOOK] - (later[...] * inv - cinv)) * counted
        acc_loss[0:1, :] += jnp.sum(err * err, 0, keepdims=True)
        acc_loss[1:2, :] += jnp.sum(counted, 0, keepdims=True)
        d4 = (2.0 * err).astype(BF16)
        acc4[0:OUTLOOK, :] += fold_lanes(d4.astype(F32))
        dz4[0:OUTLOOK, here] = d4
        d4 = dz4[:, here]
        fore_out[...] = mm(ftab[...], d4) * (1.0 / 48.0)

        def back(upstream, z, slot, row):
            d = (upstream * silu_slope(z)).astype(BF16)
            acc[row] += fold_lanes(d.astype(F32))
            slot[:, here] = d
            return d

        d3 = back(mm(wf[:, F_OUT:F_ALL], d4), z3, dz3, 2)
        d2 = back(mm(m3_t[...], d3), z2, dz2, 1)
        dz1_out[...] = back(mm(m2_t[...], d2), z1, dz1, 0)

    emit_tiles(step - tiles, keep, send, grad, perm, T_PAD // TILE,
               (dz1, res), (dz2, a1), (dz3, a2), (a3, dz4))

    @pl.when(step == pl.num_programs(0) - 1)
    def _():
        small[...] = last_row(acc4[...])
        loss = jnp.sum(acc_loss[0:1, :], 1, keepdims=True)
        tally = jnp.sum(acc_loss[1:2, :], 1, keepdims=True)
        row = iota((8, O_PAD), 0)
        small[...] = jnp.where(
            row == 3,
            small[...],
            jnp.where(row == 4, loss, jnp.where(row == 5, tally, 0.0)),
        )
        small[0:3, 0:HID] = hidden_rows(acc, perm[...])[0:3]


def emit_tiles(at, keep, send, grad, perm, in_tiles, first, second, third, fourth):
    half = HID // 2

    def emit(g):
        keep[...] = g[0:half]
        send[...] = g[half:HID].astype(BF16)

    @pl.when((at >= 0) & (at < in_tiles))
    def _():
        lo = pl.multiple_of(at * TILE, TILE)
        emit(mm(first[0][...], first[1][pl.ds(lo, TILE), :], NT))

    for index, (lhs, rhs) in enumerate((second, third)):

        @pl.when(at == in_tiles + 2 * index)
        def _():
            hi, mid, low = split3(mm(lhs[...], rhs[...], NT))
            grad[0] = hi
            grad[1] = mid
            grad[2] = low

        @pl.when((at >= in_tiles + 2 * index) & (at < in_tiles + 2 * index + 2))
        def _():
            lo = pl.multiple_of((at - in_tiles - 2 * index) * TILE, TILE)
            p = perm[:, pl.ds(lo, TILE)]
            emit(mm(grad[0], p) + mm(grad[1], p) + mm(grad[2], p))

    @pl.when(at >= in_tiles + 4)
    def _():
        lo = pl.multiple_of((at - in_tiles - 4) * TILE, TILE)
        emit(mm(fourth[0][...], fourth[1][pl.ds(lo, TILE), :], NT))


def back_kernel(dz1f, fore, lens, z, pooled_in, wf, btab, wc, abscol,
                keep, send, small,
                pooled, a1, a2, a3, dz1, dz2, dz3, dz4, w_in, m0_t, m1_t, perm, acc, acc4, grad):
    cols = dz1f.shape[1]
    tiles = pooled.shape[1] // cols
    step = pl.program_id(0)

    @pl.when(step == 0)
    def _():
        p = (iota((HID, HID), 1) == abscol[...]).astype(BF16)
        perm[...] = p
        m0_t[...] = mm(p, wc[:, C_M0 : C_M0 + HID], NT).astype(BF16)
        m1_t[...] = mm(p, wc[:, C_M1 : C_M1 + HID], NT).astype(BF16)
        eye = (iota((256, 256), 0) == iota((256, 256), 1)).astype(BF16)
        for lo in range(0, T_PAD, 256):
            w_in[lo : lo + 256, :] = mm(eye, wf[:, lo : lo + 256], NT).astype(BF16)
        acc[...] = jnp.zeros_like(acc)
        acc4[...] = jnp.zeros_like(acc4)

    @pl.when(step < tiles)
    def _():
        here = pl.ds(pl.multiple_of(step * cols, cols), cols)
        begin = LOOKBACK - lens[...]
        d1f = dz1f[...]
        total = jnp.zeros((256, cols), F32)
        for lo in range(0, T_LIVE, 512):
            width = min(512, T_LIVE - lo)
            d = mm(w_in[lo : lo + width, :], d1f)
            seen = iota((width, cols), 0) >= begin - lo
            d = jnp.where(seen, d, 0.0).astype(BF16)
            total += mm(btab[:, lo : lo + width], d)
        row = iota((256, cols), 0)
        d4 = (jnp.where(row < BACK, total * (-1.0 / 48.0), 0.0) + fore[...]).astype(BF16)
        dz4[:, here] = d4
        acc4[...] += fold_lanes(d4.astype(F32))
        pooled[:, here] = pooled_in[...]
        z1 = z[0:HID, :]
        z2 = z[HID : 2 * HID, :]
        z3 = z[2 * HID : 3 * HID, :]
        a1[:, here] = silu(z1).astype(BF16)
        a2[:, here] = silu(z2).astype(BF16)
        a3[:, here] = silu(z3).astype(BF16)

        def back(upstream, zz, slot, row):
            d = (upstream * silu_slope(zz)).astype(BF16)
            acc[row] += fold_lanes(d.astype(F32))
            slot[:, here] = d
            return d

        d3 = back(mm(wc[:, C_OUT:C_ALL], d4), z3, dz3, 2)
        d2 = back(mm(m1_t[...], d3), z2, dz2, 1)
        back(mm(m0_t[...], d2), z1, dz1, 0)

    emit_tiles(step - tiles, keep, send, grad, perm, HID // TILE,
               (dz1, pooled), (dz2, a1), (dz3, a2), (a3, dz4))

    @pl.when(step == pl.num_programs(0) - 1)
    def _():
        small[...] = jnp.zeros_like(small)
        small[0:3, :] = hidden_rows(acc, perm[...])[0:3]
        small[3:4, 0:256] = last_row(acc4[...])[0:1]


def adam_math(weight, mean_old, square_old, grad):
    mean_new = beta_first * mean_old + (1.0 - beta_first) * grad
    square_new = beta_second * square_old + (1.0 - beta_second) * grad * grad
    mean_hat = mean_new / (1.0 - beta_first**STEP)
    square_hat = square_new / (1.0 - beta_second**STEP)
    weight_new = weight - learn_rate * (
        mean_hat / (jnp.sqrt(square_hat) + adam_epsilon) + weight_decay * weight
    )
    return weight_new, mean_new, square_new


def adam_kernel(scale, gc, gf, relrow, *refs):
    ins, outs = refs[:15], refs[15:]
    share = gc.shape[0]
    s = scale[0, 0]
    place = (iota((share, share), 1) == relrow[...]).astype(BF16)

    def step(i, part, at, width, index):
        grad = mm_exact2(place, part[:, at : at + width], TN) * s
        old = [ins[i + 5 * k][index] for k in range(3)]
        for k, value in enumerate(adam_math(*old, grad)):
            outs[i + 5 * k][index] = value

    every = slice(None)
    step(0, gc, C_IN, LP, (every, every))
    step(1, gc, C_M0, HID, 0)
    step(1, gc, C_M1, HID, 1)
    step(1, gf, F_M2, HID, 2)
    step(1, gf, F_M3, HID, 3)
    step(2, gc, C_OUT, BACK + FORE, (every, every))
    step(4, gf, F_OUT, OUTLOOK, (every, every))
    for lo in range(0, LOOKBACK, 512):
        width = min(512, LOOKBACK - lo)
        step(3, gf, F_IN + lo, width, (every, slice(lo, lo + width)))


def interp_table(count, length, first_row, rows, cols):
    spots = np.clip((np.arange(length) + 0.5) * (count / length) - 0.5, 0.0, count - 1.0)
    table = np.maximum(0.0, 1.0 - np.abs(spots[None, :] - np.arange(count)[:, None]))
    out = np.zeros((rows, cols), np.float32)
    out[first_row : first_row + count, :length] = np.round(table * 48.0)
    return out


def spec(shape, index):
    return pl.BlockSpec(shape, index)


def fixed(shape):
    return pl.BlockSpec(shape, lambda i: (0,) * len(shape), pipeline_mode=pl.Buffered(1))


def whole_vmem(n):
    return [pl.BlockSpec(memory_space=pltpu.VMEM)] * n


def body(
    history, later_observed, lengths, counted_flags, series,
    coarse_in, middle, rough_final_matrix, fine_in, sharp_final_matrix, offset_vectors,
    coarse_in_mean, middle_mean, rough_final_first, fine_in_mean, sharp_final_first, biases_mean,
    coarse_in_square, middle_square, rough_final_second, fine_in_square, sharp_final_second,
    biases_square,
):
    dp, fsdp = lax.axis_size("dp"), lax.axis_size("fsdp")
    d_here, f_here = lax.axis_index("dp"), lax.axis_index("fsdp")
    rows = history.shape[0]
    share = HID // fsdp
    part = share // dp

    def exchange(x, bit_dp, bit_fsdp):
        return swap(x, dp, fsdp, bit_dp, bit_fsdp)

    def join(p, q):
        return jnp.concatenate([p, q], 0)

    here = f_here * share + d_here * part
    order = row_order(dp, fsdp)
    abscol = (jnp.asarray(order, jnp.int32) ^ here).reshape(HID, 1)

    wc_part, wf_part = pl.pallas_call(
        pack_kernel,
        out_shape=(
            jax.ShapeDtypeStruct((part, C_ALL), BF16),
            jax.ShapeDtypeStruct((part, F_ALL), BF16),
        ),
        in_specs=[pl.BlockSpec(memory_space=pltpu.SMEM)] + whole_vmem(5),
        out_specs=tuple(whole_vmem(2)),
        compiler_params=vmem(32),
        name="pack_weights",
    )(
        d_here.reshape(1),
        coarse_in.T,
        middle.transpose(0, 2, 1),
        rough_final_matrix,
        fine_in.T,
        sharp_final_matrix,
    )
    wc = gather_rows(wc_part, dp, fsdp, exchange, join)
    wf = gather_rows(wf_part, dp, fsdp, exchange, join)

    hist = history.T
    lens = lengths.reshape(1, rows)
    series_row = series.reshape(1, rows)
    r = 256
    tiles = rows // r
    last = tiles - 1

    def col_spec(height):
        return spec((height, r), lambda i: (0, jnp.minimum(i, last)))

    def out_spec():
        return spec((HID // 2, TILE), lambda i: (0, jnp.maximum(i - tiles, 0)))

    pooled_raw, table = pl.pallas_call(
        stats_kernel,
        grid=(rows // 128,),
        out_shape=(
            jax.ShapeDtypeStruct((HID, rows), F32),
            jax.ShapeDtypeStruct((8, SERIES), F32),
        ),
        in_specs=[spec((h, 128), lambda i: (0, i)) for h in (LOOKBACK, 1, 1)],
        out_specs=(
            spec((HID, 128), lambda i: (0, i)),
            pl.BlockSpec((8, SERIES), lambda i: (0, 0)),
        ),
        compiler_params=vmem(40),
        name="window_stats",
    )(hist, lens, series_row)
    for bit in bits_of(fsdp):
        table = table + exchange(table, 0, bit)
    for bit in bits_of(dp):
        table = table + exchange(table, bit, 0)

    hidden = offset_vectors[: 6 * HID].reshape(6, HID)
    rough_bias = offset_vectors[6 * HID : 6 * HID + BACK + FORE]
    sharp_bias = offset_vectors[6 * HID + BACK + FORE :]

    def bias_cols(three, last, width):
        out = jnp.pad(three, ((0, 0), (0, width - HID)))
        out = join(out, jnp.pad(last, (0, width - last.shape[0]))[None])
        return jnp.pad(out, ((0, 4), (0, 0))).T

    coarse_offs = bias_cols(hidden[:3], rough_bias, HID)
    fine_offs = bias_cols(hidden[3:], sharp_bias, O_PAD)

    square = pltpu.VMEM((HID, HID), BF16)
    wide = pltpu.VMEM((HID, rows), BF16)
    z, pooled, th, look = pl.pallas_call(
        coarse_kernel,
        grid=(tiles,),
        out_shape=(
            jax.ShapeDtypeStruct((3 * HID, rows), F32),
            jax.ShapeDtypeStruct((HID, rows), BF16),
            jax.ShapeDtypeStruct((HID, rows), BF16),
            jax.ShapeDtypeStruct((8, rows), F32),
        ),
        in_specs=[
            col_spec(HID),
            col_spec(1),
            col_spec(1),
            fixed((8, SERIES)),
            fixed((HID, C_ALL)),
            fixed((HID, 8)),
            fixed((HID, 1)),
        ],
        out_specs=(col_spec(3 * HID), col_spec(HID), col_spec(HID), col_spec(8)),
        scratch_shapes=[
            pltpu.VMEM((16, SERIES), BF16),
            square,
            square,
            pltpu.VMEM((256, HID), BF16),
            pltpu.VMEM((HID, 8), F32),
        ],
        compiler_params=vmem(50),
        name="coarse_forward",
    )(pooled_raw, lens, series_row, table, wc, coarse_offs, abscol)

    back_table = interp_table(BACK, LOOKBACK, 0, 256, T_PAD)
    btab = jnp.asarray(back_table, BF16)
    back_table[CINV_AT : CINV_AT + 3, :LOOKBACK] = 1.0
    btab_t = jnp.asarray(back_table.T, BF16)
    fore_table = interp_table(FORE, OUTLOOK, BACK, 256, O_PAD)
    ftab = jnp.asarray(fore_table, BF16)
    ftab_t = jnp.asarray(fore_table.T, BF16)

    dz1f, fore, f_keep, f_send, f_small = pl.pallas_call(
        fine_kernel,
        grid=(tiles + F_ALL // TILE,),
        out_shape=(
            jax.ShapeDtypeStruct((HID, rows), BF16),
            jax.ShapeDtypeStruct((256, rows), F32),
            jax.ShapeDtypeStruct((HID // 2, F_ALL), F32),
            jax.ShapeDtypeStruct((HID // 2, F_ALL), BF16),
            jax.ShapeDtypeStruct((8, O_PAD), F32),
        ),
        in_specs=[
            col_spec(LOOKBACK),
            col_spec(OUTLOOK),
            col_spec(OUTLOOK),
            col_spec(8),
            col_spec(1),
            col_spec(HID),
            fixed((HID, F_ALL)),
            fixed((T_PAD, 256)),
            fixed((256, O_PAD)),
            fixed((O_PAD, 256)),
            fixed((O_PAD, 8)),
            fixed((HID, 1)),
        ],
        out_specs=(
            col_spec(HID),
            col_spec(256),
            out_spec(),
            out_spec(),
            pl.BlockSpec((8, O_PAD), lambda i: (0, 0)),
        ),
        scratch_shapes=[
            pltpu.VMEM((T_PAD, rows), BF16),
            wide, wide, wide, wide, wide, wide,
            pltpu.VMEM((O_PAD, rows), BF16),
            square, square, square, square,
            pltpu.VMEM((O_PAD, HID), BF16),
            pltpu.VMEM((HID, 8), F32),
            square,
            pltpu.VMEM((3, HID, 128), F32),
            pltpu.VMEM((O_PAD, 128), F32),
            pltpu.VMEM((8, r), F32),
            pltpu.VMEM((3, HID, HID), BF16),
        ],
        compiler_params=vmem(63),
        name="fine_block",
    )(
        hist, later_observed.T, counted_flags.T, look, lens, th,
        wf, btab_t, ftab, ftab_t, fine_offs, abscol,
    )

    c_keep, c_send, c_small = pl.pallas_call(
        back_kernel,
        grid=(tiles + C_ALL // TILE,),
        out_shape=(
            jax.ShapeDtypeStruct((HID // 2, C_ALL), F32),
            jax.ShapeDtypeStruct((HID // 2, C_ALL), BF16),
            jax.ShapeDtypeStruct((8, HID), F32),
        ),
        in_specs=[
            col_spec(HID),
            col_spec(256),
            col_spec(1),
            col_spec(3 * HID),
            col_spec(HID),
            fixed((HID, T_PAD)),
            fixed((256, T_PAD)),
            fixed((HID, C_ALL)),
            fixed((HID, 1)),
        ],
        out_specs=(out_spec(), out_spec(), pl.BlockSpec((8, HID), lambda i: (0, 0))),
        scratch_shapes=[
            wide, wide, wide, wide, wide, wide, wide,
            pltpu.VMEM((256, rows), BF16),
            pltpu.VMEM((T_PAD, HID), BF16),
            square, square, square,
            pltpu.VMEM((3, HID, 128), F32),
            pltpu.VMEM((256, 128), F32),
            pltpu.VMEM((3, HID, HID), BF16),
        ],
        compiler_params=vmem(60),
        name="coarse_backward",
    )(dz1f, fore, lens, z, pooled, wf, btab, wc, abscol)

    def step_sum(keep, send, bit_dp, bit_fsdp):
        return keep + exchange(send.astype(BF16), bit_dp, bit_fsdp).astype(F32)

    def halve(x, bit_dp, bit_fsdp):
        half = x.shape[0] // 2
        return step_sum(x[:half], x[half:], bit_dp, bit_fsdp)

    def scatter_rows(keep, send):
        far = bits_of(fsdp)
        x = step_sum(keep, send, 0, far[0])
        half = x.shape[0] // 2
        a, b = x[:half], x[half:]
        for first, second in zip(bits_of(dp), reversed(bits_of(dp))):
            a, b = halve(a, first, 0), halve(b, second, 0)
        x = join(a, b)
        for bit in far[1:]:
            x = halve(x, 0, bit)
        return x

    def share_rows(x):
        half = x.shape[0] // 2
        a, b = x[:half], x[half:]
        for first, second in zip(reversed(bits_of(dp)), bits_of(dp)):
            a2, b2 = exchange(a, first, 0), exchange(b, second, 0)
            a, b = join(a, a2), join(b, b2)
        return join(a, b)

    gf_part = scatter_rows(f_keep, f_send)
    gc_part = scatter_rows(c_keep, c_send)
    gf = share_rows(gf_part)
    gc = share_rows(gc_part)

    rel = np.arange(part)
    lo, hi = rel[: part // 2], rel[part // 2 :]
    for first, second in zip(reversed(bits_of(dp)), bits_of(dp)):
        lo = np.concatenate([lo, lo ^ (first * part)])
        hi = np.concatenate([hi, hi ^ (second * part)])
    relrow = (
        jnp.asarray(np.concatenate([lo, hi]), jnp.int32) ^ (d_here * part)
    ).reshape(share, 1)

    squares = jnp.sum(gf_part * gf_part) + jnp.sum(gc_part * gc_part)
    small = jnp.concatenate([f_small, c_small], 1)
    small = jnp.where(
        (iota(small.shape, 0) == 6) & (iota(small.shape, 1) == 0), squares, small
    )
    for bit in bits_of(dp):
        small = small + exchange(small, bit, 0)
    for bit in bits_of(fsdp):
        small = small + exchange(small, 0, bit)
    bias_sum = jnp.concatenate(
        [
            small[0:3, O_PAD : O_PAD + HID].reshape(-1),
            small[0:3, 0:HID].reshape(-1),
            small[3, O_PAD : O_PAD + BACK + FORE],
            small[3, 0:OUTLOOK],
        ]
    )
    loss_sum = small[4, 0]
    usable_tally = small[5, 0]
    total_square = small[6, 0] + jnp.sum(bias_sum * bias_sum)
    grad_norm = jnp.sqrt(total_square) / usable_tally
    factor = clip_level / jnp.maximum(grad_norm, clip_level)
    scale = factor / usable_tally

    def by_hidden(cin, mid, cout, fin, fout):
        return (cin.T, mid.transpose(0, 2, 1), cout, fin.T, fout)

    shards = (
        *by_hidden(coarse_in, middle, rough_final_matrix, fine_in, sharp_final_matrix),
        *by_hidden(
            coarse_in_mean, middle_mean, rough_final_first, fine_in_mean, sharp_final_first
        ),
        *by_hidden(
            coarse_in_square, middle_square, rough_final_second, fine_in_square,
            sharp_final_second,
        ),
    )
    new = pl.pallas_call(
        adam_kernel,
        out_shape=tuple(jax.ShapeDtypeStruct(x.shape, F32) for x in shards),
        in_specs=[pl.BlockSpec(memory_space=pltpu.SMEM)] + whole_vmem(18),
        out_specs=tuple(whole_vmem(15)),
        compiler_params=vmem(60),
        name="adam",
    )(scale.reshape(1, 1), gc, gf, relrow, *shards)
    bias_new = adam_math(offset_vectors, biases_mean, biases_square, bias_sum * scale)
    return (
        loss_sum, usable_tally, grad_norm,
        *by_hidden(*new[0:5]), bias_new[0],
        *by_hidden(*new[5:10]), bias_new[1],
        *by_hidden(*new[10:15]), bias_new[2],
    )


def solution(mesh):
    rows2 = P(("dp", "fsdp"), None)
    rows1 = P(("dp", "fsdp"))
    weights = (P(None, "fsdp"), P(None, None, "fsdp"), P("fsdp", None), P(None, "fsdp"), P("fsdp", None), P())
    in_specs = (rows2, rows2, rows1, rows2, rows1) + weights * 3
    out_specs = (P(), P(), P()) + weights * 3
    return jax.shard_map(body, mesh=mesh, in_specs=in_specs, out_specs=out_specs, check_vma=False)
```

```python
import functools

import jax
import jax.numpy as jnp
import numpy as np
from jax import lax
from jax.experimental import pallas as pl
from jax.experimental.pallas import tpu as pltpu
from jax.sharding import PartitionSpec as P

LOOKBACK = 3600
OUTLOOK = 720
HID = 512
SERIES = 1024
STEP = 10
LP = 450
BACK = 150
FORE = 30
RATIO = 24
beta_first = 0.9
beta_second = 0.999
learn_rate = 0.01
weight_decay = 0.01
adam_epsilon = 1e-08
clip_level = 0.01

C_IN, C_M0, C_M1, C_OUT, C_ALL = 0, 512, 1024, 1536, 1792
F_IN, F_M2, F_M3, F_OUT, F_ALL = 0, 3840, 4352, 4864, 5632
T_PAD = 3840
LATEST = 2700
T_LIVE = 3712
T_WHOLE = 3584
O_PAD = 768
TILE = 256
CINV_AT = 180

F32 = jnp.float32
BF16 = jnp.bfloat16
NN = (((1,), (0,)), ((), ()))
NT = (((1,), (1,)), ((), ()))
TN = (((0,), (0,)), ((), ()))


def mm(a, b, dims=NN):
    return lax.dot_general(a, b, dims, preferred_element_type=F32)


def iota(shape, axis):
    return lax.broadcasted_iota(jnp.int32, shape, axis)


def split3(v):
    hi = v.astype(BF16)
    rest = v - hi.astype(F32)
    mid = rest.astype(BF16)
    return hi, mid, (rest - mid.astype(F32)).astype(BF16)


def mm_exact(v, sel, dims=NN):
    hi, mid, low = split3(v)
    return mm(hi, sel, dims) + mm(mid, sel, dims) + mm(low, sel, dims)


def mm_exact2(sel, v, dims=NN):
    hi, mid, low = split3(v)
    return mm(sel, hi, dims) + mm(sel, mid, dims) + mm(sel, low, dims)


def activate(h):
    u = 1.0 + jnp.tanh(h)
    return h * u, u


def slope_once(h, u, value):
    return u * ((0.5 + h) - 0.5 * value)


def slope_twice(h, u, value):
    return u * ((1.0 + h) + (h - value))


def cost(micros):
    return pl.CostEstimate(
        flops=int(micros * 1.15e9), bytes_accessed=int(micros * 3e6), transcendentals=0
    )


def mask_rows(value, lo, begin):
    if lo >= LATEST:
        return value
    seen = iota(value.shape, 0) >= begin - lo
    return jnp.where(seen, value, jnp.zeros_like(value))


def vmem(limit=60):
    return pltpu.CompilerParams(vmem_limit_bytes=limit * 1024 * 1024)


def bits_of(size):
    return [1 << b for b in range(size.bit_length() - 1)]


def swap(x, dp, fsdp, bit_dp, bit_fsdp):
    pairs = []
    for d in range(dp):
        for f in range(fsdp):
            pairs.append((d * fsdp + f, (d ^ bit_dp) * fsdp + (f ^ bit_fsdp)))
    return lax.ppermute(x, ("dp", "fsdp"), pairs)


def gather_rows(x, dp, fsdp, swap_fn, join):
    far = bits_of(fsdp)
    for bit in reversed(far[1:]):
        x = join(x, swap_fn(x, 0, bit))
    half = x.shape[0] // 2
    a, b = x[:half], x[half:]
    for first, second in zip(reversed(bits_of(dp)), bits_of(dp)):
        a2 = swap_fn(a, first, 0)
        b2 = swap_fn(b, second, 0)
        a, b = join(a, a2), join(b, b2)
    x = join(a, b)
    return join(x, swap_fn(x, 0, far[0]))


def row_order(dp, fsdp):
    share = HID // fsdp
    part = share // dp
    start = np.arange(part)

    def shifted(x, bit_dp, bit_fsdp):
        return x ^ (bit_fsdp * share + bit_dp * part)

    return gather_rows(
        start, dp, fsdp, shifted, lambda p, q: np.concatenate([p, q])
    )


def pack_kernel(d_ref, cin, mid, cout, fin, fout, wc, wf):
    share = cout.shape[0]
    part = wc.shape[0]
    rows = max(part, 16)
    sel = (iota((rows, share), 1) == d_ref[0] * part + iota((rows, share), 0)).astype(BF16)
    wc[...] = jnp.zeros_like(wc)
    wf[...] = jnp.zeros_like(wf)

    def put(ref, at, value, scale=0.5):
        picked = mm(sel, value.astype(BF16)) * scale
        ref[:, at : at + value.shape[1]] = picked[:part].astype(BF16)

    put(wc, C_IN, cin[...])
    put(wc, C_M0, mid[0])
    put(wc, C_M1, mid[1])
    put(wc, C_OUT, cout[...], 1.0)
    put(wf, F_IN, fin[...])
    put(wf, F_M2, mid[2])
    put(wf, F_M3, mid[3])
    put(wf, F_OUT, fout[...], 1.0)


def stats_kernel(count, *refs):
    pooled, table = refs[-2:]
    lens, series = refs[count : count + 2]
    hists = refs[:count]
    wide = hists[0].shape[1]

    @pl.when(pl.program_id(0) == 0)
    def _():
        table[...] = jnp.zeros_like(table)

    chunk = 32
    at = LP // chunk * chunk
    rest = LP - at
    base = iota((chunk, wide), 0) * 8
    pooled[at:HID, :] = jnp.zeros((HID - at, pooled.shape[1]), F32)
    for q, hist in enumerate(hists):
        cols = slice(q * wide, (q + 1) * wide)
        begin = LOOKBACK - lens[:, cols]
        sums = jnp.zeros((8, wide), F32)
        squares = jnp.zeros((8, wide), F32)

        def load(g, s, count):
            h = hist[pl.ds(g * 8 + s, count, stride=8), :]
            if g * 8 >= LATEST:
                return h
            return jnp.where(base[0:count] >= begin - (g * 8 + s), h, 0.0)

        for g in range(0, at, chunk):
            total = load(g, 0, chunk)
            sq = total * total
            for s in range(1, 8):
                h = load(g, s, chunk)
                total += h
                sq += h * h
            for v in range(0, chunk, 8):
                sums += total[v : v + 8]
                squares += sq[v : v + 8]
            pooled[g : g + chunk, cols] = total * 0.125
        total = load(at, 0, rest)
        sq = total * total
        for s in range(1, 8):
            h = load(at, s, rest)
            total += h
            sq += h * h
        pooled[at:LP, cols] = total * 0.125
        sum_row = jnp.sum(sums, 0, keepdims=True) + jnp.sum(total, 0, keepdims=True)
        square_row = jnp.sum(squares, 0, keepdims=True) + jnp.sum(sq, 0, keepdims=True)
        row = iota((16, wide), 0)
        kind = row % 3
        v = jnp.where(
            kind == 0,
            sum_row,
            jnp.where(kind == 1, square_row, lens[:, cols].astype(F32)),
        )
        hi, mid, low = split3(v)
        piece = jnp.where(
            row < 3,
            hi.astype(F32),
            jnp.where(row < 6, mid.astype(F32), jnp.where(row < 9, low.astype(F32), 0.0)),
        ).astype(BF16)
        hot = (iota((SERIES, wide), 0) == series[:, cols]).astype(BF16)
        t = mm(piece, hot, NT)
        table[0:3, :] += t[0:3] + t[3:6] + t[6:9]


def prepare_kernel(w00, w01, w10, w11, offs, abscol, m0, m1, offs_p):
    perm = (iota((HID, HID), 1) == abscol[...]).astype(BF16)
    half = HID // 2
    for left, right, out in ((w00, w01, m0), (w10, w11, m1)):
        out[...] = (
            mm(left[...], perm[:, :half], NT) + mm(right[...], perm[:, half:], NT)
        ).astype(BF16)
    offs_p[...] = mm_exact2(perm, offs[0:HID, :])


def coarse_kernel(p_in, lens, series, table, wc, offs, m0, m1, offs_p,
                  pooled_out, th_out, look_out, looker):
    cols = p_in.shape[1]

    @pl.when(pl.program_id(0) == 0)
    def _():
        count = jnp.maximum(table[2:3, :], 1.0)
        centre = table[0:1, :] / count
        spread = jnp.sqrt(table[1:2, :] / count + 1e-05)
        inverse = 1.0 / spread
        shifted = centre / spread
        row = iota((16, SERIES), 0)
        v = jnp.where(row < 3, inverse, shifted)
        hi, mid, low = split3(v)
        kind = row % 3
        looker[...] = jnp.where(
            row < 6,
            jnp.where(
                kind == 0,
                hi.astype(F32),
                jnp.where(kind == 1, mid.astype(F32), low.astype(F32)),
            ),
            0.0,
        ).astype(BF16)

    hot = (iota((SERIES, cols), 0) == series[...]).astype(BF16)
    got = mm(looker[...], hot)
    inv = got[0:1] + got[1:2] + got[2:3]
    cinv = got[3:4] + got[4:5] + got[5:6]
    look_out[...] = jnp.where(iota((8, cols), 0) == 0, inv, cinv)
    group = iota((HID, cols), 0)
    begin = LOOKBACK - lens[...]
    share = jnp.clip(group * 8 + 8 - begin, 0, 8).astype(F32) * 0.125
    pooled = jnp.where(group < LP, p_in[...] * inv - cinv * share, 0.0).astype(BF16)
    pooled_out[...] = pooled
    v = activate(mm(wc[:, C_IN : C_IN + HID], pooled) + offs_p[:, 0:1])[0]
    v = activate(mm(m0[...], v.astype(BF16)) + offs_p[:, 1:2])[0]
    v = activate(mm(m1[...], v.astype(BF16)) + offs_p[:, 2:3])[0]
    theta = mm(wc[:, C_OUT:C_ALL], v.astype(BF16), TN) + offs[0:256, 3:4]
    theta = theta * (1.0 / 48.0)
    hi = theta.astype(BF16).astype(F32)
    at = iota((256, cols), 0)
    c_hi, c_mid, c_low = split3(cinv)
    with_shift = jnp.where(
        at == CINV_AT,
        c_hi.astype(F32),
        jnp.where(
            at == CINV_AT + 1,
            c_mid.astype(F32),
            jnp.where(at == CINV_AT + 2, c_low.astype(F32), hi),
        ),
    )
    th_out[...] = with_shift.astype(BF16)


def fold_lanes(x):
    total = x[:, 0:128]
    for at in range(128, x.shape[1], 128):
        total = total + x[:, at : at + 128]
    return total


def hidden_rows(acc, perm):
    lane = iota((HID, 128), 1)
    v = jnp.zeros((HID, 128), F32)
    for k in range(3):
        v = jnp.where(lane == k, jnp.sum(acc[k], 1, keepdims=True), v)
    return mm_exact(v, perm, TN)[0:8]


def last_row(acc):
    v = jnp.broadcast_to(jnp.sum(acc, 1, keepdims=True), acc.shape)
    return jnp.transpose(v, (1, 0))[0:8]


def perm_of(abscol):
    return (iota((HID, HID), 1) == abscol[...]).astype(BF16)


def fine_kernel(hist, later, flags, look, lens, th, wf, btab_t, ftab, ftab_t, offs, abscol,
                m2, m3, offs_p,
                res, a1, a2, a3, dz1, dz2, dz3, dz4, fore, small,
                acc, acc4, acc_loss):
    cols = hist.shape[1]
    step = pl.program_id(0)

    @pl.when(step == 0)
    def _():
        acc[...] = jnp.zeros_like(acc)
        acc4[...] = jnp.zeros_like(acc4)
        acc_loss[...] = jnp.zeros_like(acc_loss)

    inv = look[0:1, :]
    cinv = look[1:2, :]
    begin = LOOKBACK - lens[...]
    th_hi = th[...]
    res[LOOKBACK:T_PAD, :] = jnp.zeros((T_PAD - LOOKBACK, cols), BF16)
    h1 = offs_p[:, 0:1]
    for at in range(0, T_LIVE, 1024):
        end = min(at + 1024, T_LIVE)
        for lo in range(at, min(end, LOOKBACK), 512):
            width = min(512, LOOKBACK - lo)
            shift = mm(btab_t[lo : lo + width, :], th_hi)
            r = hist[lo : lo + width, :] * inv - shift
            res[lo : lo + width, :] = mask_rows(r, lo, begin).astype(BF16)
        h1 = h1 + mm(wf[:, F_IN + at : F_IN + end], res[at:end, :])
    v1, u1 = activate(h1)
    b1 = v1.astype(BF16)
    a1[...] = b1
    h2 = mm(m2[...], b1) + offs_p[:, 1:2]
    v2, u2 = activate(h2)
    b2 = v2.astype(BF16)
    a2[...] = b2
    h3 = mm(m3[...], b2) + offs_p[:, 2:3]
    v3, u3 = activate(h3)
    b3 = v3.astype(BF16)
    a3[...] = b3
    est = mm(wf[:, F_OUT:F_ALL], b3, TN) + mm(ftab_t[...], th_hi) + offs[:, 3:4]
    counted = flags[...].astype(F32)
    err = (est[0:OUTLOOK] - (later[...] * inv - cinv)) * counted
    acc_loss[0:1, :] += jnp.sum(err * err, 0, keepdims=True)
    acc_loss[1:2, :] += jnp.sum(counted, 0, keepdims=True)
    d4 = (2.0 * err).astype(BF16)
    acc4[0:OUTLOOK, :] += fold_lanes(d4.astype(F32))
    dz4[0:OUTLOOK, :] = d4
    dz4[OUTLOOK:O_PAD, :] = jnp.zeros((O_PAD - OUTLOOK, cols), BF16)
    d4 = dz4[...]
    fore[...] = mm(ftab[...], d4) * (1.0 / 48.0)

    def back(upstream, slope, slot, row):
        d = (upstream * slope).astype(BF16)
        acc[row] += fold_lanes(d.astype(F32))
        slot[...] = d
        return d

    d3 = back(mm(wf[:, F_OUT:F_ALL], d4), slope_once(h3, u3, v3), dz3, 2)
    d2 = back(mm(m3[...], d3, TN), slope_twice(h2, u2, v2), dz2, 1)
    back(mm(m2[...], d2, TN), slope_twice(h1, u1, v1), dz1, 0)

    @pl.when(step == pl.num_programs(0) - 1)
    def _():
        small[...] = last_row(acc4[...])
        loss = jnp.sum(acc_loss[0:1, :], 1, keepdims=True)
        tally = jnp.sum(acc_loss[1:2, :], 1, keepdims=True)
        row = iota((8, O_PAD), 0)
        small[...] = jnp.where(
            row == 3,
            small[...],
            jnp.where(row == 4, loss, jnp.where(row == 5, tally, 0.0)),
        )
        small[0:3, 0:HID] = hidden_rows(acc, perm_of(abscol))[0:3]


def put_halves(keep, send, g):
    half = HID // 2
    keep[...] = g[0:half]
    send[...] = g[half:HID].astype(BF16)


def natural_columns(g, perm):
    half = HID // 2
    hi = g.astype(BF16)
    low = (g - hi.astype(F32)).astype(BF16)
    out = mm(hi, perm)
    return jnp.concatenate([out[0:half] + mm(low[0:half], perm), out[half:HID]], 0)


def fine_in_grad_kernel(dz1, res, keep, send):
    put_halves(keep, send, mm(dz1[...], res[...], NT))


def fine_rest_grad_kernel(dz2, a1, dz3, a2, a3, dz4, abscol, keep_in, send_in,
                          keep, send, total, keep_part, send_part, sems):
    del keep_in, send_in
    step = pl.program_id(0)
    half = HID // 2
    pieces = ((dz2, a1), (dz3, a2), (a3, dz4))
    places = (slice(0, HID), slice(HID, 2 * HID), slice(2 * HID, F_ALL - F_M2))

    @pl.when(step == 0)
    def _():
        for (lhs, rhs), cols in zip(pieces, places):
            total[:, cols] = mm(lhs[...], rhs[...], NT)

    @pl.when(step > 0)
    def _():
        for (lhs, rhs), cols in zip(pieces, places):
            total[:, cols] += mm(lhs[...], rhs[...], NT)

    @pl.when(step == pl.num_programs(0) - 1)
    def _():
        perm = perm_of(abscol)
        copies = []
        for k, cols in enumerate(places):
            g = total[:, cols]
            if k < 2:
                g = natural_columns(g, perm)
            keep_part[:, cols] = g[0:half]
            send_part[:, cols] = g[half:HID].astype(BF16)
            there = slice(F_M2 + cols.start, F_M2 + cols.stop)
            copies += [
                pltpu.make_async_copy(keep_part.at[:, cols], keep.at[:, there], sems.at[k, 0]),
                pltpu.make_async_copy(send_part.at[:, cols], send.at[:, there], sems.at[k, 1]),
            ]
            copies[-2].start()
            copies[-1].start()
        for copy in copies:
            copy.wait()


def back_kernel(first, *refs):
    dz1f, fore, lens, pooled_in, wf, btab, wc, abscol, m0, m1, offs_p = refs[:11]
    before = () if first else refs[11:12]
    outs = refs[11 + len(before) : -10]
    pooled, a1, a2, a3, dz1, dz2, dz3, dz4, acc, acc4 = refs[-10:]
    small = outs[-1]
    cols = dz1f.shape[1]
    tiles = pooled.shape[1] // cols
    step = pl.program_id(0)

    @pl.when(step == 0)
    def _():
        acc[...] = jnp.zeros_like(acc)
        acc4[...] = jnp.zeros_like(acc4)

    @pl.when(step < tiles)
    def _():
        here = pl.ds(pl.multiple_of(step * cols, cols), cols)
        begin = LOOKBACK - lens[...]
        d1f = dz1f[...]
        total = jnp.zeros((256, cols), F32)
        for lo in range(0, T_LIVE, 512):
            width = min(512, T_LIVE - lo)
            d = mask_rows(mm(wf[:, lo : lo + width], d1f, TN), lo, begin).astype(BF16)
            total += mm(btab[:, lo : lo + width], d)
        row = iota((256, cols), 0)
        d4 = (jnp.where(row < BACK, total * (-2.0 / 48.0), 0.0) + fore[...]).astype(BF16)
        dz4[:, here] = d4
        acc4[...] += fold_lanes(d4.astype(F32))
        p = pooled_in[...]
        pooled[:, here] = p

        def ahead(w, entering, k, slot):
            h = mm(w, entering) + offs_p[:, k : k + 1]
            value, u = activate(h)
            low = value.astype(BF16)
            slot[:, here] = low
            return h, u, value, low

        h1, u1, v1, b1 = ahead(wc[:, C_IN : C_IN + HID], p, 0, a1)
        h2, u2, v2, b2 = ahead(m0[...], b1, 1, a2)
        h3, u3, v3, _ = ahead(m1[...], b2, 2, a3)

        def back(upstream, slope, slot, row):
            d = (upstream * slope).astype(BF16)
            acc[row] += fold_lanes(d.astype(F32))
            slot[:, here] = d
            return d

        d3 = back(mm(wc[:, C_OUT:C_ALL], d4), slope_once(h3, u3, v3), dz3, 2)
        d2 = back(mm(m1[...], d3, TN), slope_twice(h2, u2, v2), dz2, 1)
        back(mm(m0[...], d2, TN), slope_twice(h1, u1, v1), dz1, 0)

    half = HID // 2

    def put(at, g, perm=None):
        cols = slice(at, at + g.shape[1])
        if first:
            outs[0][:, cols] = g
            return
        g = g + before[0][:, cols]
        if perm is not None:
            g = natural_columns(g, perm)
        outs[0][:, cols] = g[0:half]
        outs[1][:, cols] = g[half:HID].astype(BF16)

    @pl.when(step == tiles)
    def _():
        perm = perm_of(abscol)
        put(C_IN, mm(dz1[...], pooled[...], NT))
        put(C_M0, mm(dz2[...], a1[...], NT), perm)
        put(C_M1, mm(dz3[...], a2[...], NT), perm)
        put(C_OUT, mm(a3[...], dz4[...], NT))
        small[...] = jnp.zeros_like(small)
        small[0:3, :] = hidden_rows(acc, perm)[0:3]
        small[3:4, 0:256] = last_row(acc4[...])[0:1]


def adam_math(weight, mean_old, square_old, grad):
    mean_new = beta_first * mean_old + (1.0 - beta_first) * grad
    square_new = beta_second * square_old + (1.0 - beta_second) * grad * grad
    mean_hat = mean_new / (1.0 - beta_first**STEP)
    square_hat = square_new / (1.0 - beta_second**STEP)
    weight_new = weight - learn_rate * (
        mean_hat / (jnp.sqrt(square_hat) + adam_epsilon) + weight_decay * weight
    )
    return weight_new, mean_new, square_new


def adam_kernel(scale, gc, gf, relrow, *refs):
    ins, outs = refs[:15], refs[15:]
    share = gc.shape[0]
    s = scale[0, 0]
    place = (iota((share, share), 1) == relrow[...]).astype(BF16)

    def step(i, part, at, width, index):
        grad = mm_exact2(place, part[:, at : at + width], TN) * s
        old = [ins[i + 5 * k][index] for k in range(3)]
        for k, value in enumerate(adam_math(*old, grad)):
            outs[i + 5 * k][index] = value

    every = slice(None)
    step(0, gc, C_IN, LP, (every, every))
    step(1, gc, C_M0, HID, 0)
    step(1, gc, C_M1, HID, 1)
    step(1, gf, F_M2, HID, 2)
    step(1, gf, F_M3, HID, 3)
    step(2, gc, C_OUT, BACK + FORE, (every, every))
    step(4, gf, F_OUT, OUTLOOK, (every, every))
    for lo in range(0, LOOKBACK, 512):
        width = min(512, LOOKBACK - lo)
        step(3, gf, F_IN + lo, width, (every, slice(lo, lo + width)))


def interp_table(count, length, first_row, rows, cols):
    spots = np.clip((np.arange(length) + 0.5) * (count / length) - 0.5, 0.0, count - 1.0)
    table = np.maximum(0.0, 1.0 - np.abs(spots[None, :] - np.arange(count)[:, None]))
    out = np.zeros((rows, cols), np.float32)
    out[first_row : first_row + count, :length] = np.round(table * 48.0)
    return out


def spec(shape, index):
    return pl.BlockSpec(shape, index)


def fixed(shape):
    return pl.BlockSpec(shape, lambda i: (0,) * len(shape), pipeline_mode=pl.Buffered(1))


def body(
    history, later_observed, lengths, counted_flags, series,
    coarse_in, middle, rough_final_matrix, fine_in, sharp_final_matrix, offset_vectors,
    coarse_in_mean, middle_mean, rough_final_first, fine_in_mean, sharp_final_first, biases_mean,
    coarse_in_square, middle_square, rough_final_second, fine_in_square, sharp_final_second,
    biases_square,
):
    dp, fsdp = lax.axis_size("dp"), lax.axis_size("fsdp")
    d_here, f_here = lax.axis_index("dp"), lax.axis_index("fsdp")
    rows = history.shape[0]
    share = HID // fsdp
    part = share // dp

    def exchange(x, bit_dp, bit_fsdp):
        return swap(x, dp, fsdp, bit_dp, bit_fsdp)

    def join(p, q):
        return jnp.concatenate([p, q], 0)

    here = f_here * share + d_here * part
    order = row_order(dp, fsdp)
    abscol = (jnp.asarray(order, jnp.int32) ^ here).reshape(HID, 1)
    together = lax.optimization_barrier

    def by_hidden(cin, mid, cout, fin, fout):
        return (cin.T, mid.transpose(0, 2, 1), cout, fin.T, fout)

    def one_step(arrays):
        return [
            pl.BlockSpec(x.shape, lambda i, n=len(x.shape): (0,) * n) for x in arrays
        ]

    shard_now = by_hidden(
        coarse_in, middle, rough_final_matrix, fine_in, sharp_final_matrix
    )

    parts = pl.pallas_call(
        pack_kernel,
        out_shape=(
            jax.ShapeDtypeStruct((part, C_ALL), BF16),
            jax.ShapeDtypeStruct((part, F_ALL), BF16),
        ),
        grid=(1,),
        in_specs=[pl.BlockSpec(memory_space=pltpu.SMEM)] + one_step(shard_now),
        out_specs=tuple([pl.BlockSpec((part, n), lambda i: (0, 0)) for n in (C_ALL, F_ALL)]),
        compiler_params=vmem(32),
        cost_estimate=cost(1),
        name="pack_weights",
    )(d_here.reshape(1), *shard_now)

    hist = history.T
    lens = lengths.reshape(1, rows)
    series_row = series.reshape(1, rows)
    side = rows // 2

    def stats(which, lens_row, pool):
        count = 2
        steps = side // (128 * count)
        at = which * steps

        def hist_spec(q):
            return spec((LOOKBACK, 128), lambda i: (0, (at + i) * count + q))

        def row_spec():
            return spec((1, 128 * count), lambda i: (0, at + i))

        return pl.pallas_call(
            functools.partial(stats_kernel, count),
            grid=(steps,),
            out_shape=(
                jax.ShapeDtypeStruct((HID, rows), F32),
                jax.ShapeDtypeStruct((8, SERIES), F32),
            ),
            in_specs=[hist_spec(q) for q in range(count)]
            + [row_spec(), row_spec()]
            + [pl.BlockSpec(memory_space=pl.ANY) for _ in pool],
            out_specs=(
                spec((HID, 128 * count), lambda i: (0, at + i)),
                pl.BlockSpec((8, SERIES), lambda i: (0, 0)),
            ),
            compiler_params=vmem(24),
            cost_estimate=cost(6),
            input_output_aliases={count + 2: 0} if pool else {},
            name="window_stats",
        )(*[hist] * count, lens_row, series_row, *pool)

    pools, tables = [], []
    for bit in reversed(bits_of(fsdp)[1:]):
        got = [exchange(x, 0, bit) for x in parts]
        if len(pools) < 2:
            lens_row, *parts = together((lens, *parts))
            pool, table = stats(len(pools), lens_row, pools[-1:])
            *got, table = together((*got, table))
            pools.append(pool)
            tables.append(table)
        parts = [join(x, y) for x, y in zip(parts, got)]
    table = tables[0] + tables[1]
    halves = []
    for x in parts:
        halves += [x[: x.shape[0] // 2], x[x.shape[0] // 2 :]]
    small_steps = [(0, bit) for bit in bits_of(fsdp)] + [(bit, 0) for bit in bits_of(dp)]
    cut = len(small_steps) - len(bits_of(dp))
    groups = [small_steps[:cut], small_steps[cut:]]
    for first, second in zip(reversed(bits_of(dp)), bits_of(dp)):
        got = [exchange(x, (first, second)[k % 2], 0) for k, x in enumerate(halves)]
        for bit_dp, bit_fsdp in groups.pop(0) if groups else ():
            table = table + exchange(table, bit_dp, bit_fsdp)
        *got, table = together((*got, table))
        halves = [join(x, y) for x, y in zip(halves, got)]
    for group in groups:
        for bit_dp, bit_fsdp in group:
            table = table + exchange(table, bit_dp, bit_fsdp)
    parts = [join(halves[0], halves[1]), join(halves[2], halves[3])]
    got = [exchange(x, 0, 1) for x in parts]
    wc = join(parts[0], got[0])

    hidden = offset_vectors[: 6 * HID].reshape(6, HID)
    rough_bias = offset_vectors[6 * HID : 6 * HID + BACK + FORE]
    sharp_bias = offset_vectors[6 * HID + BACK + FORE :]

    def bias_cols(three, last, width):
        out = jnp.pad(three, ((0, 0), (0, width - HID)))
        out = join(out, jnp.pad(last, (0, width - last.shape[0]))[None])
        return jnp.pad(out, ((0, 4), (0, 0))).T

    coarse_offs = bias_cols(0.5 * hidden[:3], rough_bias, HID)
    fine_offs = bias_cols(0.5 * hidden[3:], sharp_bias, O_PAD)

    def prepare(w, at, offs, name):
        square = jax.ShapeDtypeStruct((HID, HID), BF16)

        def block(k):
            return pl.BlockSpec((HID, HID // 2), lambda i: (0, at // (HID // 2) + k))

        shapes = (square, square, jax.ShapeDtypeStruct((HID, 8), F32))
        return pl.pallas_call(
            prepare_kernel,
            grid=(1,),
            out_shape=shapes,
            in_specs=[block(k) for k in range(4)] + one_step([offs, abscol]),
            out_specs=tuple(one_step(shapes)),
            compiler_params=vmem(20),
            cost_estimate=cost(2),
            name=name,
        )(w, w, w, w, offs, abscol)

    m0, m1, coarse_offs_p = prepare(wc, C_M0, coarse_offs, "prepare_coarse")

    r = 512
    tiles = rows // r

    def col_spec(height, begin=0, last=tiles - 1):
        return spec((height, r), lambda i: (0, jnp.minimum(begin + i, last)))

    pooled, th, look = pl.pallas_call(
        coarse_kernel,
        grid=(tiles,),
        out_shape=(
            jax.ShapeDtypeStruct((HID, rows), BF16),
            jax.ShapeDtypeStruct((256, rows), BF16),
            jax.ShapeDtypeStruct((8, rows), F32),
        ),
        in_specs=[
            col_spec(HID),
            col_spec(1),
            col_spec(1),
            fixed((8, SERIES)),
            fixed((HID, C_ALL)),
            fixed((HID, 8)),
            fixed((HID, HID)),
            fixed((HID, HID)),
            fixed((HID, 8)),
        ],
        out_specs=(col_spec(HID), col_spec(256), col_spec(8)),
        scratch_shapes=[pltpu.VMEM((16, SERIES), BF16)],
        compiler_params=vmem(50),
        cost_estimate=cost(10),
        name="coarse_forward",
    )(
        pools[-1], lens, series_row, table, wc, coarse_offs, m0, m1, coarse_offs_p,
    )
    got_f, look = together((got[1], look))
    wf = join(parts[1], got_f)
    m2, m3, fine_offs_p = prepare(wf, F_M2, fine_offs, "prepare_fine")

    back_table = interp_table(BACK, LOOKBACK, 0, 256, T_PAD)
    btab = jnp.asarray(back_table, BF16)
    back_table[CINV_AT : CINV_AT + 3, :LOOKBACK] = 1.0
    btab_t = jnp.asarray(back_table.T, BF16)
    fore_table = interp_table(FORE, OUTLOOK, BACK, 256, O_PAD)
    ftab = jnp.asarray(fore_table, BF16)
    ftab_t = jnp.asarray(fore_table.T, BF16)

    tall = jax.ShapeDtypeStruct((HID, rows), BF16)
    res, a1, a2, a3, dz1, dz2, dz3, dz4, fore, f_small = pl.pallas_call(
        fine_kernel,
        grid=(tiles,),
        out_shape=(
            jax.ShapeDtypeStruct((T_PAD, rows), BF16),
            tall, tall, tall, tall, tall, tall,
            jax.ShapeDtypeStruct((O_PAD, rows), BF16),
            jax.ShapeDtypeStruct((256, rows), F32),
            jax.ShapeDtypeStruct((8, O_PAD), F32),
        ),
        in_specs=[
            col_spec(LOOKBACK),
            col_spec(OUTLOOK),
            col_spec(OUTLOOK),
            col_spec(8),
            col_spec(1),
            col_spec(256),
            fixed((HID, F_ALL)),
            fixed((T_PAD, 256)),
            fixed((256, O_PAD)),
            fixed((O_PAD, 256)),
            fixed((O_PAD, 8)),
            fixed((HID, 1)),
            *[fixed((HID, HID))] * 2,
            fixed((HID, 8)),
        ],
        out_specs=(
            col_spec(T_PAD),
            *[col_spec(HID)] * 6,
            col_spec(O_PAD),
            col_spec(256),
            pl.BlockSpec((8, O_PAD), lambda i: (0, 0)),
        ),
        scratch_shapes=[
            pltpu.VMEM((3, HID, 128), F32),
            pltpu.VMEM((O_PAD, 128), F32),
            pltpu.VMEM((8, r), F32),
        ],
        compiler_params=vmem(63),
        cost_estimate=cost(40),
        name="fine_block",
    )(
        hist, later_observed.T, counted_flags.T, look, lens, th,
        wf, btab_t, ftab, ftab_t, fine_offs, abscol,
        m2, m3, fine_offs_p,
    )

    wide = 768
    f_shapes = (
        jax.ShapeDtypeStruct((HID // 2, F_ALL), F32),
        jax.ShapeDtypeStruct((HID // 2, F_ALL), BF16),
    )

    f_keep, f_send = pl.pallas_call(
        fine_in_grad_kernel,
        grid=(T_PAD // wide,),
        out_shape=f_shapes,
        in_specs=[fixed((HID, rows)), spec((wide, rows), lambda i: (i, 0))],
        out_specs=tuple([spec((HID // 2, wide), lambda i: (0, i))] * 2),
        compiler_params=vmem(32),
        cost_estimate=cost(10),
        name="fine_in_grad",
    )(dz1, res)
    rest = (dz2, a1, dz3, a2, a3, dz4, abscol)
    f_keep, f_send = pl.pallas_call(
        fine_rest_grad_kernel,
        grid=(tiles,),
        out_shape=f_shapes,
        in_specs=[col_spec(HID)] * 5
        + [col_spec(O_PAD), fixed((HID, 1))]
        + [pl.BlockSpec(memory_space=pl.ANY)] * 2,
        out_specs=tuple([pl.BlockSpec(memory_space=pl.ANY)] * 2),
        scratch_shapes=[
            pltpu.VMEM((HID, F_ALL - F_M2), F32),
            pltpu.VMEM((HID // 2, F_ALL - F_M2), F32),
            pltpu.VMEM((HID // 2, F_ALL - F_M2), BF16),
            pltpu.SemaphoreType.DMA((3, 2)),
        ],
        input_output_aliases={7: 0, 8: 1},
        compiler_params=vmem(50),
        cost_estimate=cost(6),
        name="fine_rest_grad",
    )(*rest, f_keep, f_send)

    def backward(which, fore, before):
        steps = side // r
        at = which * steps
        first = not before
        if first:
            shapes = (jax.ShapeDtypeStruct((HID, C_ALL), F32),)
        else:
            shapes = (
                jax.ShapeDtypeStruct((HID // 2, C_ALL), F32),
                jax.ShapeDtypeStruct((HID // 2, C_ALL), BF16),
            )
        shapes += (jax.ShapeDtypeStruct((8, HID), F32),)

        def rows_of(height):
            return col_spec(height, at, at + steps - 1)

        tall = pltpu.VMEM((HID, side), BF16)
        return pl.pallas_call(
            functools.partial(back_kernel, first),
            grid=(steps + 1,),
            out_shape=shapes,
            in_specs=[
                rows_of(HID),
                rows_of(256),
                rows_of(1),
                rows_of(HID),
                fixed((HID, T_PAD)),
                fixed((256, T_PAD)),
                fixed((HID, C_ALL)),
                fixed((HID, 1)),
                fixed((HID, HID)),
                fixed((HID, HID)),
                fixed((HID, 8)),
            ]
            + [fixed((HID, C_ALL)) for _ in before],
            out_specs=tuple(pl.BlockSpec(s.shape, lambda i: (0, 0)) for s in shapes),
            scratch_shapes=[
                *[tall] * 7,
                pltpu.VMEM((256, side), BF16),
                pltpu.VMEM((3, HID, 128), F32),
                pltpu.VMEM((256, 128), F32),
            ],
            compiler_params=vmem(60),
            cost_estimate=cost(12),
            name="coarse_backward",
        )(dz1, fore, lens, pooled, wf, btab, wc, abscol, m0, m1, coarse_offs_p, *before)

    def added(keep, got):
        return keep + got.astype(F32)

    def cut_rows(x):
        half = x.shape[0] // 2
        return x[:half], x[half:]

    def send_rows(x, bit_dp, bit_fsdp):
        keep, send = cut_rows(x)
        return keep, exchange(send.astype(BF16), bit_dp, bit_fsdp)

    up = bits_of(dp)
    pairs = list(zip(up, reversed(up)))

    got = exchange(f_send, 0, 1)
    fore, f_keep = together((fore, f_keep))
    c_part, c_small0 = backward(0, fore, ())
    got, c_part = together((got, c_part))
    f_a, f_b = cut_rows(added(f_keep, got))
    (first, second), *pairs_left = pairs
    f_a, got_a = send_rows(f_a, first, 0)
    f_b, got_b = send_rows(f_b, second, 0)
    fore, f_a, f_b = together((fore, f_a, f_b))
    c_keep, c_send, c_small = backward(1, fore, (c_part,))
    got_a, got_b, c_keep, c_send = together((got_a, got_b, c_keep, c_send))
    f_a, f_b = added(f_a, got_a), added(f_b, got_b)
    c_small = c_small + c_small0

    def scatter_rest(a, b, pairs):
        for first, second in pairs:
            a, got_a = send_rows(a, first, 0)
            b, got_b = send_rows(b, second, 0)
            a, b = added(a, got_a), added(b, got_b)
        x = join(a, b)
        for bit in bits_of(fsdp)[1:]:
            x, got = send_rows(x, 0, bit)
            x = added(x, got)
        return x

    def share_rows(x):
        a, b = cut_rows(x)
        for first, second in zip(reversed(up), up):
            a2, b2 = exchange(a, first, 0), exchange(b, second, 0)
            a, b = join(a, a2), join(b, b2)
        return join(a, b)

    gf_part = scatter_rest(f_a, f_b, pairs_left)
    c_a, c_b = cut_rows(added(c_keep, exchange(c_send, 0, 1)))
    gc_part = scatter_rest(c_a, c_b, pairs)
    gf = share_rows(gf_part)
    gc = share_rows(gc_part)

    rel = np.arange(part)
    lo, hi = rel[: part // 2], rel[part // 2 :]
    for first, second in zip(reversed(bits_of(dp)), bits_of(dp)):
        lo = np.concatenate([lo, lo ^ (first * part)])
        hi = np.concatenate([hi, hi ^ (second * part)])
    relrow = (
        jnp.asarray(np.concatenate([lo, hi]), jnp.int32) ^ (d_here * part)
    ).reshape(share, 1)

    squares = jnp.sum(gf_part * gf_part) + jnp.sum(gc_part * gc_part)
    small = jnp.concatenate([f_small, c_small], 1)
    small = jnp.where(
        (iota(small.shape, 0) == 6) & (iota(small.shape, 1) == 0), squares, small
    )
    for bit in bits_of(dp):
        small = small + exchange(small, bit, 0)
    for bit in bits_of(fsdp):
        small = small + exchange(small, 0, bit)
    bias_sum = jnp.concatenate(
        [
            small[0:3, O_PAD : O_PAD + HID].reshape(-1),
            small[0:3, 0:HID].reshape(-1),
            small[3, O_PAD : O_PAD + BACK + FORE],
            small[3, 0:OUTLOOK],
        ]
    )
    loss_sum = small[4, 0]
    usable_tally = small[5, 0]
    total_square = small[6, 0] + jnp.sum(bias_sum * bias_sum)
    grad_norm = jnp.sqrt(total_square) / usable_tally
    factor = clip_level / jnp.maximum(grad_norm, clip_level)
    scale = factor / usable_tally

    shards = (
        *shard_now,
        *by_hidden(
            coarse_in_mean, middle_mean, rough_final_first, fine_in_mean, sharp_final_first
        ),
        *by_hidden(
            coarse_in_square, middle_square, rough_final_second, fine_in_square,
            sharp_final_second,
        ),
    )
    new = pl.pallas_call(
        adam_kernel,
        out_shape=tuple(jax.ShapeDtypeStruct(x.shape, F32) for x in shards),
        grid=(1,),
        in_specs=[pl.BlockSpec(memory_space=pltpu.SMEM)] + one_step((gc, gf, relrow, *shards)),
        out_specs=tuple(one_step(shards)),
        compiler_params=vmem(60),
        cost_estimate=cost(6),
        name="adam",
    )(scale.reshape(1, 1), gc, gf, relrow, *shards)
    bias_new = adam_math(offset_vectors, biases_mean, biases_square, bias_sum * scale)
    return (
        loss_sum, usable_tally, grad_norm,
        *by_hidden(*new[0:5]), bias_new[0],
        *by_hidden(*new[5:10]), bias_new[1],
        *by_hidden(*new[10:15]), bias_new[2],
    )


def solution(mesh):
    rows2 = P(("dp", "fsdp"), None)
    rows1 = P(("dp", "fsdp"))
    weights = (P(None, "fsdp"), P(None, None, "fsdp"), P("fsdp", None), P(None, "fsdp"), P("fsdp", None), P())
    in_specs = (rows2, rows2, rows1, rows2, rows1) + weights * 3
    out_specs = (P(), P(), P()) + weights * 3
    return jax.shard_map(body, mesh=mesh, in_specs=in_specs, out_specs=out_specs, check_vma=False)
```

```python
import functools

import jax
import jax.numpy as jnp
import numpy as np
from jax import lax
from jax.experimental import pallas as pl
from jax.experimental.pallas import tpu as pltpu
from jax.sharding import PartitionSpec as P

LOOKBACK = 3600
OUTLOOK = 720
HID = 512
SERIES = 1024
STEP = 10
LP = 450
BACK = 150
FORE = 30
RATIO = 24
beta_first = 0.9
beta_second = 0.999
learn_rate = 0.01
weight_decay = 0.01
adam_epsilon = 1e-08
clip_level = 0.01

C_IN, C_M0, C_M1, C_OUT, C_ALL = 0, 512, 1024, 1536, 1792
R_M2, R_M3, R_OUT, R_ALL = 0, 512, 1024, 1792
T_PAD = 3840
F_ALL = T_PAD + R_ALL
LATEST = 2700
T_LIVE = 3712
T_WHOLE = 3584
O_PAD = 768
TILE = 256
CINV_AT = 180

F32 = jnp.float32
BF16 = jnp.bfloat16
NN = (((1,), (0,)), ((), ()))
NT = (((1,), (1,)), ((), ()))
TN = (((0,), (0,)), ((), ()))


def mm(a, b, dims=NN):
    return lax.dot_general(a, b, dims, preferred_element_type=F32)


def iota(shape, axis):
    return lax.broadcasted_iota(jnp.int32, shape, axis)


def split3(v):
    hi = v.astype(BF16)
    rest = v - hi.astype(F32)
    mid = rest.astype(BF16)
    return hi, mid, (rest - mid.astype(F32)).astype(BF16)


def mm_exact(v, sel, dims=NN):
    hi, mid, low = split3(v)
    return mm(hi, sel, dims) + mm(mid, sel, dims) + mm(low, sel, dims)


def mm_exact2(sel, v, dims=NN):
    hi, mid, low = split3(v)
    return mm(sel, hi, dims) + mm(sel, mid, dims) + mm(sel, low, dims)


def activate(h):
    u = 1.0 + jnp.tanh(h)
    return h * u, u


def slope_once(h, u, value):
    return u * ((0.5 + h) - 0.5 * value)


def slope_twice(h, u, value):
    return u * ((1.0 + h) + (h - value))


def cost(micros):
    return pl.CostEstimate(
        flops=int(micros * 1.15e9), bytes_accessed=int(micros * 3e6), transcendentals=0
    )


def mask_rows(value, lo, begin):
    if lo >= LATEST:
        return value
    seen = iota(value.shape, 0) >= begin - lo
    return jnp.where(seen, value, jnp.zeros_like(value))


def vmem(limit=60):
    return pltpu.CompilerParams(vmem_limit_bytes=limit * 1024 * 1024)


def bits_of(size):
    return [1 << b for b in range(size.bit_length() - 1)]


def swap(x, dp, fsdp, bit_dp, bit_fsdp):
    pairs = []
    for d in range(dp):
        for f in range(fsdp):
            pairs.append((d * fsdp + f, (d ^ bit_dp) * fsdp + (f ^ bit_fsdp)))
    return lax.ppermute(x, ("dp", "fsdp"), pairs)


def gather_rows(x, dp, fsdp, swap_fn, join):
    far = bits_of(fsdp)
    for bit in reversed(far[1:]):
        x = join(x, swap_fn(x, 0, bit))
    half = x.shape[0] // 2
    a, b = x[:half], x[half:]
    for first, second in zip(reversed(bits_of(dp)), bits_of(dp)):
        a2 = swap_fn(a, first, 0)
        b2 = swap_fn(b, second, 0)
        a, b = join(a, a2), join(b, b2)
    x = join(a, b)
    return join(x, swap_fn(x, 0, far[0]))


def row_order(dp, fsdp):
    share = HID // fsdp
    part = share // dp
    start = np.arange(part)

    def shifted(x, bit_dp, bit_fsdp):
        return x ^ (bit_fsdp * share + bit_dp * part)

    return gather_rows(
        start, dp, fsdp, shifted, lambda p, q: np.concatenate([p, q])
    )


def pack_kernel(d_ref, cin, mid, cout, fin, fout, wx, w1):
    share = cout.shape[0]
    part = wx.shape[0]
    rows = max(part, 16)
    sel = (iota((rows, share), 1) == d_ref[0] * part + iota((rows, share), 0)).astype(BF16)
    wx[...] = jnp.zeros_like(wx)
    w1[:, T_WHOLE:T_PAD] = jnp.zeros((share, T_PAD - T_WHOLE), BF16)
    w1[:, 0:LOOKBACK] = (fin[...] * 0.5).astype(BF16)

    def put(at, value, scale=0.5):
        picked = mm(sel, value.astype(BF16)) * scale
        wx[:, at : at + value.shape[1]] = picked[:part].astype(BF16)

    put(C_IN, cin[...])
    put(C_M0, mid[0])
    put(C_M1, mid[1])
    put(C_OUT, cout[...], 1.0)
    put(C_ALL + R_M2, mid[2])
    put(C_ALL + R_M3, mid[3])
    put(C_ALL + R_OUT, fout[...], 1.0)


def stats_kernel(count, *refs):
    pooled, table = refs[-2:]
    lens, series = refs[count : count + 2]
    hists = refs[:count]
    wide = hists[0].shape[1]

    @pl.when(pl.program_id(0) == 0)
    def _():
        table[...] = jnp.zeros_like(table)

    chunk = 32
    at = LP // chunk * chunk
    rest = LP - at
    base = iota((chunk, wide), 0) * 8
    pooled[at:HID, :] = jnp.zeros((HID - at, pooled.shape[1]), F32)
    for q, hist in enumerate(hists):
        cols = slice(q * wide, (q + 1) * wide)
        begin = LOOKBACK - lens[:, cols]
        sums = jnp.zeros((8, wide), F32)
        squares = jnp.zeros((8, wide), F32)

        def load(g, s, count):
            h = hist[pl.ds(g * 8 + s, count, stride=8), :]
            if g * 8 >= LATEST:
                return h
            return jnp.where(base[0:count] >= begin - (g * 8 + s), h, 0.0)

        for g in range(0, at, chunk):
            total = load(g, 0, chunk)
            sq = total * total
            for s in range(1, 8):
                h = load(g, s, chunk)
                total += h
                sq += h * h
            for v in range(0, chunk, 8):
                sums += total[v : v + 8]
                squares += sq[v : v + 8]
            pooled[g : g + chunk, cols] = total * 0.125
        total = load(at, 0, rest)
        sq = total * total
        for s in range(1, 8):
            h = load(at, s, rest)
            total += h
            sq += h * h
        pooled[at:LP, cols] = total * 0.125
        sum_row = jnp.sum(sums, 0, keepdims=True) + jnp.sum(total, 0, keepdims=True)
        square_row = jnp.sum(squares, 0, keepdims=True) + jnp.sum(sq, 0, keepdims=True)
        row = iota((16, wide), 0)
        kind = row % 3
        v = jnp.where(
            kind == 0,
            sum_row,
            jnp.where(kind == 1, square_row, lens[:, cols].astype(F32)),
        )
        hi, mid, low = split3(v)
        piece = jnp.where(
            row < 3,
            hi.astype(F32),
            jnp.where(row < 6, mid.astype(F32), jnp.where(row < 9, low.astype(F32), 0.0)),
        ).astype(BF16)
        hot = (iota((SERIES, wide), 0) == series[:, cols]).astype(BF16)
        t = mm(piece, hot, NT)
        table[0:3, :] += t[0:3] + t[3:6] + t[6:9]


def coarse_kernel(p_in, lens, series, table, x_top, x_low, offs, abscol,
                  pooled_out, th_out, look_out, wc, offs_p, looker):
    cols = p_in.shape[1]

    @pl.when(pl.program_id(0) == 0)
    def _():
        perm = perm_of(abscol)
        half = HID // 2
        wc[0:half, :] = x_top[...]
        wc[half:HID, :] = x_low[...]
        for at in (C_M0, C_M1):
            wc[:, at : at + HID] = mm(wc[:, at : at + HID], perm, NT).astype(BF16)
        offs_p[...] = mm_exact2(perm, offs[0:HID, :])
        count = jnp.maximum(table[2:3, :], 1.0)
        centre = table[0:1, :] / count
        spread = jnp.sqrt(table[1:2, :] / count + 1e-05)
        inverse = 1.0 / spread
        shifted = centre / spread
        row = iota((16, SERIES), 0)
        v = jnp.where(row < 3, inverse, shifted)
        hi, mid, low = split3(v)
        kind = row % 3
        looker[...] = jnp.where(
            row < 6,
            jnp.where(
                kind == 0,
                hi.astype(F32),
                jnp.where(kind == 1, mid.astype(F32), low.astype(F32)),
            ),
            0.0,
        ).astype(BF16)

    hot = (iota((SERIES, cols), 0) == series[...]).astype(BF16)
    got = mm(looker[...], hot)
    inv = got[0:1] + got[1:2] + got[2:3]
    cinv = got[3:4] + got[4:5] + got[5:6]
    look_out[...] = jnp.where(iota((8, cols), 0) == 0, inv, cinv)
    group = iota((HID, cols), 0)
    begin = LOOKBACK - lens[...]
    share = jnp.clip(group * 8 + 8 - begin, 0, 8).astype(F32) * 0.125
    pooled = jnp.where(group < LP, p_in[...] * inv - cinv * share, 0.0).astype(BF16)
    pooled_out[...] = pooled
    v = activate(mm(wc[:, C_IN : C_IN + HID], pooled) + offs_p[:, 0:1])[0]
    v = activate(mm(wc[:, C_M0:C_M1], v.astype(BF16)) + offs_p[:, 1:2])[0]
    v = activate(mm(wc[:, C_M1:C_OUT], v.astype(BF16)) + offs_p[:, 2:3])[0]
    theta = mm(wc[:, C_OUT:C_ALL], v.astype(BF16), TN) + offs[0:256, 3:4]
    theta = theta * (1.0 / 48.0)
    hi = theta.astype(BF16).astype(F32)
    at = iota((256, cols), 0)
    c_hi, c_mid, c_low = split3(cinv)
    with_shift = jnp.where(
        at == CINV_AT,
        c_hi.astype(F32),
        jnp.where(
            at == CINV_AT + 1,
            c_mid.astype(F32),
            jnp.where(at == CINV_AT + 2, c_low.astype(F32), hi),
        ),
    )
    th_out[...] = with_shift.astype(BF16)


def fold_lanes(x):
    total = x[:, 0:128]
    for at in range(128, x.shape[1], 128):
        total = total + x[:, at : at + 128]
    return total


def hidden_rows(acc, perm):
    lane = iota((HID, 128), 1)
    v = jnp.zeros((HID, 128), F32)
    for k in range(3):
        v = jnp.where(lane == k, jnp.sum(acc[k], 1, keepdims=True), v)
    return mm_exact(v, perm, TN)[0:8]


def last_row(acc):
    v = jnp.broadcast_to(jnp.sum(acc, 1, keepdims=True), acc.shape)
    return jnp.transpose(v, (1, 0))[0:8]


def perm_of(abscol):
    return (iota((HID, HID), 1) == abscol[...]).astype(BF16)


def fine_kernel(hist, later, flags, look, lens, th, w1, x_top, x_low, btab_t, ftab, ftab_t, offs, abscol,
                res, dz1, dz1_p, fore, small, keep, send,
                acc, acc4, acc_loss, dz4, total, wr, offs_p, perm):
    cols = hist.shape[1]
    step = pl.program_id(0)

    @pl.when(step == 0)
    def _():
        acc[...] = jnp.zeros_like(acc)
        acc4[...] = jnp.zeros_like(acc4)
        acc_loss[...] = jnp.zeros_like(acc_loss)
        perm[...] = perm_of(abscol)
        wr[0 : HID // 2, :] = x_top[...]
        wr[HID // 2 : HID, :] = x_low[...]
        wr[:, R_M3:R_OUT] = mm(wr[:, R_M3:R_OUT], perm[...], NT).astype(BF16)
        offs_p[...] = mm_exact2(perm[...], offs[0:HID, :])
        total[...] = jnp.zeros_like(total)
        dz4[OUTLOOK:O_PAD, :] = jnp.zeros((O_PAD - OUTLOOK, cols), BF16)

    inv = look[0:1, :]
    cinv = look[1:2, :]
    begin = LOOKBACK - lens[...]
    th_hi = th[...]
    res[LOOKBACK:T_PAD, :] = jnp.zeros((T_PAD - LOOKBACK, cols), BF16)
    h1 = offs[0:HID, 0:1]
    for at in range(0, T_LIVE, 1024):
        end = min(at + 1024, T_LIVE)
        for lo in range(at, min(end, LOOKBACK), 512):
            width = min(512, LOOKBACK - lo)
            shift = mm(btab_t[lo : lo + width, :], th_hi)
            r = hist[lo : lo + width, :] * inv - shift
            res[lo : lo + width, :] = mask_rows(r, lo, begin).astype(BF16)
        h1 = h1 + mm(w1[:, at:end], res[at:end, :])
    v1, u1 = activate(h1)
    b1 = v1.astype(BF16)
    h2 = mm(wr[:, R_M2:R_M3], b1) + offs_p[:, 1:2]
    v2, u2 = activate(h2)
    b2 = v2.astype(BF16)
    h3 = mm(wr[:, R_M3:R_OUT], b2) + offs_p[:, 2:3]
    v3, u3 = activate(h3)
    b3 = v3.astype(BF16)
    est = mm(wr[:, R_OUT:R_ALL], b3, TN) + mm(ftab_t[...], th_hi) + offs[:, 3:4]
    counted = flags[...].astype(F32)
    err = (est[0:OUTLOOK] - (later[...] * inv - cinv)) * counted
    acc_loss[0:1, :] += jnp.sum(err * err, 0, keepdims=True)
    acc_loss[1:2, :] += jnp.sum(counted, 0, keepdims=True)
    d4 = (2.0 * err).astype(BF16)
    acc4[0:OUTLOOK, :] += fold_lanes(d4.astype(F32))
    dz4[0:OUTLOOK, :] = d4
    d4 = dz4[...]
    fore[...] = mm(ftab[...], d4) * (1.0 / 48.0)

    def back(upstream, slope, row):
        d = (upstream * slope).astype(BF16)
        acc[row] += fold_lanes(d.astype(F32))
        return d

    d3 = back(mm(wr[:, R_OUT:R_ALL], d4), slope_once(h3, u3, v3), 2)
    total[:, R_OUT:R_ALL] += mm(b3, d4, NT)
    d2 = back(mm(wr[:, R_M3:R_OUT], d3, TN), slope_twice(h2, u2, v2), 1)
    total[:, R_M3:R_OUT] += mm(d3, b2, NT)
    d1 = back(mm(wr[:, R_M2:R_M3], d2, TN), slope_twice(h1, u1, v1), 0)
    dz1[...] = d1
    dz1_p[...] = mm(perm[...], d1).astype(BF16)
    total[:, R_M2:R_M3] += mm(d2, b1, NT)

    @pl.when(step == pl.num_programs(0) - 1)
    def _():
        small[...] = last_row(acc4[...])
        loss = jnp.sum(acc_loss[0:1, :], 1, keepdims=True)
        tally = jnp.sum(acc_loss[1:2, :], 1, keepdims=True)
        row = iota((8, O_PAD), 0)
        small[...] = jnp.where(
            row == 3,
            small[...],
            jnp.where(row == 4, loss, jnp.where(row == 5, tally, 0.0)),
        )
        half = HID // 2
        for cols_k in (slice(R_M2, R_M3), slice(R_M3, R_OUT), slice(R_OUT, R_ALL)):
            g = total[:, cols_k]
            if cols_k.start == R_M3:
                g = natural_columns(g, perm[...])
            keep[:, cols_k] = g[0:half]
            send[:, cols_k] = g[half:HID].astype(BF16)
        small[0:3, 0:HID] = hidden_rows(acc, perm[...])[0:3]
        small[0:1, 0:HID] = last_row(acc[0])[0:1]


def natural_columns(g, perm):
    half = HID // 2
    hi = g.astype(BF16)
    low = (g - hi.astype(F32)).astype(BF16)
    out = mm(hi, perm)
    return jnp.concatenate([out[0:half] + mm(low[0:half], perm), out[half:HID]], 0)


def fine_in_grad_kernel(dz1, res, rest, out):
    step = pl.program_id(0)
    tile = out.shape[1]
    whole = T_PAD // tile

    def product(width):
        return mm(dz1[...], res[0:width, :], NT).astype(out.dtype)

    @pl.when(step < whole)
    def _():
        out[...] = product(tile)

    for k in range(whole, F_ALL // tile):

        @pl.when(step == k)
        def _():
            edge = max(T_PAD - k * tile, 0)
            if edge:
                out[:, 0:edge] = product(edge)
            begin = k * tile + edge - T_PAD
            out[:, edge:tile] = rest[:, begin : begin + tile - edge]


def back_kernel(first, final, *refs):
    dz1f, fore, lens, pooled, w1, btab, wc, abscol, offs_p = refs[:9]
    outs = refs[9 if first else 10 : -3]
    small = outs[-1]
    acc, acc4, total = refs[-3:]
    cols = dz1f.shape[1]
    step = pl.program_id(0)

    @pl.when(step == 0)
    def _():
        acc[...] = jnp.zeros_like(acc)
        acc4[...] = jnp.zeros_like(acc4)
        total[...] = jnp.zeros_like(total) if first else refs[9][...]

    begin = LOOKBACK - lens[...]
    d1f = dz1f[...]
    back_grad = jnp.zeros((256, cols), F32)
    for lo in range(0, T_LIVE, 512):
        width = min(512, T_LIVE - lo)
        d = mask_rows(mm(w1[:, lo : lo + width], d1f, TN), lo, begin).astype(BF16)
        back_grad += mm(btab[:, lo : lo + width], d)
    row = iota((256, cols), 0)
    d4 = (jnp.where(row < BACK, back_grad * (-2.0 / 48.0), 0.0) + fore[...]).astype(BF16)
    acc4[...] += fold_lanes(d4.astype(F32))

    def ahead(w, entering, k):
        h = mm(w, entering) + offs_p[:, k : k + 1]
        value, u = activate(h)
        return h, u, value, value.astype(BF16)

    p = pooled[...]
    h1, u1, v1, b1 = ahead(wc[:, C_IN : C_IN + HID], p, 0)
    h2, u2, v2, b2 = ahead(wc[:, C_M0:C_M1], b1, 1)
    h3, u3, v3, b3 = ahead(wc[:, C_M1:C_OUT], b2, 2)

    def back(upstream, slope, row):
        d = (upstream * slope).astype(BF16)
        acc[row] += fold_lanes(d.astype(F32))
        return d

    d3 = back(mm(wc[:, C_OUT:C_ALL], d4), slope_once(h3, u3, v3), 2)
    total[:, C_OUT:C_ALL] += mm(b3, d4, NT)
    d2 = back(mm(wc[:, C_M1:C_OUT], d3, TN), slope_twice(h2, u2, v2), 1)
    total[:, C_M1:C_OUT] += mm(d3, b2, NT)
    d1 = back(mm(wc[:, C_M0:C_M1], d2, TN), slope_twice(h1, u1, v1), 0)
    total[:, C_M0:C_M1] += mm(d2, b1, NT)
    total[:, C_IN:C_M0] += mm(d1, p, NT)

    @pl.when(step == pl.num_programs(0) - 1)
    def _():
        perm = perm_of(abscol)
        small[...] = jnp.zeros_like(small)
        small[0:3, :] = hidden_rows(acc, perm)[0:3]
        small[3:4, 0:256] = last_row(acc4[...])[0:1]
        if not final:
            outs[0][...] = total[...]
            return
        half = HID // 2
        for a, b in zip((C_IN, C_M0, C_M1, C_OUT), (C_M0, C_M1, C_OUT, C_ALL)):
            g = total[:, a:b]
            if a in (C_M0, C_M1):
                g = natural_columns(g, perm)
            outs[0][:, a:b] = g[0:half]
            outs[1][:, a:b] = g[half:HID].astype(BF16)


def adam_math(weight, mean_old, square_old, grad):
    mean_new = beta_first * mean_old + (1.0 - beta_first) * grad
    square_new = beta_second * square_old + (1.0 - beta_second) * grad * grad
    mean_hat = mean_new / (1.0 - beta_first**STEP)
    square_hat = square_new / (1.0 - beta_second**STEP)
    weight_new = weight - learn_rate * (
        mean_hat / (jnp.sqrt(square_hat) + adam_epsilon) + weight_decay * weight
    )
    return weight_new, mean_new, square_new


def adam_kernel(dp, small, relrow, *refs):
    pieces, refs = refs[: 2 * dp], refs[2 * dp :]
    ins, biases, outs, bias_outs = refs[:15], refs[15:18], refs[18:33], refs[33:36]
    loss, tally, norm, grads, bias_grad = refs[36:]
    part = pieces[0].shape[0]
    share = dp * part
    order = [0, *range(2, dp + 1), 1, *range(dp + 1, 2 * dp)]
    for k, index in enumerate(order):
        piece = pieces[index]
        at, row = (0, k) if k < dp else (F_ALL, k - dp)
        grads[row * part : (row + 1) * part, at : at + piece.shape[1]] = piece[...].astype(F32)
    place = (iota((share, share), 1) == relrow[...]).astype(BF16)

    count = small[5:6, 0:1]
    sums = small[0:4, :]
    bias_square = jnp.sum(jnp.sum(sums * sums, 0, keepdims=True), 1, keepdims=True)
    grad_norm = jnp.sqrt(small[6:7, 0:1] + bias_square) / count
    s = clip_level / jnp.maximum(grad_norm, clip_level) / count
    loss[...] = small[4:5, 0:1]
    tally[...] = count
    norm[...] = grad_norm
    for k in range(3):
        bias_grad[:, k * HID : (k + 1) * HID] = small[k : k + 1, O_PAD : O_PAD + HID]
        bias_grad[:, (k + 3) * HID : (k + 4) * HID] = small[k : k + 1, 0:HID]
    last = 6 * HID + BACK + FORE
    bias_grad[:, 6 * HID : last] = small[3:4, O_PAD : O_PAD + BACK + FORE]
    bias_grad[:, last : last + OUTLOOK] = small[3:4, 0:OUTLOOK]
    for out, value in zip(
        bias_outs, adam_math(*(x[...] for x in biases), bias_grad[...] * s)
    ):
        out[...] = value

    def step(i, at, width, index):
        g = grads[:, at : at + width]
        hi = g.astype(BF16)
        low = (g - hi.astype(F32)).astype(BF16)
        grad = (mm(place, hi, TN) + mm(place, low, TN)) * s
        old = [ins[i + 5 * k][index] for k in range(3)]
        for k, value in enumerate(adam_math(*old, grad)):
            outs[i + 5 * k][index] = value

    every = slice(None)
    step(0, F_ALL + C_IN, LP, (every, every))
    step(1, F_ALL + C_M0, HID, 0)
    step(1, F_ALL + C_M1, HID, 1)
    step(1, T_PAD + R_M2, HID, 2)
    step(1, T_PAD + R_M3, HID, 3)
    step(2, F_ALL + C_OUT, BACK + FORE, (every, every))
    step(4, T_PAD + R_OUT, OUTLOOK, (every, every))
    for lo in range(0, LOOKBACK, 512):
        width = min(512, LOOKBACK - lo)
        step(3, lo, width, (every, slice(lo, lo + width)))


def interp_table(count, length, first_row, rows, cols):
    spots = np.clip((np.arange(length) + 0.5) * (count / length) - 0.5, 0.0, count - 1.0)
    table = np.maximum(0.0, 1.0 - np.abs(spots[None, :] - np.arange(count)[:, None]))
    out = np.zeros((rows, cols), np.float32)
    out[first_row : first_row + count, :length] = np.round(table * 48.0)
    return out


def assemble_kernel(plan, count, *refs):
    ins, outs = refs[:count], refs[count:]
    for which, begin, at, size, out in plan:
        outs[out][at : at + size, :] = ins[which][begin : begin + size, :]


def assemble(*outs):
    if any(n % 16 or b % 16 for out in outs for _, b, n in out):
        return [
            jnp.concatenate([x[b : b + n] for x, b, n in out], 0) for out in outs
        ]
    ins, plan, shapes = [], [], []
    for k, out in enumerate(outs):
        at = 0
        for x, begin, size in out:
            which = next((i for i, y in enumerate(ins) if y is x), len(ins))
            if which == len(ins):
                ins.append(x)
            plan.append((which, begin, at, size, k))
            at += size
        shapes.append(jax.ShapeDtypeStruct((at, out[0][0].shape[1]), out[0][0].dtype))
    def blocks(arrays):
        return [pl.BlockSpec(x.shape, lambda i: (0, 0)) for x in arrays]

    return pl.pallas_call(
        functools.partial(assemble_kernel, tuple(plan), len(ins)),
        grid=(1,),
        out_shape=tuple(shapes),
        in_specs=blocks(ins),
        out_specs=tuple(blocks(shapes)),
        compiler_params=vmem(63),
        cost_estimate=cost(1),
        name="assemble",
    )(*ins)


def add_rows(pairs, plan):
    sums = [keep + got.astype(F32) for keep, got in pairs]
    return [
        sums[which][begin : begin + size].astype(kind) for which, begin, size, kind in plan
    ]


def spec(shape, index):
    return pl.BlockSpec(shape, index)


def fixed(shape):
    return pl.BlockSpec(shape, lambda i: (0,) * len(shape), pipeline_mode=pl.Buffered(1))


def body(
    history, later_observed, lengths, counted_flags, series,
    coarse_in, middle, rough_final_matrix, fine_in, sharp_final_matrix, offset_vectors,
    coarse_in_mean, middle_mean, rough_final_first, fine_in_mean, sharp_final_first, biases_mean,
    coarse_in_square, middle_square, rough_final_second, fine_in_square, sharp_final_second,
    biases_square,
):
    dp, fsdp = lax.axis_size("dp"), lax.axis_size("fsdp")
    d_here, f_here = lax.axis_index("dp"), lax.axis_index("fsdp")
    rows = history.shape[0]
    share = HID // fsdp
    part = share // dp

    def exchange(x, bit_dp, bit_fsdp):
        return swap(x, dp, fsdp, bit_dp, bit_fsdp)

    def join(p, q):
        return jnp.concatenate([p, q], 0)

    here = f_here * share + d_here * part
    order = row_order(dp, fsdp)
    abscol = (jnp.asarray(order, jnp.int32) ^ here).reshape(HID, 1)
    together = lax.optimization_barrier

    def by_hidden(cin, mid, cout, fin, fout):
        return (cin.T, mid.transpose(0, 2, 1), cout, fin.T, fout)

    def one_step(arrays):
        return [
            pl.BlockSpec(x.shape, lambda i, n=len(x.shape): (0,) * n) for x in arrays
        ]

    shard_now = by_hidden(
        coarse_in, middle, rough_final_matrix, fine_in, sharp_final_matrix
    )

    x_part, w1_part = pl.pallas_call(
        pack_kernel,
        out_shape=(
            jax.ShapeDtypeStruct((part, C_ALL + R_ALL), BF16),
            jax.ShapeDtypeStruct((share, T_PAD), BF16),
        ),
        grid=(1,),
        in_specs=[pl.BlockSpec(memory_space=pltpu.SMEM)] + one_step(shard_now),
        out_specs=(
            pl.BlockSpec((part, C_ALL + R_ALL), lambda i: (0, 0)),
            pl.BlockSpec((share, T_PAD), lambda i: (0, 0)),
        ),
        compiler_params=vmem(63),
        cost_estimate=cost(1),
        name="pack_weights",
    )(d_here.reshape(1), *shard_now)

    hist = history.T
    lens = lengths.reshape(1, rows)
    series_row = series.reshape(1, rows)
    side = rows // 2
    calls = (1, 1, 2)

    def stats(which, lens_row, pool):
        count = 2
        unit = rows // (128 * count * sum(calls))
        steps = calls[which] * unit
        at = sum(calls[:which]) * unit

        def hist_spec(q):
            return spec((LOOKBACK, 128), lambda i: (0, (at + i) * count + q))

        def row_spec():
            return spec((1, 128 * count), lambda i: (0, at + i))

        return pl.pallas_call(
            functools.partial(stats_kernel, count),
            grid=(steps,),
            out_shape=(
                jax.ShapeDtypeStruct((HID, rows), F32),
                jax.ShapeDtypeStruct((8, SERIES), F32),
            ),
            in_specs=[hist_spec(q) for q in range(count)]
            + [row_spec(), row_spec()]
            + [pl.BlockSpec(memory_space=pl.ANY) for _ in pool],
            out_specs=(
                spec((HID, 128 * count), lambda i: (0, at + i)),
                pl.BlockSpec((8, SERIES), lambda i: (0, 0)),
            ),
            compiler_params=vmem(63),
            cost_estimate=cost(6),
            input_output_aliases={count + 2: 0} if pool else {},
            name="window_stats",
        )(*[hist] * count, lens_row, series_row, *pool)

    up, down = bits_of(dp), bits_of(dp)[::-1]
    near, *far = bits_of(fsdp)
    moves = [(0, bit) for bit in reversed(far)] + list(zip(down, up)) + [(0, near)]

    def cut_rows(x):
        half = x.shape[0] // 2
        return x[:half], x[half:]

    def add_over(table, steps):
        for bit_dp, bit_fsdp in steps:
            table = table + exchange(table, bit_dp, bit_fsdp)
        return table

    x = [x_part]
    pools, tables, table = [], [], None
    sums = [[(0, bit) for bit in bits_of(fsdp)], [(bit, 0) for bit in up]]
    for k, move in enumerate(moves[:-1]):
        along_dp = k >= len(far)
        if along_dp and len(x) == 1:
            x = list(cut_rows(x[0]))
        got = [exchange(h, b, 0) for h, b in zip(x, move)] if along_dp else [exchange(x[0], *move)]
        if k < len(calls):
            lens_row, *x = together((lens, *x))
            pool, this = stats(k, lens_row, pools[-1:])
            pools.append(pool)
            *got, this = together((*got, this))
            tables.append(this)
        elif sums:
            if table is None:
                table = sum(tables[1:], tables[0])
            table = add_over(table, sums.pop(0))
            *got, table = together((*got, table))
        if k == len(far) - 1:
            w1_part, *got = together((w1_part, *got))
            w1 = lax.all_gather(w1_part, "fsdp", axis=0, tiled=True)
        if k < len(moves) - 2:
            x = [join(h, g) for h, g in zip(x, got)]
    x_top = assemble(
        [(h, 0, h.shape[0]) for pair in zip(x, got) for h in pair]
    )[0]
    x_low = exchange(x_top, *moves[-1])
    for steps in sums:
        table = add_over(table, steps)

    hidden = offset_vectors[: 6 * HID].reshape(6, HID)
    rough_bias = offset_vectors[6 * HID : 6 * HID + BACK + FORE]
    sharp_bias = offset_vectors[6 * HID + BACK + FORE :]

    def bias_cols(three, last, width):
        out = jnp.pad(three, ((0, 0), (0, width - HID)))
        out = join(out, jnp.pad(last, (0, width - last.shape[0]))[None])
        return jnp.pad(out, ((0, 4), (0, 0))).T

    coarse_offs = bias_cols(0.5 * hidden[:3], rough_bias, HID)
    fine_offs = bias_cols(0.5 * hidden[3:], sharp_bias, O_PAD)

    r = 512
    tiles = rows // r

    def col_spec(height, begin=0, last=tiles - 1):
        return spec((height, r), lambda i: (0, jnp.minimum(begin + i, last)))

    half_block = pl.BlockSpec(
        (HID // 2, C_ALL), lambda i: (0, 0), pipeline_mode=pl.Buffered(1)
    )
    pooled, th, look, wc, offs_p = pl.pallas_call(
        coarse_kernel,
        grid=(tiles,),
        out_shape=(
            jax.ShapeDtypeStruct((HID, rows), BF16),
            jax.ShapeDtypeStruct((256, rows), BF16),
            jax.ShapeDtypeStruct((8, rows), F32),
            jax.ShapeDtypeStruct((HID, C_ALL), BF16),
            jax.ShapeDtypeStruct((HID, 8), F32),
        ),
        in_specs=[
            col_spec(HID),
            col_spec(1),
            col_spec(1),
            fixed((8, SERIES)),
            half_block,
            half_block,
            fixed((HID, 8)),
            fixed((HID, 1)),
        ],
        out_specs=(
            col_spec(HID),
            col_spec(256),
            col_spec(8),
            pl.BlockSpec((HID, C_ALL), lambda i: (0, 0)),
            pl.BlockSpec((HID, 8), lambda i: (0, 0)),
        ),
        scratch_shapes=[pltpu.VMEM((16, SERIES), BF16)],
        compiler_params=vmem(63),
        cost_estimate=cost(10),
        name="coarse_forward",
    )(
        pools[-1], lens, series_row, table, x_top, x_low, coarse_offs, abscol,
    )
    back_table = interp_table(BACK, LOOKBACK, 0, 256, T_PAD)
    btab = jnp.asarray(back_table, BF16)
    back_table[CINV_AT : CINV_AT + 3, :LOOKBACK] = 1.0
    btab_t = jnp.asarray(back_table.T, BF16)
    fore_table = interp_table(FORE, OUTLOOK, BACK, 256, O_PAD)
    ftab = jnp.asarray(fore_table, BF16)
    ftab_t = jnp.asarray(fore_table.T, BF16)

    tall = jax.ShapeDtypeStruct((HID, rows), BF16)
    r_shapes = (
        jax.ShapeDtypeStruct((HID // 2, R_ALL), F32),
        jax.ShapeDtypeStruct((HID // 2, R_ALL), BF16),
    )
    rest_block = pl.BlockSpec(
        (HID // 2, R_ALL), lambda i: (0, 1), pipeline_mode=pl.Buffered(1)
    )
    res, dz1, dz1_p, fore, f_small, r_keep, r_send = pl.pallas_call(
        fine_kernel,
        grid=(tiles,),
        out_shape=(
            jax.ShapeDtypeStruct((T_PAD, rows), BF16),
            tall,
            tall,
            jax.ShapeDtypeStruct((256, rows), F32),
            jax.ShapeDtypeStruct((8, O_PAD), F32),
            *r_shapes,
        ),
        in_specs=[
            col_spec(LOOKBACK),
            col_spec(OUTLOOK),
            col_spec(OUTLOOK),
            col_spec(8),
            col_spec(1),
            col_spec(256),
            fixed((HID, T_PAD)),
            rest_block,
            rest_block,
            fixed((T_PAD, 256)),
            fixed((256, O_PAD)),
            fixed((O_PAD, 256)),
            fixed((O_PAD, 8)),
            fixed((HID, 1)),
        ],
        out_specs=(
            col_spec(T_PAD),
            col_spec(HID),
            col_spec(HID),
            col_spec(256),
            pl.BlockSpec((8, O_PAD), lambda i: (0, 0)),
            *[pl.BlockSpec((HID // 2, R_ALL), lambda i: (0, 0))] * 2,
        ),
        scratch_shapes=[
            pltpu.VMEM((3, HID, 128), F32),
            pltpu.VMEM((O_PAD, 128), F32),
            pltpu.VMEM((8, r), F32),
            pltpu.VMEM((O_PAD, r), BF16),
            pltpu.VMEM((HID, R_ALL), F32),
            pltpu.VMEM((HID, R_ALL), BF16),
            pltpu.VMEM((HID, 8), F32),
            pltpu.VMEM((HID, HID), BF16),
        ],
        compiler_params=vmem(63),
        cost_estimate=cost(40),
        name="fine_block",
    )(
        hist, later_observed.T, counted_flags.T, look, lens, th,
        w1, x_top, x_low, btab_t, ftab, ftab_t, fine_offs, abscol,
    )

    wide = F_ALL // 4
    res_last = -(-T_PAD // wide) - 1

    def fine_in_grad(side, rest, kind):
        return pl.pallas_call(
            fine_in_grad_kernel,
            grid=(F_ALL // wide,),
            out_shape=jax.ShapeDtypeStruct((HID // 2, F_ALL), kind),
            in_specs=[
                pl.BlockSpec((HID // 2, rows), lambda i: (side, 0), pipeline_mode=pl.Buffered(1)),
                spec((wide, rows), lambda i: (jnp.minimum(i, res_last), 0)),
                fixed((HID // 2, R_ALL)),
            ],
            out_specs=spec((HID // 2, wide), lambda i: (0, i)),
            compiler_params=vmem(63),
            cost_estimate=cost(7),
            name="fine_in_grad",
        )(dz1_p, res, rest)

    def backward(at, steps, fore, before):
        first = not before
        final = at + steps == tiles
        half = HID // 2
        shapes = (
            [jax.ShapeDtypeStruct((HID, C_ALL), F32)]
            if not final
            else [jax.ShapeDtypeStruct((half, C_ALL), t) for t in (F32, BF16)]
        ) + [jax.ShapeDtypeStruct((8, HID), F32)]

        def rows_of(height):
            return col_spec(height, at)

        return pl.pallas_call(
            functools.partial(back_kernel, first, final),
            grid=(steps,),
            out_shape=tuple(shapes),
            in_specs=[
                rows_of(HID),
                rows_of(256),
                rows_of(1),
                rows_of(HID),
                fixed((HID, T_PAD)),
                fixed((256, T_PAD)),
                fixed((HID, C_ALL)),
                fixed((HID, 1)),
                fixed((HID, 8)),
            ]
            + [fixed(x.shape) for x in before],
            out_specs=tuple(pl.BlockSpec(s.shape, lambda i: (0, 0)) for s in shapes),
            scratch_shapes=[
                pltpu.VMEM((3, HID, 128), F32),
                pltpu.VMEM((256, 128), F32),
                pltpu.VMEM((HID, C_ALL), F32),
            ],
            compiler_params=vmem(63),
            cost_estimate=cost(17),
            name="coarse_backward",
        )(dz1, fore, lens, pooled, w1, btab, wc, abscol, offs_p, *before)

    legs = [(0, near)] + list(zip(up, down)) + [(0, bit) for bit in far]

    def split(j):
        return 1 <= j <= len(up)

    def sum_and_cut(pairs, j):
        n = pairs[0][0].shape[0]
        if j + 1 == len(legs):
            plan = [(0, 0, n, F32)]
        elif not split(j + 1):
            plan = [(0, 0, n, F32), (1, 0, n, BF16)] if len(pairs) == 2 else [
                (0, 0, n // 2, F32), (0, n // 2, n // 2, BF16)
            ]
        else:
            size = n // 2 if len(pairs) == 2 else n // 4
            plan = []
            for k in range(2):
                which, begin = (k, 0) if len(pairs) == 2 else (0, 2 * k * size)
                plan += [(which, begin, size, F32), (which, begin + size, size, BF16)]
        flat = add_rows(pairs, plan)
        return [tuple(flat[k : k + 2]) for k in range(0, len(flat), 2)]

    def travel(state, j):
        if split(j):
            return [exchange(send, bit, 0) for (_, send), bit in zip(state, legs[j])]
        return [exchange(state[0][1], *legs[j])]

    def kept(state, got):
        return [(pair[0], g) for pair, g in zip(state, got)]

    def beside(got, *others):
        return together((*got, *others))[: len(got)]

    def hold(state, value):
        return together((value, *(x for pair in state for x in pair)))[0]

    f_send = fine_in_grad(1, r_send, BF16)
    got = [exchange(f_send, 0, near)]
    r_keep, f_send = together((r_keep, f_send))
    f_keep = fine_in_grad(0, r_keep, F32)
    state = sum_and_cut([(f_keep, *beside(got, f_keep))], 0)
    quarter = max(tiles // 4, 1)
    smalls, c_part, at = [], (), 0
    for j, count in enumerate((tiles - 2 * quarter, quarter, quarter)):
        got = travel(state, j + 1)
        *c_part, this = backward(at, count, hold(state, fore), tuple(c_part))
        smalls.append(this)
        at += count
        both = together((*got, *c_part))
        got, c_part = both[: len(got)], both[len(got) :]
        state = sum_and_cut(kept(state, got), j + 1)
    f_state, f_leg = state, 4
    c_keep, c_send = c_part
    c_small = sum(smalls[1:], smalls[0])

    c_got = exchange(c_send, 0, near)
    f_got = travel(f_state, f_leg) if f_leg < len(legs) else None
    c_state = sum_and_cut([(c_keep, c_got)], 0)
    for j in range(1, len(legs)):
        got = travel(c_state, j)
        c_state = sum_and_cut(kept(c_state, got), j)
        if j == 1:
            while f_leg < len(legs):
                f_got = f_got or travel(f_state, f_leg)
                f_got = beside(f_got, *c_state[0])
                f_state = sum_and_cut(kept(f_state, f_got), f_leg)
                f_got, f_leg = None, f_leg + 1
            gf_part = f_state[0][0]
            f_wire = gf_part.astype(BF16)
            f_all = [f_wire] + [exchange(f_wire, d, 0) for d in range(1, dp)]
        if j == len(legs) - 2:
            flat = [x for pair in c_state for x in pair]
            *flat, = together((*flat, *f_all))
            f_all = flat[2 * len(c_state) :]
            c_state = [tuple(flat[2 * k : 2 * k + 2]) for k in range(len(c_state))]
    gc_part = c_state[0][0]
    c_all = [gc_part] + [exchange(gc_part, d, 0) for d in range(1, dp)]

    rel = np.concatenate([np.arange(part) ^ (d * part) for d in range(dp)])
    relrow = (jnp.asarray(rel, jnp.int32) ^ (d_here * part)).reshape(share, 1)

    squares = jnp.sum(gf_part * gf_part) + jnp.sum(gc_part * gc_part)
    small = jnp.concatenate([f_small, c_small], 1)
    small = jnp.where(
        (iota(small.shape, 0) == 6) & (iota(small.shape, 1) == 0), squares, small
    )
    small = add_over(small, [(bit, 0) for bit in up] + [(0, near)])
    *c_all, small = together((*c_all, small))
    small = add_over(small, [(0, bit) for bit in far])
    pieces = [f_all[0], c_all[0], *f_all[1:], *c_all[1:]]
    shards = (
        *shard_now,
        *by_hidden(
            coarse_in_mean, middle_mean, rough_final_first, fine_in_mean, sharp_final_first
        ),
        *by_hidden(
            coarse_in_square, middle_square, rough_final_second, fine_in_square,
            sharp_final_second,
        ),
    )
    biases = [x.reshape(1, -1) for x in (offset_vectors, biases_mean, biases_square)]
    given = (small, relrow, *pieces, *shards, *biases)
    results = tuple(jax.ShapeDtypeStruct(x.shape, F32) for x in (*shards, *biases)) + (
        jax.ShapeDtypeStruct((1, 1), F32),
    ) * 3
    new = pl.pallas_call(
        functools.partial(adam_kernel, dp),
        out_shape=results,
        grid=(1,),
        in_specs=one_step(given),
        out_specs=tuple(one_step(results)),
        scratch_shapes=[
            pltpu.VMEM((share, F_ALL + C_ALL), F32),
            pltpu.VMEM(biases[0].shape, F32),
        ],
        compiler_params=vmem(63),
        cost_estimate=cost(6),
        name="adam",
    )(*given)
    return (
        *(x.reshape(()) for x in new[18:21]),
        *by_hidden(*new[0:5]), new[15].reshape(-1),
        *by_hidden(*new[5:10]), new[16].reshape(-1),
        *by_hidden(*new[10:15]), new[17].reshape(-1),
    )


def solution(mesh):
    rows2 = P(("dp", "fsdp"), None)
    rows1 = P(("dp", "fsdp"))
    weights = (P(None, "fsdp"), P(None, None, "fsdp"), P("fsdp", None), P(None, "fsdp"), P("fsdp", None), P())
    in_specs = (rows2, rows2, rows1, rows2, rows1) + weights * 3
    out_specs = (P(), P(), P()) + weights * 3
    return jax.shard_map(body, mesh=mesh, in_specs=in_specs, out_specs=out_specs, check_vma=False)
```

```python
import functools

import jax
import jax.numpy as jnp
import numpy as np
from jax import lax
from jax.experimental import pallas as pl
from jax.experimental.pallas import tpu as pltpu
from jax.sharding import PartitionSpec as P

LOOKBACK = 3600
OUTLOOK = 720
HID = 512
SERIES = 1024
STEP = 10
LP = 450
BACK = 150
FORE = 30
RATIO = 24
beta_first = 0.9
beta_second = 0.999
learn_rate = 0.01
weight_decay = 0.01
adam_epsilon = 1e-08
clip_level = 0.01

C_IN, C_M0, C_M1, C_OUT, C_ALL = 0, 512, 1024, 1536, 1792
R_M2, R_M3, R_OUT, R_ALL = 0, 512, 1024, 1792
T_PAD = 3840
F_ALL = T_PAD + R_ALL
LATEST = 2700
T_LIVE = 3712
T_WHOLE = 3584
O_PAD = 768
TILE = 256
CINV_AT = 180
FORE_ROWS = slice(144, 184)

F32 = jnp.float32
BF16 = jnp.bfloat16
NN = (((1,), (0,)), ((), ()))
NT = (((1,), (1,)), ((), ()))
TN = (((0,), (0,)), ((), ()))


def mm(a, b, dims=NN):
    return lax.dot_general(a, b, dims, preferred_element_type=F32)


def iota(shape, axis):
    return lax.broadcasted_iota(jnp.int32, shape, axis)


def split3(v):
    hi = v.astype(BF16)
    rest = v - hi.astype(F32)
    mid = rest.astype(BF16)
    return hi, mid, (rest - mid.astype(F32)).astype(BF16)


def mm_exact(v, sel, dims=NN):
    hi, mid, low = split3(v)
    return mm(hi, sel, dims) + mm(mid, sel, dims) + mm(low, sel, dims)


def mm_exact2(sel, v, dims=NN):
    hi, mid, low = split3(v)
    return mm(sel, hi, dims) + mm(sel, mid, dims) + mm(sel, low, dims)


def activate(h):
    u = 1.0 + jnp.tanh(h)
    return h * u, u


def slope_once(h, u, value):
    return u * ((0.5 + h) - 0.5 * value)


def slope_twice(h, u, value):
    return u * ((1.0 + h) + (h - value))


def cost(micros):
    return pl.CostEstimate(
        flops=int(micros * 1.15e9), bytes_accessed=int(micros * 3e6), transcendentals=0
    )


def mask_rows(value, lo, begin):
    if lo >= LATEST:
        return value
    seen = iota(value.shape, 0) >= begin - lo
    return jnp.where(seen, value, jnp.zeros_like(value))


def vmem(limit=60):
    return pltpu.CompilerParams(vmem_limit_bytes=limit * 1024 * 1024)


def bits_of(size):
    return [1 << b for b in range(size.bit_length() - 1)]


def swap(x, dp, fsdp, bit_dp, bit_fsdp):
    pairs = []
    for d in range(dp):
        for f in range(fsdp):
            pairs.append((d * fsdp + f, (d ^ bit_dp) * fsdp + (f ^ bit_fsdp)))
    return lax.ppermute(x, ("dp", "fsdp"), pairs)


def gather_rows(x, dp, fsdp, swap_fn, join):
    far = bits_of(fsdp)
    for bit in reversed(far[1:]):
        x = join(x, swap_fn(x, 0, bit))
    half = x.shape[0] // 2
    a, b = x[:half], x[half:]
    for first, second in zip(reversed(bits_of(dp)), bits_of(dp)):
        a2 = swap_fn(a, first, 0)
        b2 = swap_fn(b, second, 0)
        a, b = join(a, a2), join(b, b2)
    x = join(a, b)
    return join(x, swap_fn(x, 0, far[0]))


def row_order(dp, fsdp):
    share = HID // fsdp
    part = share // dp
    start = np.arange(part)

    def shifted(x, bit_dp, bit_fsdp):
        return x ^ (bit_fsdp * share + bit_dp * part)

    return gather_rows(
        start, dp, fsdp, shifted, lambda p, q: np.concatenate([p, q])
    )


def pack_kernel(d_ref, cin, mid, cout, fin, fout, wx, w1):
    share = cout.shape[0]
    part = wx.shape[0]
    rows = max(part, 16)
    sel = (iota((rows, share), 1) == d_ref[0] * part + iota((rows, share), 0)).astype(BF16)
    wx[...] = jnp.zeros_like(wx)
    w1[:, T_WHOLE:T_PAD] = jnp.zeros((share, T_PAD - T_WHOLE), BF16)
    w1[:, 0:LOOKBACK] = (fin[...] * 0.5).astype(BF16)

    def put(at, value, scale=0.5):
        picked = mm(sel, value.astype(BF16)) * scale
        wx[:, at : at + value.shape[1]] = picked[:part].astype(BF16)

    put(C_IN, cin[...])
    put(C_M0, mid[0])
    put(C_M1, mid[1])
    put(C_OUT, cout[...], 1.0)
    put(C_ALL + R_M2, mid[2])
    put(C_ALL + R_M3, mid[3])
    put(C_ALL + R_OUT, fout[...], 1.0)


def stats_kernel(count, *refs):
    pooled, table = refs[-2:]
    lens, series = refs[count : count + 2]
    hists = refs[:count]
    wide = hists[0].shape[1]

    @pl.when(pl.program_id(0) == 0)
    def _():
        table[...] = jnp.zeros_like(table)

    chunk = 32
    at = LP // chunk * chunk
    rest = LP - at
    pooled[at:HID, :] = jnp.zeros((HID - at, pooled.shape[1]), F32)
    for q, hist in enumerate(hists):
        cols = slice(q * wide, (q + 1) * wide)
        ahead = iota((chunk, wide), 0) * 8 + (lens[:, cols] - LOOKBACK)
        sums = jnp.zeros((8, wide), F32)
        squares = jnp.zeros((8, wide), F32)

        def load(g, s, count):
            h = hist[pl.ds(g * 8 + s, count, stride=8), :]
            if g * 8 >= LATEST:
                return h
            return jnp.where(ahead[0:count] >= -(g * 8 + s), h, 0.0)

        for g in range(0, at, chunk):
            total = load(g, 0, chunk)
            sq = total * total
            for s in range(1, 8):
                h = load(g, s, chunk)
                total += h
                sq += h * h
            for v in range(0, chunk, 8):
                sums += total[v : v + 8]
                squares += sq[v : v + 8]
            pooled[g : g + chunk, cols] = total * 0.125
        total = load(at, 0, rest)
        sq = total * total
        for s in range(1, 8):
            h = load(at, s, rest)
            total += h
            sq += h * h
        pooled[at:LP, cols] = total * 0.125
        sum_row = jnp.sum(sums, 0, keepdims=True) + jnp.sum(total, 0, keepdims=True)
        square_row = jnp.sum(squares, 0, keepdims=True) + jnp.sum(sq, 0, keepdims=True)
        row = iota((16, wide), 0)
        kind = row % 3
        v = jnp.where(
            kind == 0,
            sum_row,
            jnp.where(kind == 1, square_row, lens[:, cols].astype(F32)),
        )
        hi, mid, low = split3(v)
        piece = jnp.where(
            row < 3,
            hi.astype(F32),
            jnp.where(row < 6, mid.astype(F32), jnp.where(row < 9, low.astype(F32), 0.0)),
        ).astype(BF16)
        hot = (iota((SERIES, wide), 0) == series[:, cols]).astype(BF16)
        t = mm(piece, hot, NT)
        table[0:3, :] += t[0:3] + t[3:6] + t[6:9]


def coarse_kernel(p_in, lens, series, table, x_top, x_low, offs, abscol,
                  pooled_out, th_out, look_out, wc, offs_p, looker):
    cols = p_in.shape[1]

    @pl.when(pl.program_id(0) == 0)
    def _():
        perm = perm_of(abscol)
        half = HID // 2
        wc[0:half, :] = x_top[...]
        wc[half:HID, :] = x_low[...]
        for at in (C_M0, C_M1):
            wc[:, at : at + HID] = mm(wc[:, at : at + HID], perm, NT).astype(BF16)
        offs_p[...] = mm_exact2(perm, offs[0:HID, :])
        count = jnp.maximum(table[2:3, :], 1.0)
        centre = table[0:1, :] / count
        spread = jnp.sqrt(table[1:2, :] / count + 1e-05)
        inverse = 1.0 / spread
        shifted = centre / spread
        row = iota((16, SERIES), 0)
        v = jnp.where(row < 3, inverse, shifted)
        hi, mid, low = split3(v)
        kind = row % 3
        looker[...] = jnp.where(
            row < 6,
            jnp.where(
                kind == 0,
                hi.astype(F32),
                jnp.where(kind == 1, mid.astype(F32), low.astype(F32)),
            ),
            0.0,
        ).astype(BF16)

    hot = (iota((SERIES, cols), 0) == series[...]).astype(BF16)
    got = mm(looker[...], hot)
    inv = got[0:1] + got[1:2] + got[2:3]
    cinv = got[3:4] + got[4:5] + got[5:6]
    look_out[...] = jnp.where(iota((8, cols), 0) == 0, inv, cinv)
    group = iota((HID, cols), 0)
    begin = LOOKBACK - lens[...]
    share = jnp.clip(group * 8 + 8 - begin, 0, 8).astype(F32) * 0.125
    pooled = jnp.where(group < LP, p_in[...] * inv - cinv * share, 0.0).astype(BF16)
    pooled_out[...] = pooled
    v = activate(mm(wc[:, C_IN : C_IN + HID], pooled) + offs_p[:, 0:1])[0]
    v = activate(mm(wc[:, C_M0:C_M1], v.astype(BF16)) + offs_p[:, 1:2])[0]
    v = activate(mm(wc[:, C_M1:C_OUT], v.astype(BF16)) + offs_p[:, 2:3])[0]
    theta = mm(wc[:, C_OUT:C_ALL], v.astype(BF16), TN) + offs[0:256, 3:4]
    theta = theta * (1.0 / 48.0)
    hi = theta.astype(BF16).astype(F32)
    at = iota((256, cols), 0)
    c_hi, c_mid, c_low = split3(cinv)
    with_shift = jnp.where(
        at == CINV_AT,
        c_hi.astype(F32),
        jnp.where(
            at == CINV_AT + 1,
            c_mid.astype(F32),
            jnp.where(at == CINV_AT + 2, c_low.astype(F32), hi),
        ),
    )
    th_out[...] = with_shift.astype(BF16)


def fold_lanes(x):
    total = x[:, 0:128]
    for at in range(128, x.shape[1], 128):
        total = total + x[:, at : at + 128]
    return total


def hidden_rows(acc, perm):
    lane = iota((HID, 128), 1)
    v = jnp.zeros((HID, 128), F32)
    for k in range(3):
        v = jnp.where(lane == k, jnp.sum(acc[k], 1, keepdims=True), v)
    return mm_exact(v, perm, TN)[0:8]


def last_row(acc):
    v = jnp.broadcast_to(jnp.sum(acc, 1, keepdims=True), acc.shape)
    return jnp.transpose(v, (1, 0))[0:8]


def perm_of(abscol):
    return (iota((HID, HID), 1) == abscol[...]).astype(BF16)


def fine_kernel(hist, later, flags, look, lens, th, w1, x_top, x_low, btab_t, ftab, ftab_t, offs, abscol,
                res, dz1, dz1_p, fore, small, keep, send,
                acc, acc4, acc_loss, dz4, total, wr, offs_p, perm):
    cols = hist.shape[1]
    step = pl.program_id(0)

    @pl.when(step == 0)
    def _():
        acc[...] = jnp.zeros_like(acc)
        acc4[...] = jnp.zeros_like(acc4)
        acc_loss[...] = jnp.zeros_like(acc_loss)
        perm[...] = perm_of(abscol)
        wr[0 : HID // 2, :] = x_top[...]
        wr[HID // 2 : HID, :] = x_low[...]
        wr[:, R_M3:R_OUT] = mm(wr[:, R_M3:R_OUT], perm[...], NT).astype(BF16)
        offs_p[...] = mm_exact2(perm[...], offs[0:HID, :])
        total[...] = jnp.zeros_like(total)
        dz4[OUTLOOK:O_PAD, :] = jnp.zeros((O_PAD - OUTLOOK, cols), BF16)

    inv = look[0:1, :]
    cinv = look[1:2, :]
    begin = LOOKBACK - lens[...]
    th_hi = th[...]
    res[LOOKBACK:T_PAD, :] = jnp.zeros((T_PAD - LOOKBACK, cols), BF16)
    h1 = offs[0:HID, 0:1]
    for at in range(0, T_LIVE, 1024):
        end = min(at + 1024, T_LIVE)
        live = min(end, LOOKBACK)
        shift = mm(btab_t[at:live, :], th_hi)
        for lo in range(at, live, 512):
            width = min(512, live - lo)
            r = hist[lo : lo + width, :] * inv - shift[lo - at : lo - at + width]
            res[lo : lo + width, :] = mask_rows(r, lo, begin).astype(BF16)
        h1 = h1 + mm(w1[:, at:end], res[at:end, :])
    v1, u1 = activate(h1)
    b1 = v1.astype(BF16)
    h2 = mm(wr[:, R_M2:R_M3], b1) + offs_p[:, 1:2]
    v2, u2 = activate(h2)
    b2 = v2.astype(BF16)
    h3 = mm(wr[:, R_M3:R_OUT], b2) + offs_p[:, 2:3]
    v3, u3 = activate(h3)
    b3 = v3.astype(BF16)
    est = mm(wr[:, R_OUT:R_ALL], b3, TN) + mm(ftab_t[...], th_hi) + offs[:, 3:4]
    counted = flags[...].astype(F32)
    err = (est[0:OUTLOOK] - (later[...] * inv - cinv)) * counted
    acc_loss[0:1, :] += jnp.sum(err * err, 0, keepdims=True)
    acc_loss[1:2, :] += jnp.sum(counted, 0, keepdims=True)
    d4 = (2.0 * err).astype(BF16)
    acc4[0:OUTLOOK, :] += fold_lanes(d4.astype(F32))
    dz4[0:OUTLOOK, :] = d4
    d4 = dz4[...]
    fore[...] = jnp.zeros_like(fore)
    fore[FORE_ROWS, :] = mm(ftab[FORE_ROWS, :], d4) * (1.0 / 48.0)

    def back(upstream, slope, row):
        d = (upstream * slope).astype(BF16)
        acc[row] += fold_lanes(d.astype(F32))
        return d

    d3 = back(mm(wr[:, R_OUT:R_ALL], d4), slope_once(h3, u3, v3), 2)
    total[:, R_OUT:R_ALL] += mm(b3, d4, NT)
    d2 = back(mm(wr[:, R_M3:R_OUT], d3, TN), slope_twice(h2, u2, v2), 1)
    total[:, R_M3:R_OUT] += mm(d3, b2, NT)
    d1 = back(mm(wr[:, R_M2:R_M3], d2, TN), slope_twice(h1, u1, v1), 0)
    dz1[...] = d1
    dz1_p[...] = mm(perm[...], d1).astype(BF16)
    total[:, R_M2:R_M3] += mm(d2, b1, NT)

    @pl.when(step == pl.num_programs(0) - 1)
    def _():
        small[...] = last_row(acc4[...])
        loss = jnp.sum(acc_loss[0:1, :], 1, keepdims=True)
        tally = jnp.sum(acc_loss[1:2, :], 1, keepdims=True)
        row = iota((8, O_PAD), 0)
        small[...] = jnp.where(
            row == 3,
            small[...],
            jnp.where(row == 4, loss, jnp.where(row == 5, tally, 0.0)),
        )
        half = HID // 2
        for cols_k in (slice(R_M2, R_M3), slice(R_M3, R_OUT), slice(R_OUT, R_ALL)):
            g = total[:, cols_k]
            if cols_k.start == R_M3:
                g = natural_columns(g, perm[...])
            keep[:, cols_k] = g[0:half]
            send[:, cols_k] = g[half:HID].astype(BF16)
        small[0:3, 0:HID] = hidden_rows(acc, perm[...])[0:3]
        small[0:1, 0:HID] = last_row(acc[0])[0:1]


def natural_columns(g, perm):
    half = HID // 2
    hi = g.astype(BF16)
    low = (g - hi.astype(F32)).astype(BF16)
    out = mm(hi, perm)
    return jnp.concatenate([out[0:half] + mm(low[0:half], perm), out[half:HID]], 0)


def fine_in_grad_kernel(dz1, res, rest, out):
    step = pl.program_id(0)
    tile = out.shape[1]
    whole = T_PAD // tile

    def product(width):
        for lo in range(0, width, 512):
            end = min(lo + 512, width)
            g = mm(res[lo:end, :], dz1[...], NT)
            out[:, lo:end] = jnp.transpose(g, (1, 0)).astype(out.dtype)

    @pl.when(step < whole)
    def _():
        product(tile)

    for k in range(whole, F_ALL // tile):

        @pl.when(step == k)
        def _():
            edge = max(T_PAD - k * tile, 0)
            if edge:
                product(edge)
            begin = k * tile + edge - T_PAD
            out[:, edge:tile] = rest[:, begin : begin + tile - edge]


def back_kernel(first, final, *refs):
    dz1f, fore, lens, pooled, w1, btab, wc, abscol, offs_p = refs[:9]
    outs = refs[9 if first else 10 : -4]
    small = outs[-1]
    acc, acc4, total, back_grad = refs[-4:]
    cols = dz1f.shape[1]
    step = pl.program_id(0)

    @pl.when(step == 0)
    def _():
        acc[...] = jnp.zeros_like(acc)
        acc4[...] = jnp.zeros_like(acc4)
        total[...] = jnp.zeros_like(total) if first else refs[9][...]

    begin = LOOKBACK - lens[...]
    d1f = dz1f[...]
    back_grad[...] = jnp.zeros_like(back_grad)
    for at in range(0, T_LIVE, T_LIVE // 2):
        wide = mm(w1[:, at : at + T_LIVE // 2], d1f, TN)
        for lo in range(at, at + T_LIVE // 2, 512):
            width = min(512, at + T_LIVE // 2 - lo)
            d = mask_rows(wide[lo - at : lo - at + width], lo, begin).astype(BF16)
            first_knot = max(lo // RATIO - 1, 0) // 8 * 8
            last_knot = min(-(-(lo + width + RATIO) // RATIO), BACK)
            last_knot = -(-last_knot // 8) * 8
            knots = slice(first_knot, last_knot)
            back_grad[knots, :] += mm(btab[knots, lo : lo + width], d)
    row = iota((256, cols), 0)
    d4 = (jnp.where(row < BACK, back_grad[...] * (-2.0 / 48.0), 0.0) + fore[...]).astype(BF16)
    acc4[...] += fold_lanes(d4.astype(F32))

    def ahead(w, entering, k):
        h = mm(w, entering) + offs_p[:, k : k + 1]
        value, u = activate(h)
        return h, u, value, value.astype(BF16)

    p = pooled[...]
    h1, u1, v1, b1 = ahead(wc[:, C_IN : C_IN + HID], p, 0)
    h2, u2, v2, b2 = ahead(wc[:, C_M0:C_M1], b1, 1)
    h3, u3, v3, b3 = ahead(wc[:, C_M1:C_OUT], b2, 2)

    def back(upstream, slope, row):
        d = (upstream * slope).astype(BF16)
        acc[row] += fold_lanes(d.astype(F32))
        return d

    d3 = back(mm(wc[:, C_OUT:C_ALL], d4), slope_once(h3, u3, v3), 2)
    total[:, C_OUT:C_ALL] += mm(b3, d4, NT)
    d2 = back(mm(wc[:, C_M1:C_OUT], d3, TN), slope_twice(h2, u2, v2), 1)
    total[:, C_M1:C_OUT] += mm(d3, b2, NT)
    d1 = back(mm(wc[:, C_M0:C_M1], d2, TN), slope_twice(h1, u1, v1), 0)
    total[:, C_M0:C_M1] += mm(d2, b1, NT)
    total[:, C_IN:C_M0] += mm(d1, p, NT)

    @pl.when(step == pl.num_programs(0) - 1)
    def _():
        perm = perm_of(abscol)
        small[...] = jnp.zeros_like(small)
        small[0:3, :] = hidden_rows(acc, perm)[0:3]
        small[3:4, 0:256] = last_row(acc4[...])[0:1]
        if not final:
            outs[0][...] = total[...]
            return
        half = HID // 2
        for a, b in zip((C_IN, C_M0, C_M1, C_OUT), (C_M0, C_M1, C_OUT, C_ALL)):
            g = total[:, a:b]
            if a in (C_M0, C_M1):
                g = natural_columns(g, perm)
            outs[0][:, a:b] = g[0:half]
            outs[1][:, a:b] = g[half:HID].astype(BF16)


def adam_math(weight, mean_old, square_old, grad):
    mean_new = beta_first * mean_old + (1.0 - beta_first) * grad
    square_new = beta_second * square_old + (1.0 - beta_second) * grad * grad
    fix = (1.0 - beta_second**STEP) ** 0.5
    gain = learn_rate * fix / (1.0 - beta_first**STEP)
    weight_new = weight * (1.0 - learn_rate * weight_decay) - gain * mean_new / (
        jnp.sqrt(square_new) + adam_epsilon * fix
    )
    return weight_new, mean_new, square_new


def adam_kernel(dp, small, relrow, *refs):
    pieces, refs = refs[: 2 * dp], refs[2 * dp :]
    ins, biases, outs, bias_outs = refs[:15], refs[15:18], refs[18:33], refs[33:36]
    loss, tally, norm, grads, bias_grad = refs[36:]
    part = pieces[0].shape[0]
    share = dp * part
    order = [0, *range(2, dp + 1), 1, *range(dp + 1, 2 * dp)]
    for k, index in enumerate(order):
        piece = pieces[index]
        at, row = (0, k) if k < dp else (F_ALL, k - dp)
        grads[row * part : (row + 1) * part, at : at + piece.shape[1]] = piece[...].astype(F32)
    place = (iota((share, share), 1) == relrow[...]).astype(BF16)

    count = small[5:6, 0:1]
    sums = small[0:4, :]
    bias_square = jnp.sum(jnp.sum(sums * sums, 0, keepdims=True), 1, keepdims=True)
    grad_norm = jnp.sqrt(small[6:7, 0:1] + bias_square) / count
    s = clip_level / jnp.maximum(grad_norm, clip_level) / count
    loss[...] = small[4:5, 0:1]
    tally[...] = count
    norm[...] = grad_norm
    for k in range(3):
        bias_grad[:, k * HID : (k + 1) * HID] = small[k : k + 1, O_PAD : O_PAD + HID]
        bias_grad[:, (k + 3) * HID : (k + 4) * HID] = small[k : k + 1, 0:HID]
    last = 6 * HID + BACK + FORE
    bias_grad[:, 6 * HID : last] = small[3:4, O_PAD : O_PAD + BACK + FORE]
    bias_grad[:, last : last + OUTLOOK] = small[3:4, 0:OUTLOOK]
    for out, value in zip(
        bias_outs, adam_math(*(x[...] for x in biases), bias_grad[...] * s)
    ):
        out[...] = value

    def step(i, at, width, index):
        g = grads[:, at : at + width]
        hi = g.astype(BF16)
        low = (g - hi.astype(F32)).astype(BF16)
        grad = (mm(place, hi, TN) + mm(place, low, TN)) * s
        old = [ins[i + 5 * k][index] for k in range(3)]
        for k, value in enumerate(adam_math(*old, grad)):
            outs[i + 5 * k][index] = value

    every = slice(None)
    step(0, F_ALL + C_IN, LP, (every, every))
    step(1, F_ALL + C_M0, HID, 0)
    step(1, F_ALL + C_M1, HID, 1)
    step(1, T_PAD + R_M2, HID, 2)
    step(1, T_PAD + R_M3, HID, 3)
    step(2, F_ALL + C_OUT, BACK + FORE, (every, every))
    step(4, T_PAD + R_OUT, OUTLOOK, (every, every))
    for lo in range(0, LOOKBACK, 512):
        width = min(512, LOOKBACK - lo)
        step(3, lo, width, (every, slice(lo, lo + width)))


def interp_table(count, length, first_row, rows, cols):
    spots = np.clip((np.arange(length) + 0.5) * (count / length) - 0.5, 0.0, count - 1.0)
    table = np.maximum(0.0, 1.0 - np.abs(spots[None, :] - np.arange(count)[:, None]))
    out = np.zeros((rows, cols), np.float32)
    out[first_row : first_row + count, :length] = np.round(table * 48.0)
    return out


def assemble_kernel(plan, count, *refs):
    ins, outs = refs[:count], refs[count:]
    for which, begin, at, size, out in plan:
        outs[out][at : at + size, :] = ins[which][begin : begin + size, :]


def assemble(*outs):
    if any(n % 16 or b % 16 for out in outs for _, b, n in out):
        return [
            jnp.concatenate([x[b : b + n] for x, b, n in out], 0) for out in outs
        ]
    ins, plan, shapes = [], [], []
    for k, out in enumerate(outs):
        at = 0
        for x, begin, size in out:
            which = next((i for i, y in enumerate(ins) if y is x), len(ins))
            if which == len(ins):
                ins.append(x)
            plan.append((which, begin, at, size, k))
            at += size
        shapes.append(jax.ShapeDtypeStruct((at, out[0][0].shape[1]), out[0][0].dtype))
    def blocks(arrays):
        return [pl.BlockSpec(x.shape, lambda i: (0, 0)) for x in arrays]

    return pl.pallas_call(
        functools.partial(assemble_kernel, tuple(plan), len(ins)),
        grid=(1,),
        out_shape=tuple(shapes),
        in_specs=blocks(ins),
        out_specs=tuple(blocks(shapes)),
        compiler_params=vmem(63),
        cost_estimate=cost(1),
        name="assemble",
    )(*ins)


def add_rows(pairs, plan):
    sums = [keep + got.astype(F32) for keep, got in pairs]
    return [
        sums[which][begin : begin + size].astype(kind) for which, begin, size, kind in plan
    ]


def spec(shape, index):
    return pl.BlockSpec(shape, index)


def fixed(shape):
    return pl.BlockSpec(shape, lambda i: (0,) * len(shape), pipeline_mode=pl.Buffered(1))


def body(
    history, later_observed, lengths, counted_flags, series,
    coarse_in, middle, rough_final_matrix, fine_in, sharp_final_matrix, offset_vectors,
    coarse_in_mean, middle_mean, rough_final_first, fine_in_mean, sharp_final_first, biases_mean,
    coarse_in_square, middle_square, rough_final_second, fine_in_square, sharp_final_second,
    biases_square,
):
    dp, fsdp = lax.axis_size("dp"), lax.axis_size("fsdp")
    d_here, f_here = lax.axis_index("dp"), lax.axis_index("fsdp")
    rows = history.shape[0]
    share = HID // fsdp
    part = share // dp

    def exchange(x, bit_dp, bit_fsdp):
        return swap(x, dp, fsdp, bit_dp, bit_fsdp)

    def join(p, q):
        return jnp.concatenate([p, q], 0)

    here = f_here * share + d_here * part
    order = row_order(dp, fsdp)
    abscol = (jnp.asarray(order, jnp.int32) ^ here).reshape(HID, 1)
    together = lax.optimization_barrier

    def by_hidden(cin, mid, cout, fin, fout):
        return (cin.T, mid.transpose(0, 2, 1), cout, fin.T, fout)

    def one_step(arrays):
        return [
            pl.BlockSpec(x.shape, lambda i, n=len(x.shape): (0,) * n) for x in arrays
        ]

    shard_now = by_hidden(
        coarse_in, middle, rough_final_matrix, fine_in, sharp_final_matrix
    )

    x_part, w1_part = pl.pallas_call(
        pack_kernel,
        out_shape=(
            jax.ShapeDtypeStruct((part, C_ALL + R_ALL), BF16),
            jax.ShapeDtypeStruct((share, T_PAD), BF16),
        ),
        grid=(1,),
        in_specs=[pl.BlockSpec(memory_space=pltpu.SMEM)] + one_step(shard_now),
        out_specs=(
            pl.BlockSpec((part, C_ALL + R_ALL), lambda i: (0, 0)),
            pl.BlockSpec((share, T_PAD), lambda i: (0, 0)),
        ),
        compiler_params=vmem(63),
        cost_estimate=cost(1),
        name="pack_weights",
    )(d_here.reshape(1), *shard_now)

    hist = history.T
    lens = lengths.reshape(1, rows)
    series_row = series.reshape(1, rows)
    side = rows // 2
    calls = (1, 1, 2)

    def stats(which, lens_row, pool):
        count = 2
        unit = rows // (128 * count * sum(calls))
        steps = calls[which] * unit
        at = sum(calls[:which]) * unit

        def hist_spec(q):
            return spec((LOOKBACK, 128), lambda i: (0, (at + i) * count + q))

        def row_spec():
            return spec((1, 128 * count), lambda i: (0, at + i))

        return pl.pallas_call(
            functools.partial(stats_kernel, count),
            grid=(steps,),
            out_shape=(
                jax.ShapeDtypeStruct((HID, rows), F32),
                jax.ShapeDtypeStruct((8, SERIES), F32),
            ),
            in_specs=[hist_spec(q) for q in range(count)]
            + [row_spec(), row_spec()]
            + [pl.BlockSpec(memory_space=pl.ANY) for _ in pool],
            out_specs=(
                spec((HID, 128 * count), lambda i: (0, at + i)),
                pl.BlockSpec((8, SERIES), lambda i: (0, 0)),
            ),
            compiler_params=vmem(63),
            cost_estimate=cost(6),
            input_output_aliases={count + 2: 0} if pool else {},
            name="window_stats",
        )(*[hist] * count, lens_row, series_row, *pool)

    up, down = bits_of(dp), bits_of(dp)[::-1]
    near, *far = bits_of(fsdp)
    moves = [(0, bit) for bit in reversed(far)] + list(zip(down, up)) + [(0, near)]

    def cut_rows(x):
        half = x.shape[0] // 2
        return x[:half], x[half:]

    def add_over(table, steps):
        for bit_dp, bit_fsdp in steps:
            table = table + exchange(table, bit_dp, bit_fsdp)
        return table

    x = [x_part]
    pools, tables, table = [], [], None
    sums = [(0, bit) for bit in bits_of(fsdp)] + [(bit, 0) for bit in up]
    sums = [sums[:3], sums[3:]]
    for k, move in enumerate(moves[:-1]):
        along_dp = k >= len(far)
        if along_dp and len(x) == 1:
            x = list(cut_rows(x[0]))
        got = [exchange(h, b, 0) for h, b in zip(x, move)] if along_dp else [exchange(x[0], *move)]
        if k < len(calls):
            lens_row, *x = together((lens, *x))
            pool, this = stats(k, lens_row, pools[-1:])
            pools.append(pool)
            *got, this = together((*got, this))
            tables.append(this)
        elif sums:
            if table is None:
                table = sum(tables[1:], tables[0])
            table = add_over(table, sums.pop(0))
            *got, table = together((*got, table))
        if k == len(far) - 1:
            w1_part, *got = together((w1_part, *got))
            w1 = lax.all_gather(w1_part, "fsdp", axis=0, tiled=True)
        if k < len(moves) - 2:
            x = [join(h, g) for h, g in zip(x, got)]
    x_top = assemble(
        [(h, 0, h.shape[0]) for pair in zip(x, got) for h in pair]
    )[0]
    x_low = exchange(x_top, *moves[-1])
    for steps in sums:
        table = add_over(table, steps)

    hidden = offset_vectors[: 6 * HID].reshape(6, HID)
    rough_bias = offset_vectors[6 * HID : 6 * HID + BACK + FORE]
    sharp_bias = offset_vectors[6 * HID + BACK + FORE :]

    def bias_cols(three, last, width):
        out = jnp.pad(three, ((0, 0), (0, width - HID)))
        out = join(out, jnp.pad(last, (0, width - last.shape[0]))[None])
        return jnp.pad(out, ((0, 4), (0, 0))).T

    coarse_offs = bias_cols(0.5 * hidden[:3], rough_bias, HID)
    fine_offs = bias_cols(0.5 * hidden[3:], sharp_bias, O_PAD)

    r = 512
    tiles = rows // r

    def col_spec(height, begin=0, last=tiles - 1):
        return spec((height, r), lambda i: (0, jnp.minimum(begin + i, last)))

    half_block = pl.BlockSpec(
        (HID // 2, C_ALL), lambda i: (0, 0), pipeline_mode=pl.Buffered(1)
    )
    pooled, th, look, wc, offs_p = pl.pallas_call(
        coarse_kernel,
        grid=(tiles,),
        out_shape=(
            jax.ShapeDtypeStruct((HID, rows), BF16),
            jax.ShapeDtypeStruct((256, rows), BF16),
            jax.ShapeDtypeStruct((8, rows), F32),
            jax.ShapeDtypeStruct((HID, C_ALL), BF16),
            jax.ShapeDtypeStruct((HID, 8), F32),
        ),
        in_specs=[
            col_spec(HID),
            col_spec(1),
            col_spec(1),
            fixed((8, SERIES)),
            half_block,
            half_block,
            fixed((HID, 8)),
            fixed((HID, 1)),
        ],
        out_specs=(
            col_spec(HID),
            col_spec(256),
            col_spec(8),
            pl.BlockSpec((HID, C_ALL), lambda i: (0, 0)),
            pl.BlockSpec((HID, 8), lambda i: (0, 0)),
        ),
        scratch_shapes=[pltpu.VMEM((16, SERIES), BF16)],
        compiler_params=vmem(63),
        cost_estimate=cost(10),
        name="coarse_forward",
    )(
        pools[-1], lens, series_row, table, x_top, x_low, coarse_offs, abscol,
    )
    back_table = interp_table(BACK, LOOKBACK, 0, 256, T_PAD)
    btab = jnp.asarray(back_table, BF16)
    back_table[CINV_AT : CINV_AT + 3, :LOOKBACK] = 1.0
    btab_t = jnp.asarray(back_table.T, BF16)
    fore_table = interp_table(FORE, OUTLOOK, BACK, 256, O_PAD)
    ftab = jnp.asarray(fore_table, BF16)
    ftab_t = jnp.asarray(fore_table.T, BF16)

    tall = jax.ShapeDtypeStruct((HID, rows), BF16)
    r_shapes = (
        jax.ShapeDtypeStruct((HID // 2, R_ALL), F32),
        jax.ShapeDtypeStruct((HID // 2, R_ALL), BF16),
    )
    rest_block = pl.BlockSpec(
        (HID // 2, R_ALL), lambda i: (0, 1), pipeline_mode=pl.Buffered(1)
    )
    res, dz1, dz1_p, fore, f_small, r_keep, r_send = pl.pallas_call(
        fine_kernel,
        grid=(tiles,),
        out_shape=(
            jax.ShapeDtypeStruct((T_PAD, rows), BF16),
            tall,
            tall,
            jax.ShapeDtypeStruct((256, rows), F32),
            jax.ShapeDtypeStruct((8, O_PAD), F32),
            *r_shapes,
        ),
        in_specs=[
            col_spec(LOOKBACK),
            col_spec(OUTLOOK),
            col_spec(OUTLOOK),
            col_spec(8),
            col_spec(1),
            col_spec(256),
            fixed((HID, T_PAD)),
            rest_block,
            rest_block,
            fixed((T_PAD, 256)),
            fixed((256, O_PAD)),
            fixed((O_PAD, 256)),
            fixed((O_PAD, 8)),
            fixed((HID, 1)),
        ],
        out_specs=(
            col_spec(T_PAD),
            col_spec(HID),
            col_spec(HID),
            col_spec(256),
            pl.BlockSpec((8, O_PAD), lambda i: (0, 0)),
            *[pl.BlockSpec((HID // 2, R_ALL), lambda i: (0, 0))] * 2,
        ),
        scratch_shapes=[
            pltpu.VMEM((3, HID, 128), F32),
            pltpu.VMEM((O_PAD, 128), F32),
            pltpu.VMEM((8, r), F32),
            pltpu.VMEM((O_PAD, r), BF16),
            pltpu.VMEM((HID, R_ALL), F32),
            pltpu.VMEM((HID, R_ALL), BF16),
            pltpu.VMEM((HID, 8), F32),
            pltpu.VMEM((HID, HID), BF16),
        ],
        compiler_params=vmem(63),
        cost_estimate=cost(40),
        name="fine_block",
    )(
        hist, later_observed.T, counted_flags.T, look, lens, th,
        w1, x_top, x_low, btab_t, ftab, ftab_t, fine_offs, abscol,
    )

    wide = F_ALL // 4
    res_last = -(-T_PAD // wide) - 1

    def fine_in_grad(side, rest, kind):
        return pl.pallas_call(
            fine_in_grad_kernel,
            grid=(F_ALL // wide,),
            out_shape=jax.ShapeDtypeStruct((HID // 2, F_ALL), kind),
            in_specs=[
                pl.BlockSpec((HID // 2, rows), lambda i: (side, 0), pipeline_mode=pl.Buffered(1)),
                spec((wide, rows), lambda i: (jnp.minimum(i, res_last), 0)),
                fixed((HID // 2, R_ALL)),
            ],
            out_specs=spec((HID // 2, wide), lambda i: (0, i)),
            compiler_params=vmem(63),
            cost_estimate=cost(7),
            name="fine_in_grad",
        )(dz1_p, res, rest)

    def backward(at, steps, fore, before):
        first = not before
        final = at + steps == tiles
        half = HID // 2
        shapes = (
            [jax.ShapeDtypeStruct((HID, C_ALL), F32)]
            if not final
            else [jax.ShapeDtypeStruct((half, C_ALL), t) for t in (F32, BF16)]
        ) + [jax.ShapeDtypeStruct((8, HID), F32)]

        def rows_of(height):
            return col_spec(height, at)

        return pl.pallas_call(
            functools.partial(back_kernel, first, final),
            grid=(steps,),
            out_shape=tuple(shapes),
            in_specs=[
                rows_of(HID),
                rows_of(256),
                rows_of(1),
                rows_of(HID),
                fixed((HID, T_PAD)),
                fixed((256, T_PAD)),
                fixed((HID, C_ALL)),
                fixed((HID, 1)),
                fixed((HID, 8)),
            ]
            + [fixed(x.shape) for x in before],
            out_specs=tuple(pl.BlockSpec(s.shape, lambda i: (0, 0)) for s in shapes),
            scratch_shapes=[
                pltpu.VMEM((3, HID, 128), F32),
                pltpu.VMEM((256, 128), F32),
                pltpu.VMEM((HID, C_ALL), F32),
                pltpu.VMEM((256, r), F32),
            ],
            compiler_params=vmem(36),
            cost_estimate=cost(17),
            name="coarse_backward",
        )(dz1, fore, lens, pooled, w1, btab, wc, abscol, offs_p, *before)

    legs = [(0, near)] + list(zip(up, down)) + [(0, bit) for bit in far]

    def split(j):
        return 1 <= j <= len(up)

    def sum_and_cut(pairs, j):
        n = pairs[0][0].shape[0]
        if j + 1 == len(legs):
            plan = [(0, 0, n, F32)]
        elif not split(j + 1):
            plan = [(0, 0, n, F32), (1, 0, n, BF16)] if len(pairs) == 2 else [
                (0, 0, n // 2, F32), (0, n // 2, n // 2, BF16)
            ]
        else:
            size = n // 2 if len(pairs) == 2 else n // 4
            plan = []
            for k in range(2):
                which, begin = (k, 0) if len(pairs) == 2 else (0, 2 * k * size)
                plan += [(which, begin, size, F32), (which, begin + size, size, BF16)]
        flat = add_rows(pairs, plan)
        return [tuple(flat[k : k + 2]) for k in range(0, len(flat), 2)]

    def travel(state, j):
        if split(j):
            return [exchange(send, bit, 0) for (_, send), bit in zip(state, legs[j])]
        return [exchange(state[0][1], *legs[j])]

    def kept(state, got):
        return [(pair[0], g) for pair, g in zip(state, got)]

    def beside(got, *others):
        return together((*got, *others))[: len(got)]

    def hold(state, value):
        return together((value, *(x for pair in state for x in pair)))[0]

    f_send = fine_in_grad(1, r_send, BF16)
    got = [exchange(f_send, 0, near)]
    r_keep, f_send = together((r_keep, f_send))
    f_keep = fine_in_grad(0, r_keep, F32)
    state = sum_and_cut([(f_keep, *beside(got, f_keep))], 0)
    quarter = max(tiles // 4, 1)
    smalls, c_part, at = [], (), 0
    for j, count in enumerate((tiles - 2 * quarter, quarter, quarter)):
        got = travel(state, j + 1)
        *c_part, this = backward(at, count, hold(state, fore), tuple(c_part))
        smalls.append(this)
        at += count
        both = together((*got, *c_part))
        got, c_part = both[: len(got)], both[len(got) :]
        state = sum_and_cut(kept(state, got), j + 1)
    f_state, f_leg = state, 4
    c_keep, c_send = c_part
    c_small = sum(smalls[1:], smalls[0])

    c_got = exchange(c_send, 0, near)
    f_got = travel(f_state, f_leg) if f_leg < len(legs) else None
    c_state = sum_and_cut([(c_keep, c_got)], 0)
    for j in range(1, len(legs)):
        got = travel(c_state, j)
        c_state = sum_and_cut(kept(c_state, got), j)
        if j == 1:
            while f_leg < len(legs):
                f_got = f_got or travel(f_state, f_leg)
                f_got = beside(f_got, *c_state[0])
                f_state = sum_and_cut(kept(f_state, f_got), f_leg)
                f_got, f_leg = None, f_leg + 1
            gf_part = f_state[0][0]
            f_wire = gf_part.astype(BF16)
            f_all = [f_wire] + [exchange(f_wire, d, 0) for d in range(1, dp)]
        if j == len(legs) - 2:
            f_all = beside(f_all, *c_state[0])
    gc_part = c_state[0][0]
    c_all = [gc_part] + [exchange(gc_part, d, 0) for d in range(1, dp)]

    rel = np.concatenate([np.arange(part) ^ (d * part) for d in range(dp)])
    relrow = (jnp.asarray(rel, jnp.int32) ^ (d_here * part)).reshape(share, 1)

    squares = jnp.sum(gf_part * gf_part) + jnp.sum(gc_part * gc_part)
    small = jnp.concatenate([f_small, c_small], 1)
    small = jnp.where(
        (iota(small.shape, 0) == 6) & (iota(small.shape, 1) == 0), squares, small
    )
    small = add_over(small, [(bit, 0) for bit in up] + [(0, near)])
    *c_all, small = together((*c_all, small))
    small = add_over(small, [(0, bit) for bit in far])
    pieces = [f_all[0], c_all[0], *f_all[1:], *c_all[1:]]
    shards = (
        *shard_now,
        *by_hidden(
            coarse_in_mean, middle_mean, rough_final_first, fine_in_mean, sharp_final_first
        ),
        *by_hidden(
            coarse_in_square, middle_square, rough_final_second, fine_in_square,
            sharp_final_second,
        ),
    )
    biases = [x.reshape(1, -1) for x in (offset_vectors, biases_mean, biases_square)]
    given = (small, relrow, *pieces, *shards, *biases)
    results = tuple(jax.ShapeDtypeStruct(x.shape, F32) for x in (*shards, *biases)) + (
        jax.ShapeDtypeStruct((1, 1), F32),
    ) * 3
    new = pl.pallas_call(
        functools.partial(adam_kernel, dp),
        out_shape=results,
        grid=(1,),
        in_specs=one_step(given),
        out_specs=tuple(one_step(results)),
        scratch_shapes=[
            pltpu.VMEM((share, F_ALL + C_ALL), F32),
            pltpu.VMEM(biases[0].shape, F32),
        ],
        compiler_params=vmem(63),
        cost_estimate=cost(6),
        name="adam",
    )(*given)
    return (
        *(x.reshape(()) for x in new[18:21]),
        *by_hidden(*new[0:5]), new[15].reshape(-1),
        *by_hidden(*new[5:10]), new[16].reshape(-1),
        *by_hidden(*new[10:15]), new[17].reshape(-1),
    )


def solution(mesh):
    rows2 = P(("dp", "fsdp"), None)
    rows1 = P(("dp", "fsdp"))
    weights = (P(None, "fsdp"), P(None, None, "fsdp"), P("fsdp", None), P(None, "fsdp"), P("fsdp", None), P())
    in_specs = (rows2, rows2, rows1, rows2, rows1) + weights * 3
    out_specs = (P(), P(), P()) + weights * 3
    return jax.shard_map(body, mesh=mesh, in_specs=in_specs, out_specs=out_specs, check_vma=False)
```

```python
import functools

import jax
import jax.numpy as jnp
import numpy as np
from jax import lax
from jax.experimental import pallas as pl
from jax.experimental.pallas import tpu as pltpu
from jax.sharding import PartitionSpec as P

LOOKBACK = 3600
OUTLOOK = 720
HID = 512
SERIES = 1024
STEP = 10
LP = 450
BACK = 150
FORE = 30
RATIO = 24
beta_first = 0.9
beta_second = 0.999
learn_rate = 0.01
weight_decay = 0.01
adam_epsilon = 1e-08
clip_level = 0.01

C_IN, C_M0, C_M1, C_OUT, C_ALL = 0, 512, 1024, 1536, 1792
R_M2, R_M3, R_OUT, R_ALL = 0, 512, 1024, 1792
T_PAD = 3840
F_ALL = T_PAD + R_ALL
LATEST = 2700
T_LIVE = 3712
T_WHOLE = 3584
O_PAD = 768
TILE = 256
CINV_AT = 180
FORE_ROWS = slice(144, 184)

F32 = jnp.float32
BF16 = jnp.bfloat16
NN = (((1,), (0,)), ((), ()))
NT = (((1,), (1,)), ((), ()))
TN = (((0,), (0,)), ((), ()))


def mm(a, b, dims=NN):
    return lax.dot_general(a, b, dims, preferred_element_type=F32)


def iota(shape, axis):
    return lax.broadcasted_iota(jnp.int32, shape, axis)


def split3(v):
    hi = v.astype(BF16)
    rest = v - hi.astype(F32)
    mid = rest.astype(BF16)
    return hi, mid, (rest - mid.astype(F32)).astype(BF16)


def mm_exact(v, sel, dims=NN):
    hi, mid, low = split3(v)
    return mm(hi, sel, dims) + mm(mid, sel, dims) + mm(low, sel, dims)


def mm_exact2(sel, v, dims=NN):
    hi, mid, low = split3(v)
    return mm(sel, hi, dims) + mm(sel, mid, dims) + mm(sel, low, dims)


def activate(h):
    u = 1.0 + jnp.tanh(h)
    return h * u, u


def slope_once(h, u, value):
    return u * ((0.5 + h) - 0.5 * value)


def slope_twice(h, u, value):
    return u * ((1.0 + h) + (h - value))


def cost(micros):
    return pl.CostEstimate(
        flops=int(micros * 1.15e9), bytes_accessed=int(micros * 3e6), transcendentals=0
    )


def mask_rows(value, lo, begin):
    if lo >= LATEST:
        return value
    seen = iota(value.shape, 0) >= begin - lo
    return jnp.where(seen, value, jnp.zeros_like(value))


def vmem(limit=60):
    return pltpu.CompilerParams(vmem_limit_bytes=limit * 1024 * 1024)


def bits_of(size):
    return [1 << b for b in range(size.bit_length() - 1)]


def swap(x, dp, fsdp, bit_dp, bit_fsdp):
    pairs = []
    for d in range(dp):
        for f in range(fsdp):
            pairs.append((d * fsdp + f, (d ^ bit_dp) * fsdp + (f ^ bit_fsdp)))
    return lax.ppermute(x, ("dp", "fsdp"), pairs)


def gather_rows(x, dp, fsdp, swap_fn, join):
    far = bits_of(fsdp)
    for bit in reversed(far[1:]):
        x = join(x, swap_fn(x, 0, bit))
    half = x.shape[0] // 2
    a, b = x[:half], x[half:]
    for first, second in zip(reversed(bits_of(dp)), bits_of(dp)):
        a2 = swap_fn(a, first, 0)
        b2 = swap_fn(b, second, 0)
        a, b = join(a, a2), join(b, b2)
    x = join(a, b)
    return join(x, swap_fn(x, 0, far[0]))


def row_order(dp, fsdp):
    share = HID // fsdp
    part = share // dp
    start = np.arange(part)

    def shifted(x, bit_dp, bit_fsdp):
        return x ^ (bit_fsdp * share + bit_dp * part)

    return gather_rows(
        start, dp, fsdp, shifted, lambda p, q: np.concatenate([p, q])
    )


def pack_kernel(d_ref, cin, mid, cout, fin, fout, wx, w1):
    share = cout.shape[0]
    part = wx.shape[0]
    rows = max(part, 16)
    sel = (iota((rows, share), 1) == d_ref[0] * part + iota((rows, share), 0)).astype(BF16)
    wx[...] = jnp.zeros_like(wx)
    w1[:, T_WHOLE:T_PAD] = jnp.zeros((share, T_PAD - T_WHOLE), BF16)
    w1[:, 0:LOOKBACK] = (fin[...] * 0.5).astype(BF16)

    def put(at, value, scale=0.5):
        picked = mm(sel, value.astype(BF16)) * scale
        wx[:, at : at + value.shape[1]] = picked[:part].astype(BF16)

    put(C_IN, cin[...])
    put(C_M0, mid[0])
    put(C_M1, mid[1])
    put(C_OUT, cout[...], 1.0)
    put(C_ALL + R_M2, mid[2])
    put(C_ALL + R_M3, mid[3])
    put(C_ALL + R_OUT, fout[...], 1.0)


def stats_kernel(count, *refs):
    pooled, table = refs[-2:]
    lens, series = refs[count : count + 2]
    hists = refs[:count]
    wide = hists[0].shape[1]

    @pl.when(pl.program_id(0) == 0)
    def _():
        table[...] = jnp.zeros_like(table)

    chunk = 32
    at = LP // chunk * chunk
    rest = LP - at
    pooled[at:HID, :] = jnp.zeros((HID - at, pooled.shape[1]), F32)
    for q, hist in enumerate(hists):
        cols = slice(q * wide, (q + 1) * wide)
        ahead = iota((chunk, wide), 0) * 8 + (lens[:, cols] - LOOKBACK)
        sums = jnp.zeros((8, wide), F32)
        squares = jnp.zeros((8, wide), F32)

        def load(g, s, count):
            h = hist[pl.ds(g * 8 + s, count, stride=8), :]
            if g * 8 >= LATEST:
                return h
            return jnp.where(ahead[0:count] >= -(g * 8 + s), h, 0.0)

        for g in range(0, at, chunk):
            total = load(g, 0, chunk)
            sq = total * total
            for s in range(1, 8):
                h = load(g, s, chunk)
                total += h
                sq += h * h
            for v in range(0, chunk, 8):
                sums += total[v : v + 8]
                squares += sq[v : v + 8]
            pooled[g : g + chunk, cols] = total * 0.125
        total = load(at, 0, rest)
        sq = total * total
        for s in range(1, 8):
            h = load(at, s, rest)
            total += h
            sq += h * h
        pooled[at:LP, cols] = total * 0.125
        sum_row = jnp.sum(sums, 0, keepdims=True) + jnp.sum(total, 0, keepdims=True)
        square_row = jnp.sum(squares, 0, keepdims=True) + jnp.sum(sq, 0, keepdims=True)
        row = iota((16, wide), 0)
        kind = row % 3
        v = jnp.where(
            kind == 0,
            sum_row,
            jnp.where(kind == 1, square_row, lens[:, cols].astype(F32)),
        )
        hi, mid, low = split3(v)
        piece = jnp.where(
            row < 3,
            hi.astype(F32),
            jnp.where(row < 6, mid.astype(F32), jnp.where(row < 9, low.astype(F32), 0.0)),
        ).astype(BF16)
        hot = (iota((SERIES, wide), 0) == series[:, cols]).astype(BF16)
        t = mm(piece, hot, NT)
        table[0:3, :] += t[0:3] + t[3:6] + t[6:9]


def coarse_kernel(p_in, lens, series, table, x_top, x_low, offs, abscol,
                  pooled_out, th_out, look_out, wc, offs_p, looker):
    cols = p_in.shape[1]

    @pl.when(pl.program_id(0) == 0)
    def _():
        perm = perm_of(abscol)
        half = HID // 2
        wc[0:half, :] = x_top[...]
        wc[half:HID, :] = x_low[...]
        for at in (C_M0, C_M1):
            wc[:, at : at + HID] = mm(wc[:, at : at + HID], perm, NT).astype(BF16)
        offs_p[...] = mm_exact2(perm, offs[0:HID, :])
        count = jnp.maximum(table[2:3, :], 1.0)
        centre = table[0:1, :] / count
        spread = jnp.sqrt(table[1:2, :] / count + 1e-05)
        inverse = 1.0 / spread
        shifted = centre / spread
        row = iota((16, SERIES), 0)
        v = jnp.where(row < 3, inverse, shifted)
        hi, mid, low = split3(v)
        kind = row % 3
        looker[...] = jnp.where(
            row < 6,
            jnp.where(
                kind == 0,
                hi.astype(F32),
                jnp.where(kind == 1, mid.astype(F32), low.astype(F32)),
            ),
            0.0,
        ).astype(BF16)

    hot = (iota((SERIES, cols), 0) == series[...]).astype(BF16)
    got = mm(looker[...], hot)
    inv = got[0:1] + got[1:2] + got[2:3]
    cinv = got[3:4] + got[4:5] + got[5:6]
    look_out[...] = jnp.where(iota((8, cols), 0) == 0, inv, cinv)
    group = iota((HID, cols), 0)
    begin = LOOKBACK - lens[...]
    share = jnp.clip(group * 8 + 8 - begin, 0, 8).astype(F32) * 0.125
    pooled = jnp.where(group < LP, p_in[...] * inv - cinv * share, 0.0).astype(BF16)
    pooled_out[...] = pooled
    v = activate(mm(wc[:, C_IN : C_IN + HID], pooled) + offs_p[:, 0:1])[0]
    v = activate(mm(wc[:, C_M0:C_M1], v.astype(BF16)) + offs_p[:, 1:2])[0]
    v = activate(mm(wc[:, C_M1:C_OUT], v.astype(BF16)) + offs_p[:, 2:3])[0]
    theta = mm(wc[:, C_OUT:C_ALL], v.astype(BF16), TN) + offs[0:256, 3:4]
    theta = theta * (1.0 / 48.0)
    hi = theta.astype(BF16).astype(F32)
    at = iota((256, cols), 0)
    c_hi, c_mid, c_low = split3(cinv)
    with_shift = jnp.where(
        at == CINV_AT,
        c_hi.astype(F32),
        jnp.where(
            at == CINV_AT + 1,
            c_mid.astype(F32),
            jnp.where(at == CINV_AT + 2, c_low.astype(F32), hi),
        ),
    )
    th_out[...] = with_shift.astype(BF16)


def fold_lanes(x):
    total = x[:, 0:128]
    for at in range(128, x.shape[1], 128):
        total = total + x[:, at : at + 128]
    return total


def hidden_rows(acc, perm):
    lane = iota((HID, 128), 1)
    v = jnp.zeros((HID, 128), F32)
    for k in range(3):
        v = jnp.where(lane == k, jnp.sum(acc[k], 1, keepdims=True), v)
    return mm_exact(v, perm, TN)[0:8]


def last_row(acc):
    v = jnp.broadcast_to(jnp.sum(acc, 1, keepdims=True), acc.shape)
    return jnp.transpose(v, (1, 0))[0:8]


def perm_of(abscol):
    return (iota((HID, HID), 1) == abscol[...]).astype(BF16)


def fine_kernel(hist, later, flags, look, lens, th, w1, x_top, x_low, btab_t, ftab, ftab_t, offs, abscol,
                res, dz1, dz1_p, fore, small, keep, send,
                acc, acc4, acc_loss, dz4, total, wr, offs_p, perm):
    cols = hist.shape[1]
    step = pl.program_id(0)

    @pl.when(step == 0)
    def _():
        acc[...] = jnp.zeros_like(acc)
        acc4[...] = jnp.zeros_like(acc4)
        acc_loss[...] = jnp.zeros_like(acc_loss)
        perm[...] = perm_of(abscol)
        wr[0 : HID // 2, :] = x_top[...]
        wr[HID // 2 : HID, :] = x_low[...]
        wr[:, R_M3:R_OUT] = mm(wr[:, R_M3:R_OUT], perm[...], NT).astype(BF16)
        offs_p[...] = mm_exact2(perm[...], offs[0:HID, :])
        total[...] = jnp.zeros_like(total)
        dz4[OUTLOOK:O_PAD, :] = jnp.zeros((O_PAD - OUTLOOK, cols), BF16)

    inv = look[0:1, :]
    cinv = look[1:2, :]
    begin = LOOKBACK - lens[...]
    th_hi = th[...]
    res[LOOKBACK:T_PAD, :] = jnp.zeros((T_PAD - LOOKBACK, cols), BF16)
    h1 = offs[0:HID, 0:1]
    for at in range(0, T_LIVE, 1024):
        end = min(at + 1024, T_LIVE)
        live = min(end, LOOKBACK)
        shift = mm(btab_t[at:live, :], th_hi)
        for lo in range(at, live, 512):
            width = min(512, live - lo)
            r = hist[lo : lo + width, :] * inv - shift[lo - at : lo - at + width]
            res[lo : lo + width, :] = mask_rows(r, lo, begin).astype(BF16)
        h1 = h1 + mm(w1[:, at:end], res[at:end, :])
    v1, u1 = activate(h1)
    b1 = v1.astype(BF16)
    h2 = mm(wr[:, R_M2:R_M3], b1) + offs_p[:, 1:2]
    v2, u2 = activate(h2)
    b2 = v2.astype(BF16)
    h3 = mm(wr[:, R_M3:R_OUT], b2) + offs_p[:, 2:3]
    v3, u3 = activate(h3)
    b3 = v3.astype(BF16)
    est = mm(wr[:, R_OUT:R_ALL], b3, TN) + mm(ftab_t[...], th_hi) + offs[:, 3:4]
    counted = flags[...].astype(F32)
    err = (est[0:OUTLOOK] - (later[...] * inv - cinv)) * counted
    acc_loss[0:1, :] += jnp.sum(err * err, 0, keepdims=True)
    acc_loss[1:2, :] += jnp.sum(counted, 0, keepdims=True)
    d4 = (2.0 * err).astype(BF16)
    acc4[0:OUTLOOK, :] += fold_lanes(d4.astype(F32))
    dz4[0:OUTLOOK, :] = d4
    d4 = dz4[...]
    fore[...] = jnp.zeros_like(fore)
    fore[FORE_ROWS, :] = mm(ftab[FORE_ROWS, :], d4) * (1.0 / 48.0)

    def back(upstream, slope, row):
        d = (upstream * slope).astype(BF16)
        acc[row] += fold_lanes(d.astype(F32))
        return d

    d3 = back(mm(wr[:, R_OUT:R_ALL], d4), slope_once(h3, u3, v3), 2)
    total[:, R_OUT:R_ALL] += mm(b3, d4, NT)
    d2 = back(mm(wr[:, R_M3:R_OUT], d3, TN), slope_twice(h2, u2, v2), 1)
    total[:, R_M3:R_OUT] += mm(d3, b2, NT)
    d1 = back(mm(wr[:, R_M2:R_M3], d2, TN), slope_twice(h1, u1, v1), 0)
    dz1[...] = d1
    dz1_p[...] = mm(perm[...], d1).astype(BF16)
    total[:, R_M2:R_M3] += mm(d2, b1, NT)

    @pl.when(step == pl.num_programs(0) - 1)
    def _():
        small[...] = last_row(acc4[...])
        loss = jnp.sum(acc_loss[0:1, :], 1, keepdims=True)
        tally = jnp.sum(acc_loss[1:2, :], 1, keepdims=True)
        row = iota((8, O_PAD), 0)
        small[...] = jnp.where(
            row == 3,
            small[...],
            jnp.where(row == 4, loss, jnp.where(row == 5, tally, 0.0)),
        )
        half = HID // 2
        for cols_k in (slice(R_M2, R_M3), slice(R_M3, R_OUT), slice(R_OUT, R_ALL)):
            g = total[:, cols_k]
            if cols_k.start == R_M3:
                g = natural_columns(g, perm[...])
            keep[:, cols_k] = g[0:half]
            send[:, cols_k] = g[half:HID].astype(BF16)
        small[0:3, 0:HID] = hidden_rows(acc, perm[...])[0:3]
        small[0:1, 0:HID] = last_row(acc[0])[0:1]


def natural_columns(g, perm):
    half = HID // 2
    hi = g.astype(BF16)
    low = (g - hi.astype(F32)).astype(BF16)
    out = mm(hi, perm)
    return jnp.concatenate([out[0:half] + mm(low[0:half], perm), out[half:HID]], 0)


def fine_in_grad_kernel(dz1, res, rest_keep, rest_send, keep, send):
    step = pl.program_id(0)
    tile = keep.shape[1]
    whole = T_PAD // tile
    half = HID // 2

    def product(width):
        for lo in range(0, width, 512):
            end = min(lo + 512, width)
            g = jnp.transpose(mm(res[lo:end, :], dz1[...], NT), (1, 0))
            keep[:, lo:end] = g[0:half]
            send[:, lo:end] = g[half:HID].astype(BF16)

    @pl.when(step < whole)
    def _():
        product(tile)

    for k in range(whole, F_ALL // tile):

        @pl.when(step == k)
        def _():
            edge = max(T_PAD - k * tile, 0)
            if edge:
                product(edge)
            begin = k * tile + edge - T_PAD
            keep[:, edge:tile] = rest_keep[:, begin : begin + tile - edge]
            send[:, edge:tile] = rest_send[:, begin : begin + tile - edge]


def back_kernel(first, final, *refs):
    dz1f, fore, lens, pooled, w1, btab, wc, abscol, offs_p = refs[:9]
    outs = refs[9 if first else 10 : -4]
    small = outs[-1]
    acc, acc4, total, back_grad = refs[-4:]
    cols = dz1f.shape[1]
    step = pl.program_id(0)

    @pl.when(step == 0)
    def _():
        acc[...] = jnp.zeros_like(acc)
        acc4[...] = jnp.zeros_like(acc4)
        total[...] = jnp.zeros_like(total) if first else refs[9][...]

    begin = LOOKBACK - lens[...]
    d1f = dz1f[...]
    back_grad[...] = jnp.zeros_like(back_grad)
    for at in range(0, T_LIVE, T_LIVE // 2):
        wide = mm(w1[:, at : at + T_LIVE // 2], d1f, TN)
        for lo in range(at, at + T_LIVE // 2, 512):
            width = min(512, at + T_LIVE // 2 - lo)
            d = mask_rows(wide[lo - at : lo - at + width], lo, begin).astype(BF16)
            first_knot = max(lo // RATIO - 1, 0) // 8 * 8
            last_knot = min(-(-(lo + width + RATIO) // RATIO), BACK)
            last_knot = -(-last_knot // 8) * 8
            knots = slice(first_knot, last_knot)
            back_grad[knots, :] += mm(btab[knots, lo : lo + width], d)
    row = iota((256, cols), 0)
    d4 = (jnp.where(row < BACK, back_grad[...] * (-2.0 / 48.0), 0.0) + fore[...]).astype(BF16)
    acc4[...] += fold_lanes(d4.astype(F32))

    def ahead(w, entering, k):
        h = mm(w, entering) + offs_p[:, k : k + 1]
        value, u = activate(h)
        return h, u, value, value.astype(BF16)

    p = pooled[...]
    h1, u1, v1, b1 = ahead(wc[:, C_IN : C_IN + HID], p, 0)
    h2, u2, v2, b2 = ahead(wc[:, C_M0:C_M1], b1, 1)
    h3, u3, v3, b3 = ahead(wc[:, C_M1:C_OUT], b2, 2)

    def back(upstream, slope, row):
        d = (upstream * slope).astype(BF16)
        acc[row] += fold_lanes(d.astype(F32))
        return d

    d3 = back(mm(wc[:, C_OUT:C_ALL], d4), slope_once(h3, u3, v3), 2)
    total[:, C_OUT:C_ALL] += mm(b3, d4, NT)
    d2 = back(mm(wc[:, C_M1:C_OUT], d3, TN), slope_twice(h2, u2, v2), 1)
    total[:, C_M1:C_OUT] += mm(d3, b2, NT)
    d1 = back(mm(wc[:, C_M0:C_M1], d2, TN), slope_twice(h1, u1, v1), 0)
    total[:, C_M0:C_M1] += mm(d2, b1, NT)
    total[:, C_IN:C_M0] += mm(d1, p, NT)

    @pl.when(step == pl.num_programs(0) - 1)
    def _():
        perm = perm_of(abscol)
        small[...] = jnp.zeros_like(small)
        small[0:3, :] = hidden_rows(acc, perm)[0:3]
        small[3:4, 0:256] = last_row(acc4[...])[0:1]
        if not final:
            outs[0][...] = total[...]
            return
        half = HID // 2
        for a, b in zip((C_IN, C_M0, C_M1, C_OUT), (C_M0, C_M1, C_OUT, C_ALL)):
            g = total[:, a:b]
            if a in (C_M0, C_M1):
                g = natural_columns(g, perm)
            outs[0][:, a:b] = g[0:half]
            outs[1][:, a:b] = g[half:HID].astype(BF16)


def adam_math(weight, mean_old, square_old, grad):
    mean_new = beta_first * mean_old + (1.0 - beta_first) * grad
    square_new = beta_second * square_old + (1.0 - beta_second) * grad * grad
    fix = (1.0 - beta_second**STEP) ** 0.5
    gain = learn_rate * fix / (1.0 - beta_first**STEP)
    weight_new = weight * (1.0 - learn_rate * weight_decay) - gain * mean_new / (
        jnp.sqrt(square_new) + adam_epsilon * fix
    )
    return weight_new, mean_new, square_new


def adam_kernel(dp, small, relrow, *refs):
    pieces, refs = refs[: 2 * dp], refs[2 * dp :]
    ins, biases, outs, bias_outs = refs[:15], refs[15:18], refs[18:33], refs[33:36]
    loss, tally, norm, grads, bias_grad = refs[36:]
    part = pieces[0].shape[0]
    share = dp * part
    order = [0, *range(2, dp + 1), 1, *range(dp + 1, 2 * dp)]
    for k, index in enumerate(order):
        piece = pieces[index]
        at, row = (0, k) if k < dp else (F_ALL, k - dp)
        grads[row * part : (row + 1) * part, at : at + piece.shape[1]] = piece[...].astype(F32)
    place = (iota((share, share), 1) == relrow[...]).astype(BF16)

    count = small[5:6, 0:1]
    sums = small[0:4, :]
    bias_square = jnp.sum(jnp.sum(sums * sums, 0, keepdims=True), 1, keepdims=True)
    grad_norm = jnp.sqrt(small[6:7, 0:1] + bias_square) / count
    s = clip_level / jnp.maximum(grad_norm, clip_level) / count
    loss[...] = small[4:5, 0:1]
    tally[...] = count
    norm[...] = grad_norm
    for k in range(3):
        bias_grad[:, k * HID : (k + 1) * HID] = small[k : k + 1, O_PAD : O_PAD + HID]
        bias_grad[:, (k + 3) * HID : (k + 4) * HID] = small[k : k + 1, 0:HID]
    last = 6 * HID + BACK + FORE
    bias_grad[:, 6 * HID : last] = small[3:4, O_PAD : O_PAD + BACK + FORE]
    bias_grad[:, last : last + OUTLOOK] = small[3:4, 0:OUTLOOK]
    for out, value in zip(
        bias_outs, adam_math(*(x[...] for x in biases), bias_grad[...] * s)
    ):
        out[...] = value

    def step(i, at, width, index):
        g = grads[:, at : at + width]
        hi = g.astype(BF16)
        low = (g - hi.astype(F32)).astype(BF16)
        grad = (mm(place, hi, TN) + mm(place, low, TN)) * s
        old = [ins[i + 5 * k][index] for k in range(3)]
        for k, value in enumerate(adam_math(*old, grad)):
            outs[i + 5 * k][index] = value

    every = slice(None)
    step(0, F_ALL + C_IN, LP, (every, every))
    step(1, F_ALL + C_M0, HID, 0)
    step(1, F_ALL + C_M1, HID, 1)
    step(1, T_PAD + R_M2, HID, 2)
    step(1, T_PAD + R_M3, HID, 3)
    step(2, F_ALL + C_OUT, BACK + FORE, (every, every))
    step(4, T_PAD + R_OUT, OUTLOOK, (every, every))
    for lo in range(0, LOOKBACK, 512):
        width = min(512, LOOKBACK - lo)
        step(3, lo, width, (every, slice(lo, lo + width)))


def interp_table(count, length, first_row, rows, cols):
    spots = np.clip((np.arange(length) + 0.5) * (count / length) - 0.5, 0.0, count - 1.0)
    table = np.maximum(0.0, 1.0 - np.abs(spots[None, :] - np.arange(count)[:, None]))
    out = np.zeros((rows, cols), np.float32)
    out[first_row : first_row + count, :length] = np.round(table * 48.0)
    return out


def assemble_kernel(plan, count, *refs):
    ins, outs = refs[:count], refs[count:]
    for which, begin, at, size, out in plan:
        outs[out][at : at + size, :] = ins[which][begin : begin + size, :]


def assemble(*outs):
    if any(n % 16 or b % 16 for out in outs for _, b, n in out):
        return [
            jnp.concatenate([x[b : b + n] for x, b, n in out], 0) for out in outs
        ]
    ins, plan, shapes = [], [], []
    for k, out in enumerate(outs):
        at = 0
        for x, begin, size in out:
            which = next((i for i, y in enumerate(ins) if y is x), len(ins))
            if which == len(ins):
                ins.append(x)
            plan.append((which, begin, at, size, k))
            at += size
        shapes.append(jax.ShapeDtypeStruct((at, out[0][0].shape[1]), out[0][0].dtype))
    def blocks(arrays):
        return [pl.BlockSpec(x.shape, lambda i: (0, 0)) for x in arrays]

    return pl.pallas_call(
        functools.partial(assemble_kernel, tuple(plan), len(ins)),
        grid=(1,),
        out_shape=tuple(shapes),
        in_specs=blocks(ins),
        out_specs=tuple(blocks(shapes)),
        compiler_params=vmem(63),
        cost_estimate=cost(1),
        name="assemble",
    )(*ins)


def add_rows(pairs, plan):
    sums = [keep + got.astype(F32) for keep, got in pairs]
    return [
        sums[which][begin : begin + size].astype(kind) for which, begin, size, kind in plan
    ]


def spec(shape, index):
    return pl.BlockSpec(shape, index)


def fixed(shape):
    return pl.BlockSpec(shape, lambda i: (0,) * len(shape), pipeline_mode=pl.Buffered(1))


def body(
    history, later_observed, lengths, counted_flags, series,
    coarse_in, middle, rough_final_matrix, fine_in, sharp_final_matrix, offset_vectors,
    coarse_in_mean, middle_mean, rough_final_first, fine_in_mean, sharp_final_first, biases_mean,
    coarse_in_square, middle_square, rough_final_second, fine_in_square, sharp_final_second,
    biases_square,
):
    dp, fsdp = lax.axis_size("dp"), lax.axis_size("fsdp")
    d_here, f_here = lax.axis_index("dp"), lax.axis_index("fsdp")
    rows = history.shape[0]
    share = HID // fsdp
    part = share // dp

    def exchange(x, bit_dp, bit_fsdp):
        return swap(x, dp, fsdp, bit_dp, bit_fsdp)

    def join(p, q):
        return jnp.concatenate([p, q], 0)

    here = f_here * share + d_here * part
    order = row_order(dp, fsdp)
    abscol = (jnp.asarray(order, jnp.int32) ^ here).reshape(HID, 1)
    together = lax.optimization_barrier

    def by_hidden(cin, mid, cout, fin, fout):
        return (cin.T, mid.transpose(0, 2, 1), cout, fin.T, fout)

    def one_step(arrays):
        return [
            pl.BlockSpec(x.shape, lambda i, n=len(x.shape): (0,) * n) for x in arrays
        ]

    shard_now = by_hidden(
        coarse_in, middle, rough_final_matrix, fine_in, sharp_final_matrix
    )

    x_part, w1_part = pl.pallas_call(
        pack_kernel,
        out_shape=(
            jax.ShapeDtypeStruct((part, C_ALL + R_ALL), BF16),
            jax.ShapeDtypeStruct((share, T_PAD), BF16),
        ),
        grid=(1,),
        in_specs=[pl.BlockSpec(memory_space=pltpu.SMEM)] + one_step(shard_now),
        out_specs=(
            pl.BlockSpec((part, C_ALL + R_ALL), lambda i: (0, 0)),
            pl.BlockSpec((share, T_PAD), lambda i: (0, 0)),
        ),
        compiler_params=vmem(63),
        cost_estimate=cost(1),
        name="pack_weights",
    )(d_here.reshape(1), *shard_now)

    hist = history.T
    lens = lengths.reshape(1, rows)
    series_row = series.reshape(1, rows)
    side = rows // 2
    calls = (1, 1, 2)

    def stats(which, lens_row, pool):
        count = 2
        unit = rows // (128 * count * sum(calls))
        steps = calls[which] * unit
        at = sum(calls[:which]) * unit

        def hist_spec(q):
            return spec((LOOKBACK, 128), lambda i: (0, (at + i) * count + q))

        def row_spec():
            return spec((1, 128 * count), lambda i: (0, at + i))

        return pl.pallas_call(
            functools.partial(stats_kernel, count),
            grid=(steps,),
            out_shape=(
                jax.ShapeDtypeStruct((HID, rows), F32),
                jax.ShapeDtypeStruct((8, SERIES), F32),
            ),
            in_specs=[hist_spec(q) for q in range(count)]
            + [row_spec(), row_spec()]
            + [pl.BlockSpec(memory_space=pl.ANY) for _ in pool],
            out_specs=(
                spec((HID, 128 * count), lambda i: (0, at + i)),
                pl.BlockSpec((8, SERIES), lambda i: (0, 0)),
            ),
            compiler_params=vmem(63),
            cost_estimate=cost(6),
            input_output_aliases={count + 2: 0} if pool else {},
            name="window_stats",
        )(*[hist] * count, lens_row, series_row, *pool)

    up, down = bits_of(dp), bits_of(dp)[::-1]
    near, *far = bits_of(fsdp)
    moves = [(0, bit) for bit in reversed(far)] + list(zip(down, up)) + [(0, near)]

    def cut_rows(x):
        half = x.shape[0] // 2
        return x[:half], x[half:]

    def add_over(table, steps):
        for bit_dp, bit_fsdp in steps:
            table = table + exchange(table, bit_dp, bit_fsdp)
        return table

    x = [x_part]
    pools, tables, table = [], [], None
    sums = [(0, bit) for bit in bits_of(fsdp)] + [(bit, 0) for bit in up]
    sums = [sums[:3], sums[3:]]
    for k, move in enumerate(moves[:-1]):
        along_dp = k >= len(far)
        if along_dp and len(x) == 1:
            x = list(cut_rows(x[0]))
        got = [exchange(h, b, 0) for h, b in zip(x, move)] if along_dp else [exchange(x[0], *move)]
        if k < len(calls):
            lens_row, *x = together((lens, *x))
            pool, this = stats(k, lens_row, pools[-1:])
            pools.append(pool)
            *got, this = together((*got, this))
            tables.append(this)
        elif sums:
            if table is None:
                table = sum(tables[1:], tables[0])
            table = add_over(table, sums.pop(0))
            *got, table = together((*got, table))
        if k == len(far) - 1:
            w1_part, *got = together((w1_part, *got))
            w1 = lax.all_gather(w1_part, "fsdp", axis=0, tiled=True)
        if k < len(moves) - 2:
            x = [join(h, g) for h, g in zip(x, got)]
    x_top = jnp.concatenate([h for pair in zip(x, got) for h in pair], 0)
    x_low = exchange(x_top, *moves[-1])
    for steps in sums:
        table = add_over(table, steps)

    hidden = offset_vectors[: 6 * HID].reshape(6, HID)
    rough_bias = offset_vectors[6 * HID : 6 * HID + BACK + FORE]
    sharp_bias = offset_vectors[6 * HID + BACK + FORE :]

    def bias_cols(three, last, width):
        out = jnp.pad(three, ((0, 0), (0, width - HID)))
        out = join(out, jnp.pad(last, (0, width - last.shape[0]))[None])
        return jnp.pad(out, ((0, 4), (0, 0))).T

    coarse_offs = bias_cols(0.5 * hidden[:3], rough_bias, HID)
    fine_offs = bias_cols(0.5 * hidden[3:], sharp_bias, O_PAD)

    r = 512
    tiles = rows // r

    def col_spec(height, begin=0, last=tiles - 1):
        return spec((height, r), lambda i: (0, jnp.minimum(begin + i, last)))

    half_block = pl.BlockSpec(
        (HID // 2, C_ALL), lambda i: (0, 0), pipeline_mode=pl.Buffered(1)
    )
    pooled, th, look, wc, offs_p = pl.pallas_call(
        coarse_kernel,
        grid=(tiles,),
        out_shape=(
            jax.ShapeDtypeStruct((HID, rows), BF16),
            jax.ShapeDtypeStruct((256, rows), BF16),
            jax.ShapeDtypeStruct((8, rows), F32),
            jax.ShapeDtypeStruct((HID, C_ALL), BF16),
            jax.ShapeDtypeStruct((HID, 8), F32),
        ),
        in_specs=[
            col_spec(HID),
            col_spec(1),
            col_spec(1),
            fixed((8, SERIES)),
            half_block,
            half_block,
            fixed((HID, 8)),
            fixed((HID, 1)),
        ],
        out_specs=(
            col_spec(HID),
            col_spec(256),
            col_spec(8),
            pl.BlockSpec((HID, C_ALL), lambda i: (0, 0)),
            pl.BlockSpec((HID, 8), lambda i: (0, 0)),
        ),
        scratch_shapes=[pltpu.VMEM((16, SERIES), BF16)],
        compiler_params=vmem(63),
        cost_estimate=cost(10),
        name="coarse_forward",
    )(
        pools[-1], lens, series_row, table, x_top, x_low, coarse_offs, abscol,
    )
    back_table = interp_table(BACK, LOOKBACK, 0, 256, T_PAD)
    btab = jnp.asarray(back_table, BF16)
    back_table[CINV_AT : CINV_AT + 3, :LOOKBACK] = 1.0
    btab_t = jnp.asarray(back_table.T, BF16)
    fore_table = interp_table(FORE, OUTLOOK, BACK, 256, O_PAD)
    ftab = jnp.asarray(fore_table, BF16)
    ftab_t = jnp.asarray(fore_table.T, BF16)

    tall = jax.ShapeDtypeStruct((HID, rows), BF16)
    r_shapes = (
        jax.ShapeDtypeStruct((HID // 2, R_ALL), F32),
        jax.ShapeDtypeStruct((HID // 2, R_ALL), BF16),
    )
    rest_block = pl.BlockSpec(
        (HID // 2, R_ALL), lambda i: (0, 1), pipeline_mode=pl.Buffered(1)
    )
    res, dz1, dz1_p, fore, f_small, r_keep, r_send = pl.pallas_call(
        fine_kernel,
        grid=(tiles,),
        out_shape=(
            jax.ShapeDtypeStruct((T_PAD, rows), BF16),
            tall,
            tall,
            jax.ShapeDtypeStruct((256, rows), F32),
            jax.ShapeDtypeStruct((8, O_PAD), F32),
            *r_shapes,
        ),
        in_specs=[
            col_spec(LOOKBACK),
            col_spec(OUTLOOK),
            col_spec(OUTLOOK),
            col_spec(8),
            col_spec(1),
            col_spec(256),
            fixed((HID, T_PAD)),
            rest_block,
            rest_block,
            fixed((T_PAD, 256)),
            fixed((256, O_PAD)),
            fixed((O_PAD, 256)),
            fixed((O_PAD, 8)),
            fixed((HID, 1)),
        ],
        out_specs=(
            col_spec(T_PAD),
            col_spec(HID),
            col_spec(HID),
            col_spec(256),
            pl.BlockSpec((8, O_PAD), lambda i: (0, 0)),
            *[pl.BlockSpec((HID // 2, R_ALL), lambda i: (0, 0))] * 2,
        ),
        scratch_shapes=[
            pltpu.VMEM((3, HID, 128), F32),
            pltpu.VMEM((O_PAD, 128), F32),
            pltpu.VMEM((8, r), F32),
            pltpu.VMEM((O_PAD, r), BF16),
            pltpu.VMEM((HID, R_ALL), F32),
            pltpu.VMEM((HID, R_ALL), BF16),
            pltpu.VMEM((HID, 8), F32),
            pltpu.VMEM((HID, HID), BF16),
        ],
        compiler_params=vmem(63),
        cost_estimate=cost(40),
        name="fine_block",
    )(
        hist, later_observed.T, counted_flags.T, look, lens, th,
        w1, x_top, x_low, btab_t, ftab, ftab_t, fine_offs, abscol,
    )

    wide = F_ALL // 4
    res_last = -(-T_PAD // wide) - 1

    f_keep, f_send = pl.pallas_call(
        fine_in_grad_kernel,
        grid=(F_ALL // wide,),
        out_shape=tuple(
            jax.ShapeDtypeStruct((HID // 2, F_ALL), kind) for kind in (F32, BF16)
        ),
        in_specs=[
            fixed((HID, rows)),
            spec((wide, rows), lambda i: (jnp.minimum(i, res_last), 0)),
            fixed((HID // 2, R_ALL)),
            fixed((HID // 2, R_ALL)),
        ],
        out_specs=tuple([spec((HID // 2, wide), lambda i: (0, i))] * 2),
        compiler_params=vmem(54),
        cost_estimate=cost(12),
        name="fine_in_grad",
    )(dz1_p, res, r_keep, r_send)

    def backward(at, steps, fore, before):
        first = not before
        final = at + steps == tiles
        half = HID // 2
        shapes = (
            [jax.ShapeDtypeStruct((HID, C_ALL), F32)]
            if not final
            else [jax.ShapeDtypeStruct((half, C_ALL), t) for t in (F32, BF16)]
        ) + [jax.ShapeDtypeStruct((8, HID), F32)]

        def rows_of(height):
            return col_spec(height, at)

        return pl.pallas_call(
            functools.partial(back_kernel, first, final),
            grid=(steps,),
            out_shape=tuple(shapes),
            in_specs=[
                rows_of(HID),
                rows_of(256),
                rows_of(1),
                rows_of(HID),
                fixed((HID, T_PAD)),
                fixed((256, T_PAD)),
                fixed((HID, C_ALL)),
                fixed((HID, 1)),
                fixed((HID, 8)),
            ]
            + [fixed(x.shape) for x in before],
            out_specs=tuple(pl.BlockSpec(s.shape, lambda i: (0, 0)) for s in shapes),
            scratch_shapes=[
                pltpu.VMEM((3, HID, 128), F32),
                pltpu.VMEM((256, 128), F32),
                pltpu.VMEM((HID, C_ALL), F32),
                pltpu.VMEM((256, r), F32),
            ],
            compiler_params=vmem(36),
            cost_estimate=cost(17),
            name="coarse_backward",
        )(dz1, fore, lens, pooled, w1, btab, wc, abscol, offs_p, *before)

    legs = [(0, near)] + list(zip(up, down)) + [(0, bit) for bit in far]

    def split(j):
        return 1 <= j <= len(up)

    def sum_and_cut(pairs, j):
        n = pairs[0][0].shape[0]
        if j + 1 == len(legs):
            plan = [(0, 0, n, F32)]
        elif not split(j + 1):
            plan = [(0, 0, n, F32), (1, 0, n, BF16)] if len(pairs) == 2 else [
                (0, 0, n // 2, F32), (0, n // 2, n // 2, BF16)
            ]
        else:
            size = n // 2 if len(pairs) == 2 else n // 4
            plan = []
            for k in range(2):
                which, begin = (k, 0) if len(pairs) == 2 else (0, 2 * k * size)
                plan += [(which, begin, size, F32), (which, begin + size, size, BF16)]
        flat = add_rows(pairs, plan)
        return [tuple(flat[k : k + 2]) for k in range(0, len(flat), 2)]

    def travel(state, j):
        if split(j):
            return [exchange(send, bit, 0) for (_, send), bit in zip(state, legs[j])]
        return [exchange(state[0][1], *legs[j])]

    def kept(state, got):
        return [(pair[0], g) for pair, g in zip(state, got)]

    def beside(got, *others):
        return together((*got, *others))[: len(got)]

    def hold(state, value):
        return together((value, *(x for pair in state for x in pair)))[0]

    state, got = [(f_keep, f_send)], [exchange(f_send, 0, near)]
    quarter = max(tiles // 4, 1)
    smalls, c_part, at = [], (), 0
    for j, count in enumerate((quarter, tiles - 2 * quarter, quarter)):
        if j:
            got = travel(state, j)
        *c_part, this = backward(at, count, hold(state, fore), tuple(c_part))
        smalls.append(this)
        at += count
        both = together((*got, *c_part))
        got, c_part = both[: len(got)], both[len(got) :]
        state = sum_and_cut(kept(state, got), j)
    f_state, f_leg = state, 3
    c_keep, c_send = c_part
    c_small = sum(smalls[1:], smalls[0])

    def advance(f_state, f_got, f_leg):
        f_state = sum_and_cut(kept(f_state, f_got), f_leg)
        f_leg += 1
        return f_state, travel(f_state, f_leg) if f_leg < len(legs) else None, f_leg

    def share_out(part):
        return [part] + [exchange(part, d, 0) for d in range(1, dp)]

    c_got = exchange(c_send, 0, near)
    f_got = travel(f_state, f_leg)
    c_state = sum_and_cut([(c_keep, c_got)], 0)
    f_all = None
    for j in range(1, len(legs)):
        got = travel(c_state, j)
        c_state = sum_and_cut(kept(c_state, got), j)
        if f_got is not None:
            f_state, f_got, f_leg = advance(f_state, beside(f_got, *c_state[0]), f_leg)
            if f_got is None:
                gf_part = f_state[0][0]
                f_all = share_out(gf_part.astype(BF16))
        elif j < len(legs) - 1:
            f_all = beside(f_all, *c_state[0])
    while f_got is not None:
        f_state, f_got, f_leg = advance(f_state, f_got, f_leg)
    if f_all is None:
        gf_part = f_state[0][0]
        f_all = share_out(gf_part.astype(BF16))
    gc_part = c_state[0][0]
    c_all = share_out(gc_part)

    rel = np.concatenate([np.arange(part) ^ (d * part) for d in range(dp)])
    relrow = (jnp.asarray(rel, jnp.int32) ^ (d_here * part)).reshape(share, 1)

    squares = jnp.sum(gf_part * gf_part) + jnp.sum(gc_part * gc_part)
    small = jnp.concatenate([f_small, c_small], 1)
    small = jnp.where(
        (iota(small.shape, 0) == 6) & (iota(small.shape, 1) == 0), squares, small
    )
    small = add_over(small, [(bit, 0) for bit in up] + [(0, near)])
    *c_all, small = together((*c_all, small))
    small = add_over(small, [(0, bit) for bit in far])
    pieces = [f_all[0], c_all[0], *f_all[1:], *c_all[1:]]
    shards = (
        *shard_now,
        *by_hidden(
            coarse_in_mean, middle_mean, rough_final_first, fine_in_mean, sharp_final_first
        ),
        *by_hidden(
            coarse_in_square, middle_square, rough_final_second, fine_in_square,
            sharp_final_second,
        ),
    )
    biases = [x.reshape(1, -1) for x in (offset_vectors, biases_mean, biases_square)]
    given = (small, relrow, *pieces, *shards, *biases)
    results = tuple(jax.ShapeDtypeStruct(x.shape, F32) for x in (*shards, *biases)) + (
        jax.ShapeDtypeStruct((1, 1), F32),
    ) * 3
    new = pl.pallas_call(
        functools.partial(adam_kernel, dp),
        out_shape=results,
        grid=(1,),
        in_specs=one_step(given),
        out_specs=tuple(one_step(results)),
        scratch_shapes=[
            pltpu.VMEM((share, F_ALL + C_ALL), F32),
            pltpu.VMEM(biases[0].shape, F32),
        ],
        compiler_params=vmem(63),
        cost_estimate=cost(6),
        name="adam",
    )(*given)
    return (
        *(x.reshape(()) for x in new[18:21]),
        *by_hidden(*new[0:5]), new[15].reshape(-1),
        *by_hidden(*new[5:10]), new[16].reshape(-1),
        *by_hidden(*new[10:15]), new[17].reshape(-1),
    )


def solution(mesh):
    rows2 = P(("dp", "fsdp"), None)
    rows1 = P(("dp", "fsdp"))
    weights = (P(None, "fsdp"), P(None, None, "fsdp"), P("fsdp", None), P(None, "fsdp"), P("fsdp", None), P())
    in_specs = (rows2, rows2, rows1, rows2, rows1) + weights * 3
    out_specs = (P(), P(), P()) + weights * 3
    return jax.shard_map(body, mesh=mesh, in_specs=in_specs, out_specs=out_specs, check_vma=False)
```

```python
import functools

import jax
import jax.numpy as jnp
import numpy as np
from jax import lax
from jax.experimental import pallas as pl
from jax.experimental.pallas import tpu as pltpu
from jax.sharding import PartitionSpec as P

LOOKBACK = 3600
OUTLOOK = 720
HID = 512
SERIES = 1024
STEP = 10
LP = 450
BACK = 150
FORE = 30
RATIO = 24
beta_first = 0.9
beta_second = 0.999
learn_rate = 0.01
weight_decay = 0.01
adam_epsilon = 1e-08
clip_level = 0.01

C_IN, C_M0, C_M1, C_OUT, C_ALL = 0, 512, 1024, 1536, 1792
R_M2, R_M3, R_OUT, R_ALL = 0, 512, 1024, 1792
T_PAD = 3840
F_ALL = T_PAD + R_ALL
LATEST = 2700
T_LIVE = 3712
T_WHOLE = 3584
O_PAD = 768
TILE = 256
CINV_AT = 180
FORE_ROWS = slice(144, 184)

F32 = jnp.float32
BF16 = jnp.bfloat16
NN = (((1,), (0,)), ((), ()))
NT = (((1,), (1,)), ((), ()))
TN = (((0,), (0,)), ((), ()))


def mm(a, b, dims=NN):
    return lax.dot_general(a, b, dims, preferred_element_type=F32)


def iota(shape, axis):
    return lax.broadcasted_iota(jnp.int32, shape, axis)


def split3(v):
    hi = v.astype(BF16)
    rest = v - hi.astype(F32)
    mid = rest.astype(BF16)
    return hi, mid, (rest - mid.astype(F32)).astype(BF16)


def mm_exact(v, sel, dims=NN):
    hi, mid, low = split3(v)
    return mm(hi, sel, dims) + mm(mid, sel, dims) + mm(low, sel, dims)


def mm_exact2(sel, v, dims=NN):
    hi, mid, low = split3(v)
    return mm(sel, hi, dims) + mm(sel, mid, dims) + mm(sel, low, dims)


def activate(h):
    u = 1.0 + jnp.tanh(h)
    return h * u, u


def slope_once(h, u, value):
    return u * ((0.5 + h) - 0.5 * value)


def slope_twice(h, u, value):
    return u * ((1.0 + h) + (h - value))


def cost(micros):
    return pl.CostEstimate(
        flops=int(micros * 1.15e9), bytes_accessed=int(micros * 3e6), transcendentals=0
    )


def mask_rows(value, lo, begin):
    if lo >= LATEST:
        return value
    seen = iota(value.shape, 0) >= begin - lo
    return jnp.where(seen, value, jnp.zeros_like(value))


def vmem(limit=60):
    return pltpu.CompilerParams(vmem_limit_bytes=limit * 1024 * 1024)


def bits_of(size):
    return [1 << b for b in range(size.bit_length() - 1)]


def swap(x, dp, fsdp, bit_dp, bit_fsdp):
    pairs = []
    for d in range(dp):
        for f in range(fsdp):
            pairs.append((d * fsdp + f, (d ^ bit_dp) * fsdp + (f ^ bit_fsdp)))
    return lax.ppermute(x, ("dp", "fsdp"), pairs)


def gather_rows(x, dp, fsdp, swap_fn, join):
    far = bits_of(fsdp)
    for bit in reversed(far[1:]):
        x = join(x, swap_fn(x, 0, bit))
    half = x.shape[0] // 2
    a, b = x[:half], x[half:]
    for first, second in zip(reversed(bits_of(dp)), bits_of(dp)):
        a2 = swap_fn(a, first, 0)
        b2 = swap_fn(b, second, 0)
        a, b = join(a, a2), join(b, b2)
    x = join(a, b)
    return join(x, swap_fn(x, 0, far[0]))


def row_order(dp, fsdp):
    share = HID // fsdp
    part = share // dp
    start = np.arange(part)

    def shifted(x, bit_dp, bit_fsdp):
        return x ^ (bit_fsdp * share + bit_dp * part)

    return gather_rows(
        start, dp, fsdp, shifted, lambda p, q: np.concatenate([p, q])
    )


def pack_kernel(d_ref, cin, mid, cout, fin, fout, wx, w1):
    share = cout.shape[0]
    part = wx.shape[0]
    rows = max(part, 16)
    sel = (iota((rows, share), 1) == d_ref[0] * part + iota((rows, share), 0)).astype(BF16)
    wx[...] = jnp.zeros_like(wx)
    w1[:, T_WHOLE:T_PAD] = jnp.zeros((share, T_PAD - T_WHOLE), BF16)
    w1[:, 0:LOOKBACK] = (fin[...] * 0.5).astype(BF16)

    def put(at, value, scale=0.5):
        picked = mm(sel, value.astype(BF16)) * scale
        wx[:, at : at + value.shape[1]] = picked[:part].astype(BF16)

    put(C_IN, cin[...])
    put(C_M0, mid[0])
    put(C_M1, mid[1])
    put(C_OUT, cout[...], 1.0)
    put(C_ALL + R_M2, mid[2])
    put(C_ALL + R_M3, mid[3])
    put(C_ALL + R_OUT, fout[...], 1.0)


def stats_kernel(count, *refs):
    pooled, table = refs[-2:]
    lens, series = refs[count : count + 2]
    hists = refs[:count]
    wide = hists[0].shape[1]

    @pl.when(pl.program_id(0) == 0)
    def _():
        table[...] = jnp.zeros_like(table)

    chunk = 32
    at = LP // chunk * chunk
    rest = LP - at
    pooled[at:HID, :] = jnp.zeros((HID - at, pooled.shape[1]), F32)
    for q, hist in enumerate(hists):
        cols = slice(q * wide, (q + 1) * wide)
        ahead = iota((chunk, wide), 0) * 8 + (lens[:, cols] - LOOKBACK)
        sums = jnp.zeros((8, wide), F32)
        squares = jnp.zeros((8, wide), F32)

        def load(g, s, count):
            h = hist[pl.ds(g * 8 + s, count, stride=8), :]
            if g * 8 >= LATEST:
                return h
            return jnp.where(ahead[0:count] >= -(g * 8 + s), h, 0.0)

        for g in range(0, at, chunk):
            total = load(g, 0, chunk)
            sq = total * total
            for s in range(1, 8):
                h = load(g, s, chunk)
                total += h
                sq += h * h
            for v in range(0, chunk, 8):
                sums += total[v : v + 8]
                squares += sq[v : v + 8]
            pooled[g : g + chunk, cols] = total * 0.125
        total = load(at, 0, rest)
        sq = total * total
        for s in range(1, 8):
            h = load(at, s, rest)
            total += h
            sq += h * h
        pooled[at:LP, cols] = total * 0.125
        sum_row = jnp.sum(sums, 0, keepdims=True) + jnp.sum(total, 0, keepdims=True)
        square_row = jnp.sum(squares, 0, keepdims=True) + jnp.sum(sq, 0, keepdims=True)
        row = iota((16, wide), 0)
        kind = row % 3
        v = jnp.where(
            kind == 0,
            sum_row,
            jnp.where(kind == 1, square_row, lens[:, cols].astype(F32)),
        )
        hi, mid, low = split3(v)
        piece = jnp.where(
            row < 3,
            hi.astype(F32),
            jnp.where(row < 6, mid.astype(F32), jnp.where(row < 9, low.astype(F32), 0.0)),
        ).astype(BF16)
        hot = (iota((SERIES, wide), 0) == series[:, cols]).astype(BF16)
        t = mm(piece, hot, NT)
        table[0:3, :] += t[0:3] + t[3:6] + t[6:9]


def coarse_kernel(p_in, lens, series, table, x_top, x_low, offs, abscol,
                  pooled_out, th_out, look_out, wc, offs_p, looker):
    cols = p_in.shape[1]

    @pl.when(pl.program_id(0) == 0)
    def _():
        perm = perm_of(abscol)
        half = HID // 2
        wc[0:half, :] = x_top[...]
        wc[half:HID, :] = x_low[...]
        for at in (C_M0, C_M1):
            wc[:, at : at + HID] = mm(wc[:, at : at + HID], perm, NT).astype(BF16)
        offs_p[...] = mm_exact2(perm, offs[0:HID, :])
        count = jnp.maximum(table[2:3, :], 1.0)
        centre = table[0:1, :] / count
        spread = jnp.sqrt(table[1:2, :] / count + 1e-05)
        inverse = 1.0 / spread
        shifted = centre / spread
        row = iota((16, SERIES), 0)
        v = jnp.where(row < 3, inverse, shifted)
        hi, mid, low = split3(v)
        kind = row % 3
        looker[...] = jnp.where(
            row < 6,
            jnp.where(
                kind == 0,
                hi.astype(F32),
                jnp.where(kind == 1, mid.astype(F32), low.astype(F32)),
            ),
            0.0,
        ).astype(BF16)

    hot = (iota((SERIES, cols), 0) == series[...]).astype(BF16)
    got = mm(looker[...], hot)
    inv = got[0:1] + got[1:2] + got[2:3]
    cinv = got[3:4] + got[4:5] + got[5:6]
    look_out[...] = jnp.where(iota((8, cols), 0) == 0, inv, cinv)
    group = iota((HID, cols), 0)
    begin = LOOKBACK - lens[...]
    share = jnp.clip(group * 8 + 8 - begin, 0, 8).astype(F32) * 0.125
    pooled = jnp.where(group < LP, p_in[...] * inv - cinv * share, 0.0).astype(BF16)
    pooled_out[...] = pooled
    v = activate(mm(wc[:, C_IN : C_IN + HID], pooled) + offs_p[:, 0:1])[0]
    v = activate(mm(wc[:, C_M0:C_M1], v.astype(BF16)) + offs_p[:, 1:2])[0]
    v = activate(mm(wc[:, C_M1:C_OUT], v.astype(BF16)) + offs_p[:, 2:3])[0]
    theta = mm(wc[:, C_OUT:C_ALL], v.astype(BF16), TN) + offs[0:256, 3:4]
    theta = theta * (1.0 / 48.0)
    hi = theta.astype(BF16).astype(F32)
    at = iota((256, cols), 0)
    c_hi, c_mid, c_low = split3(cinv)
    with_shift = jnp.where(
        at == CINV_AT,
        c_hi.astype(F32),
        jnp.where(
            at == CINV_AT + 1,
            c_mid.astype(F32),
            jnp.where(at == CINV_AT + 2, c_low.astype(F32), hi),
        ),
    )
    th_out[...] = with_shift.astype(BF16)


def fold_lanes(x):
    total = x[:, 0:128]
    for at in range(128, x.shape[1], 128):
        total = total + x[:, at : at + 128]
    return total


def hidden_rows(acc, perm):
    lane = iota((HID, 128), 1)
    v = jnp.zeros((HID, 128), F32)
    for k in range(3):
        v = jnp.where(lane == k, jnp.sum(acc[k], 1, keepdims=True), v)
    return mm_exact(v, perm, TN)[0:8]


def last_row(acc):
    v = jnp.broadcast_to(jnp.sum(acc, 1, keepdims=True), acc.shape)
    return jnp.transpose(v, (1, 0))[0:8]


def perm_of(abscol):
    return (iota((HID, HID), 1) == abscol[...]).astype(BF16)


def fine_kernel(hist, later, flags, look, lens, th, w1, x_top, x_low, btab_t, ftab, ftab_t, offs, abscol,
                res, dz1, dz1_p, fore, small, keep, send,
                acc, acc4, acc_loss, dz4, total, wr, offs_p, perm):
    cols = hist.shape[1]
    step = pl.program_id(0)

    @pl.when(step == 0)
    def _():
        acc[...] = jnp.zeros_like(acc)
        acc4[...] = jnp.zeros_like(acc4)
        acc_loss[...] = jnp.zeros_like(acc_loss)
        perm[...] = perm_of(abscol)
        wr[0 : HID // 2, :] = x_top[...]
        wr[HID // 2 : HID, :] = x_low[...]
        wr[:, R_M3:R_OUT] = mm(wr[:, R_M3:R_OUT], perm[...], NT).astype(BF16)
        offs_p[...] = mm_exact2(perm[...], offs[0:HID, :])
        total[...] = jnp.zeros_like(total)
        dz4[OUTLOOK:O_PAD, :] = jnp.zeros((O_PAD - OUTLOOK, cols), BF16)

    inv = look[0:1, :]
    cinv = look[1:2, :]
    begin = LOOKBACK - lens[...]
    th_hi = th[...]
    res[LOOKBACK:T_PAD, :] = jnp.zeros((T_PAD - LOOKBACK, cols), BF16)
    h1 = offs[0:HID, 0:1]
    for at in range(0, T_LIVE, 1024):
        end = min(at + 1024, T_LIVE)
        live = min(end, LOOKBACK)
        shift = mm(btab_t[at:live, :], th_hi)
        for lo in range(at, live, 512):
            width = min(512, live - lo)
            r = hist[lo : lo + width, :] * inv - shift[lo - at : lo - at + width]
            res[lo : lo + width, :] = mask_rows(r, lo, begin).astype(BF16)
        h1 = h1 + mm(w1[:, at:end], res[at:end, :])
    v1, u1 = activate(h1)
    b1 = v1.astype(BF16)
    h2 = mm(wr[:, R_M2:R_M3], b1) + offs_p[:, 1:2]
    v2, u2 = activate(h2)
    b2 = v2.astype(BF16)
    h3 = mm(wr[:, R_M3:R_OUT], b2) + offs_p[:, 2:3]
    v3, u3 = activate(h3)
    b3 = v3.astype(BF16)
    est = mm(wr[:, R_OUT:R_ALL], b3, TN) + mm(ftab_t[...], th_hi) + offs[:, 3:4]
    counted = flags[...].astype(F32)
    err = (est[0:OUTLOOK] - (later[...] * inv - cinv)) * counted
    acc_loss[0:1, :] += jnp.sum(err * err, 0, keepdims=True)
    acc_loss[1:2, :] += jnp.sum(counted, 0, keepdims=True)
    d4 = (2.0 * err).astype(BF16)
    acc4[0:OUTLOOK, :] += fold_lanes(d4.astype(F32))
    dz4[0:OUTLOOK, :] = d4
    d4 = dz4[...]
    fore[...] = jnp.zeros_like(fore)
    fore[FORE_ROWS, :] = mm(ftab[FORE_ROWS, :], d4) * (1.0 / 48.0)

    def back(upstream, slope, row):
        d = (upstream * slope).astype(BF16)
        acc[row] += fold_lanes(d.astype(F32))
        return d

    d3 = back(mm(wr[:, R_OUT:R_ALL], d4), slope_once(h3, u3, v3), 2)
    total[:, R_OUT:R_ALL] += mm(b3, d4, NT)
    d2 = back(mm(wr[:, R_M3:R_OUT], d3, TN), slope_twice(h2, u2, v2), 1)
    total[:, R_M3:R_OUT] += mm(d3, b2, NT)
    d1 = back(mm(wr[:, R_M2:R_M3], d2, TN), slope_twice(h1, u1, v1), 0)
    dz1[...] = d1
    dz1_p[...] = mm(perm[...], d1).astype(BF16)
    total[:, R_M2:R_M3] += mm(d2, b1, NT)

    @pl.when(step == pl.num_programs(0) - 1)
    def _():
        small[...] = last_row(acc4[...])
        loss = jnp.sum(acc_loss[0:1, :], 1, keepdims=True)
        tally = jnp.sum(acc_loss[1:2, :], 1, keepdims=True)
        row = iota((8, O_PAD), 0)
        small[...] = jnp.where(
            row == 3,
            small[...],
            jnp.where(row == 4, loss, jnp.where(row == 5, tally, 0.0)),
        )
        half = HID // 2
        for cols_k in (slice(R_M2, R_M3), slice(R_M3, R_OUT), slice(R_OUT, R_ALL)):
            g = total[:, cols_k]
            if cols_k.start == R_M3:
                g = natural_columns(g, perm[...])
            keep[:, cols_k] = g[0:half]
            send[:, cols_k] = g[half:HID].astype(BF16)
        small[0:3, 0:HID] = hidden_rows(acc, perm[...])[0:3]
        small[0:1, 0:HID] = last_row(acc[0])[0:1]


def natural_columns(g, perm):
    half = HID // 2
    hi = g.astype(BF16)
    low = (g - hi.astype(F32)).astype(BF16)
    out = mm(hi, perm)
    return jnp.concatenate([out[0:half] + mm(low[0:half], perm), out[half:HID]], 0)


def fine_in_grad_kernel(dz1, res, rest_keep, rest_send, keep, send):
    step = pl.program_id(0)
    tile = keep.shape[1]
    whole = T_PAD // tile
    half = HID // 2

    def product(width):
        for lo in range(0, width, 512):
            end = min(lo + 512, width)
            g = jnp.transpose(mm(res[lo:end, :], dz1[...], NT), (1, 0))
            keep[:, lo:end] = g[0:half]
            send[:, lo:end] = g[half:HID].astype(BF16)

    @pl.when(step < whole)
    def _():
        product(tile)

    for k in range(whole, F_ALL // tile):

        @pl.when(step == k)
        def _():
            edge = max(T_PAD - k * tile, 0)
            if edge:
                product(edge)
            begin = k * tile + edge - T_PAD
            keep[:, edge:tile] = rest_keep[:, begin : begin + tile - edge]
            send[:, edge:tile] = rest_send[:, begin : begin + tile - edge]


def back_kernel(first, final, *refs):
    dz1f, fore, lens, pooled, w1, btab, wc, abscol, offs_p = refs[:9]
    outs = refs[9 if first else 10 : -4]
    small = outs[-1]
    acc, acc4, total, back_grad = refs[-4:]
    cols = dz1f.shape[1]
    step = pl.program_id(0)

    @pl.when(step == 0)
    def _():
        acc[...] = jnp.zeros_like(acc)
        acc4[...] = jnp.zeros_like(acc4)
        total[...] = jnp.zeros_like(total) if first else refs[9][...]

    begin = LOOKBACK - lens[...]
    d1f = dz1f[...]
    back_grad[...] = jnp.zeros_like(back_grad)
    for at in range(0, T_LIVE, T_LIVE // 2):
        wide = mm(w1[:, at : at + T_LIVE // 2], d1f, TN)
        for lo in range(at, at + T_LIVE // 2, 512):
            width = min(512, at + T_LIVE // 2 - lo)
            d = mask_rows(wide[lo - at : lo - at + width], lo, begin).astype(BF16)
            first_knot = max(lo // RATIO - 1, 0) // 8 * 8
            last_knot = min(-(-(lo + width + RATIO) // RATIO), BACK)
            last_knot = -(-last_knot // 8) * 8
            knots = slice(first_knot, last_knot)
            back_grad[knots, :] += mm(btab[knots, lo : lo + width], d)
    row = iota((256, cols), 0)
    d4 = (jnp.where(row < BACK, back_grad[...] * (-2.0 / 48.0), 0.0) + fore[...]).astype(BF16)
    acc4[...] += fold_lanes(d4.astype(F32))

    def ahead(w, entering, k):
        h = mm(w, entering) + offs_p[:, k : k + 1]
        value, u = activate(h)
        return h, u, value, value.astype(BF16)

    p = pooled[...]
    h1, u1, v1, b1 = ahead(wc[:, C_IN : C_IN + HID], p, 0)
    h2, u2, v2, b2 = ahead(wc[:, C_M0:C_M1], b1, 1)
    h3, u3, v3, b3 = ahead(wc[:, C_M1:C_OUT], b2, 2)

    def back(upstream, slope, row):
        d = (upstream * slope).astype(BF16)
        acc[row] += fold_lanes(d.astype(F32))
        return d

    d3 = back(mm(wc[:, C_OUT:C_ALL], d4), slope_once(h3, u3, v3), 2)
    total[:, C_OUT:C_ALL] += mm(b3, d4, NT)
    d2 = back(mm(wc[:, C_M1:C_OUT], d3, TN), slope_twice(h2, u2, v2), 1)
    total[:, C_M1:C_OUT] += mm(d3, b2, NT)
    d1 = back(mm(wc[:, C_M0:C_M1], d2, TN), slope_twice(h1, u1, v1), 0)
    total[:, C_M0:C_M1] += mm(d2, b1, NT)
    total[:, C_IN:C_M0] += mm(d1, p, NT)

    @pl.when(step == pl.num_programs(0) - 1)
    def _():
        perm = perm_of(abscol)
        small[...] = jnp.zeros_like(small)
        small[0:3, :] = hidden_rows(acc, perm)[0:3]
        small[3:4, 0:256] = last_row(acc4[...])[0:1]
        if not final:
            outs[0][...] = total[...]
            return
        half = HID // 2
        for a, b in zip((C_IN, C_M0, C_M1, C_OUT), (C_M0, C_M1, C_OUT, C_ALL)):
            g = total[:, a:b]
            if a in (C_M0, C_M1):
                g = natural_columns(g, perm)
            outs[0][:, a:b] = g[0:half]
            outs[1][:, a:b] = g[half:HID].astype(BF16)


def adam_math(weight, mean_old, square_old, grad):
    mean_new = beta_first * mean_old + (1.0 - beta_first) * grad
    square_new = beta_second * square_old + (1.0 - beta_second) * grad * grad
    fix = (1.0 - beta_second**STEP) ** 0.5
    gain = learn_rate * fix / (1.0 - beta_first**STEP)
    weight_new = weight * (1.0 - learn_rate * weight_decay) - gain * mean_new / (
        jnp.sqrt(square_new) + adam_epsilon * fix
    )
    return weight_new, mean_new, square_new


def adam_kernel(dp, small, relrow, *refs):
    pieces, refs = refs[: 2 * dp], refs[2 * dp :]
    ins, biases, outs, bias_outs = refs[:15], refs[15:18], refs[18:33], refs[33:36]
    loss, tally, norm, grads, bias_grad = refs[36:]
    part = pieces[0].shape[0]
    share = dp * part
    order = [0, *range(2, dp + 1), 1, *range(dp + 1, 2 * dp)]
    for k, index in enumerate(order):
        piece = pieces[index]
        at, row = (0, k) if k < dp else (F_ALL, k - dp)
        grads[row * part : (row + 1) * part, at : at + piece.shape[1]] = piece[...].astype(F32)
    place = (iota((share, share), 1) == relrow[...]).astype(BF16)

    count = small[5:6, 0:1]
    sums = small[0:4, :]
    bias_square = jnp.sum(jnp.sum(sums * sums, 0, keepdims=True), 1, keepdims=True)
    grad_norm = jnp.sqrt(small[6:7, 0:1] + bias_square) / count
    s = clip_level / jnp.maximum(grad_norm, clip_level) / count
    loss[...] = small[4:5, 0:1]
    tally[...] = count
    norm[...] = grad_norm
    for k in range(3):
        bias_grad[:, k * HID : (k + 1) * HID] = small[k : k + 1, O_PAD : O_PAD + HID]
        bias_grad[:, (k + 3) * HID : (k + 4) * HID] = small[k : k + 1, 0:HID]
    last = 6 * HID + BACK + FORE
    bias_grad[:, 6 * HID : last] = small[3:4, O_PAD : O_PAD + BACK + FORE]
    bias_grad[:, last : last + OUTLOOK] = small[3:4, 0:OUTLOOK]
    for out, value in zip(
        bias_outs, adam_math(*(x[...] for x in biases), bias_grad[...] * s)
    ):
        out[...] = value

    def step(i, at, width, index):
        g = grads[:, at : at + width]
        hi = g.astype(BF16)
        low = (g - hi.astype(F32)).astype(BF16)
        grad = (mm(place, hi, TN) + mm(place, low, TN)) * s
        old = [ins[i + 5 * k][index] for k in range(3)]
        for k, value in enumerate(adam_math(*old, grad)):
            outs[i + 5 * k][index] = value

    every = slice(None)
    step(0, F_ALL + C_IN, LP, (every, every))
    step(1, F_ALL + C_M0, HID, 0)
    step(1, F_ALL + C_M1, HID, 1)
    step(1, T_PAD + R_M2, HID, 2)
    step(1, T_PAD + R_M3, HID, 3)
    step(2, F_ALL + C_OUT, BACK + FORE, (every, every))
    step(4, T_PAD + R_OUT, OUTLOOK, (every, every))
    for lo in range(0, LOOKBACK, 512):
        width = min(512, LOOKBACK - lo)
        step(3, lo, width, (every, slice(lo, lo + width)))


def interp_table(count, length, first_row, rows, cols):
    spots = np.clip((np.arange(length) + 0.5) * (count / length) - 0.5, 0.0, count - 1.0)
    table = np.maximum(0.0, 1.0 - np.abs(spots[None, :] - np.arange(count)[:, None]))
    out = np.zeros((rows, cols), np.float32)
    out[first_row : first_row + count, :length] = np.round(table * 48.0)
    return out


def assemble_kernel(plan, count, *refs):
    ins, outs = refs[:count], refs[count:]
    for which, begin, at, size, out in plan:
        outs[out][at : at + size, :] = ins[which][begin : begin + size, :]


def assemble(*outs):
    if any(n % 16 or b % 16 for out in outs for _, b, n in out):
        return [
            jnp.concatenate([x[b : b + n] for x, b, n in out], 0) for out in outs
        ]
    ins, plan, shapes = [], [], []
    for k, out in enumerate(outs):
        at = 0
        for x, begin, size in out:
            which = next((i for i, y in enumerate(ins) if y is x), len(ins))
            if which == len(ins):
                ins.append(x)
            plan.append((which, begin, at, size, k))
            at += size
        shapes.append(jax.ShapeDtypeStruct((at, out[0][0].shape[1]), out[0][0].dtype))
    def blocks(arrays):
        return [pl.BlockSpec(x.shape, lambda i: (0, 0)) for x in arrays]

    return pl.pallas_call(
        functools.partial(assemble_kernel, tuple(plan), len(ins)),
        grid=(1,),
        out_shape=tuple(shapes),
        in_specs=blocks(ins),
        out_specs=tuple(blocks(shapes)),
        compiler_params=vmem(63),
        cost_estimate=cost(1),
        name="assemble",
    )(*ins)


def add_rows(pairs, plan):
    sums = [keep + got.astype(F32) for keep, got in pairs]
    return [
        sums[which][begin : begin + size].astype(kind) for which, begin, size, kind in plan
    ]


def spec(shape, index):
    return pl.BlockSpec(shape, index)


def fixed(shape):
    return pl.BlockSpec(shape, lambda i: (0,) * len(shape), pipeline_mode=pl.Buffered(1))


def body(
    history, later_observed, lengths, counted_flags, series,
    coarse_in, middle, rough_final_matrix, fine_in, sharp_final_matrix, offset_vectors,
    coarse_in_mean, middle_mean, rough_final_first, fine_in_mean, sharp_final_first, biases_mean,
    coarse_in_square, middle_square, rough_final_second, fine_in_square, sharp_final_second,
    biases_square,
):
    dp, fsdp = lax.axis_size("dp"), lax.axis_size("fsdp")
    d_here, f_here = lax.axis_index("dp"), lax.axis_index("fsdp")
    rows = history.shape[0]
    share = HID // fsdp
    part = share // dp

    def exchange(x, bit_dp, bit_fsdp):
        return swap(x, dp, fsdp, bit_dp, bit_fsdp)

    def join(p, q):
        return jnp.concatenate([p, q], 0)

    here = f_here * share + d_here * part
    order = row_order(dp, fsdp)
    abscol = (jnp.asarray(order, jnp.int32) ^ here).reshape(HID, 1)
    together = lax.optimization_barrier

    def by_hidden(cin, mid, cout, fin, fout):
        return (cin.T, mid.transpose(0, 2, 1), cout, fin.T, fout)

    def one_step(arrays):
        return [
            pl.BlockSpec(x.shape, lambda i, n=len(x.shape): (0,) * n) for x in arrays
        ]

    shard_now = by_hidden(
        coarse_in, middle, rough_final_matrix, fine_in, sharp_final_matrix
    )

    x_part, w1_part = pl.pallas_call(
        pack_kernel,
        out_shape=(
            jax.ShapeDtypeStruct((part, C_ALL + R_ALL), BF16),
            jax.ShapeDtypeStruct((share, T_PAD), BF16),
        ),
        grid=(1,),
        in_specs=[pl.BlockSpec(memory_space=pltpu.SMEM)] + one_step(shard_now),
        out_specs=(
            pl.BlockSpec((part, C_ALL + R_ALL), lambda i: (0, 0)),
            pl.BlockSpec((share, T_PAD), lambda i: (0, 0)),
        ),
        compiler_params=vmem(63),
        cost_estimate=cost(1),
        name="pack_weights",
    )(d_here.reshape(1), *shard_now)

    hist = history.T
    lens = lengths.reshape(1, rows)
    series_row = series.reshape(1, rows)
    side = rows // 2
    calls = (1, 1, 2)

    def stats(which, lens_row, pool):
        count = 2
        unit = rows // (128 * count * sum(calls))
        steps = calls[which] * unit
        at = sum(calls[:which]) * unit

        def hist_spec(q):
            return spec((LOOKBACK, 128), lambda i: (0, (at + i) * count + q))

        def row_spec():
            return spec((1, 128 * count), lambda i: (0, at + i))

        return pl.pallas_call(
            functools.partial(stats_kernel, count),
            grid=(steps,),
            out_shape=(
                jax.ShapeDtypeStruct((HID, rows), F32),
                jax.ShapeDtypeStruct((8, SERIES), F32),
            ),
            in_specs=[hist_spec(q) for q in range(count)]
            + [row_spec(), row_spec()]
            + [pl.BlockSpec(memory_space=pl.ANY) for _ in pool],
            out_specs=(
                spec((HID, 128 * count), lambda i: (0, at + i)),
                pl.BlockSpec((8, SERIES), lambda i: (0, 0)),
            ),
            compiler_params=vmem(63),
            cost_estimate=cost(6),
            input_output_aliases={count + 2: 0} if pool else {},
            name="window_stats",
        )(*[hist] * count, lens_row, series_row, *pool)

    up, down = bits_of(dp), bits_of(dp)[::-1]
    near, *far = bits_of(fsdp)
    moves = [(0, bit) for bit in reversed(far)] + list(zip(down, up)) + [(0, near)]

    def cut_rows(x):
        half = x.shape[0] // 2
        return x[:half], x[half:]

    def add_over(table, steps):
        for bit_dp, bit_fsdp in steps:
            table = table + exchange(table, bit_dp, bit_fsdp)
        return table

    x = [x_part]
    pools, tables, table = [], [], None
    sums = [(0, bit) for bit in bits_of(fsdp)] + [(bit, 0) for bit in up]
    sums = [sums[:3], sums[3:]]
    for k, move in enumerate(moves[:-1]):
        along_dp = k >= len(far)
        if along_dp and len(x) == 1:
            x = list(cut_rows(x[0]))
        got = [exchange(h, b, 0) for h, b in zip(x, move)] if along_dp else [exchange(x[0], *move)]
        if k < len(calls):
            lens_row, *x = together((lens, *x))
            pool, this = stats(k, lens_row, pools[-1:])
            pools.append(pool)
            *got, this = together((*got, this))
            tables.append(this)
        elif sums:
            if table is None:
                table = sum(tables[1:], tables[0])
            table = add_over(table, sums.pop(0))
            *got, table = together((*got, table))
        if k == 0:
            w1_part, *got = together((w1_part, *got))
            w1 = lax.all_gather(w1_part, "fsdp", axis=0, tiled=True)
        if k < len(moves) - 2:
            x = [join(h, g) for h, g in zip(x, got)]
    x_top = jnp.concatenate([h for pair in zip(x, got) for h in pair], 0)
    x_low = exchange(x_top, *moves[-1])
    for steps in sums:
        table = add_over(table, steps)

    hidden = offset_vectors[: 6 * HID].reshape(6, HID)
    rough_bias = offset_vectors[6 * HID : 6 * HID + BACK + FORE]
    sharp_bias = offset_vectors[6 * HID + BACK + FORE :]

    def bias_cols(three, last, width):
        out = jnp.pad(three, ((0, 0), (0, width - HID)))
        out = join(out, jnp.pad(last, (0, width - last.shape[0]))[None])
        return jnp.pad(out, ((0, 4), (0, 0))).T

    coarse_offs = bias_cols(0.5 * hidden[:3], rough_bias, HID)
    fine_offs = bias_cols(0.5 * hidden[3:], sharp_bias, O_PAD)

    r = 512
    tiles = rows // r

    def col_spec(height, begin=0, last=tiles - 1):
        return spec((height, r), lambda i: (0, jnp.minimum(begin + i, last)))

    wide_r = 2 * r if rows % (2 * r) == 0 else r

    def wide_spec(height):
        return spec((height, wide_r), lambda i: (0, i))

    half_block = pl.BlockSpec(
        (HID // 2, C_ALL), lambda i: (0, 0), pipeline_mode=pl.Buffered(1)
    )
    pooled, th, look, wc, offs_p = pl.pallas_call(
        coarse_kernel,
        grid=(rows // wide_r,),
        out_shape=(
            jax.ShapeDtypeStruct((HID, rows), BF16),
            jax.ShapeDtypeStruct((256, rows), BF16),
            jax.ShapeDtypeStruct((8, rows), F32),
            jax.ShapeDtypeStruct((HID, C_ALL), BF16),
            jax.ShapeDtypeStruct((HID, 8), F32),
        ),
        in_specs=[
            wide_spec(HID),
            wide_spec(1),
            wide_spec(1),
            fixed((8, SERIES)),
            half_block,
            half_block,
            fixed((HID, 8)),
            fixed((HID, 1)),
        ],
        out_specs=(
            wide_spec(HID),
            wide_spec(256),
            wide_spec(8),
            pl.BlockSpec((HID, C_ALL), lambda i: (0, 0)),
            pl.BlockSpec((HID, 8), lambda i: (0, 0)),
        ),
        scratch_shapes=[pltpu.VMEM((16, SERIES), BF16)],
        compiler_params=vmem(63),
        cost_estimate=cost(10),
        name="coarse_forward",
    )(
        pools[-1], lens, series_row, table, x_top, x_low, coarse_offs, abscol,
    )
    back_table = interp_table(BACK, LOOKBACK, 0, 256, T_PAD)
    btab = jnp.asarray(back_table, BF16)
    back_table[CINV_AT : CINV_AT + 3, :LOOKBACK] = 1.0
    btab_t = jnp.asarray(back_table.T, BF16)
    fore_table = interp_table(FORE, OUTLOOK, BACK, 256, O_PAD)
    ftab = jnp.asarray(fore_table, BF16)
    ftab_t = jnp.asarray(fore_table.T, BF16)

    tall = jax.ShapeDtypeStruct((HID, rows), BF16)
    r_shapes = (
        jax.ShapeDtypeStruct((HID // 2, R_ALL), F32),
        jax.ShapeDtypeStruct((HID // 2, R_ALL), BF16),
    )
    rest_block = pl.BlockSpec(
        (HID // 2, R_ALL), lambda i: (0, 1), pipeline_mode=pl.Buffered(1)
    )
    res, dz1, dz1_p, fore, f_small, r_keep, r_send = pl.pallas_call(
        fine_kernel,
        grid=(tiles,),
        out_shape=(
            jax.ShapeDtypeStruct((T_PAD, rows), BF16),
            tall,
            tall,
            jax.ShapeDtypeStruct((256, rows), F32),
            jax.ShapeDtypeStruct((8, O_PAD), F32),
            *r_shapes,
        ),
        in_specs=[
            col_spec(LOOKBACK),
            col_spec(OUTLOOK),
            col_spec(OUTLOOK),
            col_spec(8),
            col_spec(1),
            col_spec(256),
            fixed((HID, T_PAD)),
            rest_block,
            rest_block,
            fixed((T_PAD, 256)),
            fixed((256, O_PAD)),
            fixed((O_PAD, 256)),
            fixed((O_PAD, 8)),
            fixed((HID, 1)),
        ],
        out_specs=(
            col_spec(T_PAD),
            col_spec(HID),
            col_spec(HID),
            col_spec(256),
            pl.BlockSpec((8, O_PAD), lambda i: (0, 0)),
            *[pl.BlockSpec((HID // 2, R_ALL), lambda i: (0, 0))] * 2,
        ),
        scratch_shapes=[
            pltpu.VMEM((3, HID, 128), F32),
            pltpu.VMEM((O_PAD, 128), F32),
            pltpu.VMEM((8, r), F32),
            pltpu.VMEM((O_PAD, r), BF16),
            pltpu.VMEM((HID, R_ALL), F32),
            pltpu.VMEM((HID, R_ALL), BF16),
            pltpu.VMEM((HID, 8), F32),
            pltpu.VMEM((HID, HID), BF16),
        ],
        compiler_params=vmem(63),
        cost_estimate=cost(40),
        name="fine_block",
    )(
        hist, later_observed.T, counted_flags.T, look, lens, th,
        w1, x_top, x_low, btab_t, ftab, ftab_t, fine_offs, abscol,
    )

    wide = F_ALL // 4
    res_last = -(-T_PAD // wide) - 1

    f_keep, f_send = pl.pallas_call(
        fine_in_grad_kernel,
        grid=(F_ALL // wide,),
        out_shape=tuple(
            jax.ShapeDtypeStruct((HID // 2, F_ALL), kind) for kind in (F32, BF16)
        ),
        in_specs=[
            fixed((HID, rows)),
            spec((wide, rows), lambda i: (jnp.minimum(i, res_last), 0)),
            fixed((HID // 2, R_ALL)),
            fixed((HID // 2, R_ALL)),
        ],
        out_specs=tuple([spec((HID // 2, wide), lambda i: (0, i))] * 2),
        compiler_params=vmem(54),
        cost_estimate=cost(12),
        name="fine_in_grad",
    )(dz1_p, res, r_keep, r_send)

    def backward(at, steps, fore, before):
        first = not before
        final = at + steps == tiles
        half = HID // 2
        shapes = (
            [jax.ShapeDtypeStruct((HID, C_ALL), F32)]
            if not final
            else [jax.ShapeDtypeStruct((half, C_ALL), t) for t in (F32, BF16)]
        ) + [jax.ShapeDtypeStruct((8, HID), F32)]

        def rows_of(height):
            return col_spec(height, at)

        return pl.pallas_call(
            functools.partial(back_kernel, first, final),
            grid=(steps,),
            out_shape=tuple(shapes),
            in_specs=[
                rows_of(HID),
                rows_of(256),
                rows_of(1),
                rows_of(HID),
                fixed((HID, T_PAD)),
                fixed((256, T_PAD)),
                fixed((HID, C_ALL)),
                fixed((HID, 1)),
                fixed((HID, 8)),
            ]
            + [fixed(x.shape) for x in before],
            out_specs=tuple(pl.BlockSpec(s.shape, lambda i: (0, 0)) for s in shapes),
            scratch_shapes=[
                pltpu.VMEM((3, HID, 128), F32),
                pltpu.VMEM((256, 128), F32),
                pltpu.VMEM((HID, C_ALL), F32),
                pltpu.VMEM((256, r), F32),
            ],
            compiler_params=vmem(36),
            cost_estimate=cost(17),
            name="coarse_backward",
        )(dz1, fore, lens, pooled, w1, btab, wc, abscol, offs_p, *before)

    legs = [(0, near)] + list(zip(up, down)) + [(0, bit) for bit in far]

    def split(j):
        return 1 <= j <= len(up)

    def sum_and_cut(pairs, j):
        n = pairs[0][0].shape[0]
        if j + 1 == len(legs):
            plan = [(0, 0, n, F32)]
        elif not split(j + 1):
            plan = [(0, 0, n, F32), (1, 0, n, BF16)] if len(pairs) == 2 else [
                (0, 0, n // 2, F32), (0, n // 2, n // 2, BF16)
            ]
        else:
            size = n // 2 if len(pairs) == 2 else n // 4
            plan = []
            for k in range(2):
                which, begin = (k, 0) if len(pairs) == 2 else (0, 2 * k * size)
                plan += [(which, begin, size, F32), (which, begin + size, size, BF16)]
        flat = add_rows(pairs, plan)
        return [tuple(flat[k : k + 2]) for k in range(0, len(flat), 2)]

    def travel(state, j):
        if split(j):
            return [exchange(send, bit, 0) for (_, send), bit in zip(state, legs[j])]
        return [exchange(state[0][1], *legs[j])]

    def kept(state, got):
        return [(pair[0], g) for pair, g in zip(state, got)]

    def beside(got, *others):
        return together((*got, *others))[: len(got)]

    def hold(state, value):
        return together((value, *(x for pair in state for x in pair)))[0]

    state, got = [(f_keep, f_send)], [exchange(f_send, 0, near)]
    quarter = max(tiles // 4, 1)
    smalls, c_part, at = [], (), 0
    for j, count in enumerate((quarter, tiles - 2 * quarter, quarter)):
        if j:
            got = travel(state, j)
        *c_part, this = backward(at, count, hold(state, fore), tuple(c_part))
        smalls.append(this)
        at += count
        both = together((*got, *c_part))
        got, c_part = both[: len(got)], both[len(got) :]
        state = sum_and_cut(kept(state, got), j)
    f_state, f_leg = state, 3
    c_keep, c_send = c_part
    c_small = sum(smalls[1:], smalls[0])

    def advance(f_state, f_got, f_leg):
        f_state = sum_and_cut(kept(f_state, f_got), f_leg)
        f_leg += 1
        return f_state, travel(f_state, f_leg) if f_leg < len(legs) else None, f_leg

    def share_out(part):
        return [part] + [exchange(part, d, 0) for d in range(1, dp)]

    c_got = exchange(c_send, 0, near)
    f_got = travel(f_state, f_leg)
    c_state = sum_and_cut([(c_keep, c_got)], 0)
    f_all = None
    for j in range(1, len(legs)):
        got = travel(c_state, j)
        c_state = sum_and_cut(kept(c_state, got), j)
        if f_got is not None and j != 2:
            f_state, f_got, f_leg = advance(f_state, beside(f_got, *c_state[0]), f_leg)
            if f_got is None:
                gf_part = f_state[0][0]
                f_all = share_out(gf_part.astype(BF16))
        elif f_got is None:
            f_all = beside(f_all, *c_state[0])
    while f_got is not None:
        f_state, f_got, f_leg = advance(f_state, f_got, f_leg)
    if f_all is None:
        gf_part = f_state[0][0]
        f_all = share_out(gf_part.astype(BF16))
    gc_part = c_state[0][0]
    c_all = share_out(gc_part)

    rel = np.concatenate([np.arange(part) ^ (d * part) for d in range(dp)])
    relrow = (jnp.asarray(rel, jnp.int32) ^ (d_here * part)).reshape(share, 1)

    squares = jnp.sum(gf_part * gf_part) + jnp.sum(gc_part * gc_part)
    small = jnp.concatenate([f_small, c_small], 1)
    small = jnp.where(
        (iota(small.shape, 0) == 6) & (iota(small.shape, 1) == 0), squares, small
    )
    small = add_over(small, [(bit, 0) for bit in up] + [(0, near)])
    *c_all, small = together((*c_all, small))
    small = add_over(small, [(0, bit) for bit in far])
    pieces = [f_all[0], c_all[0], *f_all[1:], *c_all[1:]]
    shards = (
        *shard_now,
        *by_hidden(
            coarse_in_mean, middle_mean, rough_final_first, fine_in_mean, sharp_final_first
        ),
        *by_hidden(
            coarse_in_square, middle_square, rough_final_second, fine_in_square,
            sharp_final_second,
        ),
    )
    biases = [x.reshape(1, -1) for x in (offset_vectors, biases_mean, biases_square)]
    given = (small, relrow, *pieces, *shards, *biases)
    results = tuple(jax.ShapeDtypeStruct(x.shape, F32) for x in (*shards, *biases)) + (
        jax.ShapeDtypeStruct((1, 1), F32),
    ) * 3
    new = pl.pallas_call(
        functools.partial(adam_kernel, dp),
        out_shape=results,
        grid=(1,),
        in_specs=one_step(given),
        out_specs=tuple(one_step(results)),
        scratch_shapes=[
            pltpu.VMEM((share, F_ALL + C_ALL), F32),
            pltpu.VMEM(biases[0].shape, F32),
        ],
        compiler_params=vmem(63),
        cost_estimate=cost(6),
        name="adam",
    )(*given)
    return (
        *(x.reshape(()) for x in new[18:21]),
        *by_hidden(*new[0:5]), new[15].reshape(-1),
        *by_hidden(*new[5:10]), new[16].reshape(-1),
        *by_hidden(*new[10:15]), new[17].reshape(-1),
    )


def solution(mesh):
    rows2 = P(("dp", "fsdp"), None)
    rows1 = P(("dp", "fsdp"))
    weights = (P(None, "fsdp"), P(None, None, "fsdp"), P("fsdp", None), P(None, "fsdp"), P("fsdp", None), P())
    in_specs = (rows2, rows2, rows1, rows2, rows1) + weights * 3
    out_specs = (P(), P(), P()) + weights * 3
    return jax.shard_map(body, mesh=mesh, in_specs=in_specs, out_specs=out_specs, check_vma=False)
```

```python
import functools

import jax
import jax.numpy as jnp
import numpy as np
from jax import lax
from jax.experimental import pallas as pl
from jax.experimental.pallas import tpu as pltpu
from jax.sharding import PartitionSpec as P

LOOKBACK = 3600
OUTLOOK = 720
HID = 512
SERIES = 1024
STEP = 10
LP = 450
BACK = 150
FORE = 30
RATIO = 24
beta_first = 0.9
beta_second = 0.999
learn_rate = 0.01
weight_decay = 0.01
adam_epsilon = 1e-08
clip_level = 0.01

C_IN, C_M0, C_M1, C_OUT, C_ALL = 0, 512, 1024, 1536, 1792
R_M2, R_M3, R_OUT, R_ALL = 0, 512, 1024, 1792
T_PAD = 3840
F_ALL = T_PAD + R_ALL
LATEST = 2700
T_LIVE = 3712
T_WHOLE = 3584
O_PAD = 768
TILE = 256
CINV_AT = 180
FORE_ROWS = slice(144, 184)

F32 = jnp.float32
BF16 = jnp.bfloat16
NN = (((1,), (0,)), ((), ()))
NT = (((1,), (1,)), ((), ()))
TN = (((0,), (0,)), ((), ()))


def mm(a, b, dims=NN):
    return lax.dot_general(a, b, dims, preferred_element_type=F32)


def iota(shape, axis):
    return lax.broadcasted_iota(jnp.int32, shape, axis)


def split3(v):
    hi = v.astype(BF16)
    rest = v - hi.astype(F32)
    mid = rest.astype(BF16)
    return hi, mid, (rest - mid.astype(F32)).astype(BF16)


def mm_exact(v, sel, dims=NN):
    hi, mid, low = split3(v)
    return mm(hi, sel, dims) + mm(mid, sel, dims) + mm(low, sel, dims)


def mm_exact2(sel, v, dims=NN):
    hi, mid, low = split3(v)
    return mm(sel, hi, dims) + mm(sel, mid, dims) + mm(sel, low, dims)


def activate(h):
    u = 1.0 + jnp.tanh(h)
    return h * u, u


def slope_once(h, u, value):
    return u * ((0.5 + h) - 0.5 * value)


def slope_twice(h, u, value):
    return u * ((1.0 + h) + (h - value))


def cost(micros):
    return pl.CostEstimate(
        flops=int(micros * 1.15e9), bytes_accessed=int(micros * 3e6), transcendentals=0
    )


def mask_rows(value, lo, begin):
    if lo >= LATEST:
        return value
    seen = iota(value.shape, 0) >= begin - lo
    return jnp.where(seen, value, jnp.zeros_like(value))


def vmem(limit=60):
    return pltpu.CompilerParams(vmem_limit_bytes=limit * 1024 * 1024)


def bits_of(size):
    return [1 << b for b in range(size.bit_length() - 1)]


def swap(x, dp, fsdp, bit_dp, bit_fsdp):
    pairs = []
    for d in range(dp):
        for f in range(fsdp):
            pairs.append((d * fsdp + f, (d ^ bit_dp) * fsdp + (f ^ bit_fsdp)))
    return lax.ppermute(x, ("dp", "fsdp"), pairs)


def gather_rows(x, dp, fsdp, swap_fn, join):
    far = bits_of(fsdp)
    for bit in reversed(far[1:]):
        x = join(x, swap_fn(x, 0, bit))
    half = x.shape[0] // 2
    a, b = x[:half], x[half:]
    for first, second in zip(reversed(bits_of(dp)), bits_of(dp)):
        a2 = swap_fn(a, first, 0)
        b2 = swap_fn(b, second, 0)
        a, b = join(a, a2), join(b, b2)
    x = join(a, b)
    return join(x, swap_fn(x, 0, far[0]))


def row_order(dp, fsdp):
    share = HID // fsdp
    part = share // dp
    start = np.arange(part)

    def shifted(x, bit_dp, bit_fsdp):
        return x ^ (bit_fsdp * share + bit_dp * part)

    return gather_rows(
        start, dp, fsdp, shifted, lambda p, q: np.concatenate([p, q])
    )


def pack_kernel(d_ref, cin, mid, cout, fin, fout, wx, w1):
    share = cout.shape[0]
    part = wx.shape[0]
    rows = max(part, 16)
    sel = (iota((rows, share), 1) == d_ref[0] * part + iota((rows, share), 0)).astype(BF16)
    wx[...] = jnp.zeros_like(wx)
    w1[:, T_WHOLE:T_PAD] = jnp.zeros((share, T_PAD - T_WHOLE), BF16)
    w1[:, 0:LOOKBACK] = (fin[...] * 0.5).astype(BF16)

    def put(at, value, scale=0.5):
        picked = mm(sel, value.astype(BF16)) * scale
        wx[:, at : at + value.shape[1]] = picked[:part].astype(BF16)

    put(C_IN, cin[...])
    put(C_M0, mid[0])
    put(C_M1, mid[1])
    put(C_OUT, cout[...], 1.0)
    put(C_ALL + R_M2, mid[2])
    put(C_ALL + R_M3, mid[3])
    put(C_ALL + R_OUT, fout[...], 1.0)


def stats_kernel(count, *refs):
    pooled, table = refs[-2:]
    lens, series = refs[count : count + 2]
    hists = refs[:count]
    wide = hists[0].shape[1]

    @pl.when(pl.program_id(0) == 0)
    def _():
        table[...] = jnp.zeros_like(table)

    chunk = 32
    at = LP // chunk * chunk
    rest = LP - at
    pooled[at:HID, :] = jnp.zeros((HID - at, pooled.shape[1]), F32)
    for q, hist in enumerate(hists):
        cols = slice(q * wide, (q + 1) * wide)
        ahead = iota((chunk, wide), 0) * 8 + (lens[:, cols] - LOOKBACK)
        sums = jnp.zeros((8, wide), F32)
        squares = jnp.zeros((8, wide), F32)

        def load(g, s, count):
            h = hist[pl.ds(g * 8 + s, count, stride=8), :]
            if g * 8 >= LATEST:
                return h
            return jnp.where(ahead[0:count] >= -(g * 8 + s), h, 0.0)

        for g in range(0, at, chunk):
            total = load(g, 0, chunk)
            sq = total * total
            for s in range(1, 8):
                h = load(g, s, chunk)
                total += h
                sq += h * h
            for v in range(0, chunk, 8):
                sums += total[v : v + 8]
                squares += sq[v : v + 8]
            pooled[g : g + chunk, cols] = total * 0.125
        total = load(at, 0, rest)
        sq = total * total
        for s in range(1, 8):
            h = load(at, s, rest)
            total += h
            sq += h * h
        pooled[at:LP, cols] = total * 0.125
        sum_row = jnp.sum(sums, 0, keepdims=True) + jnp.sum(total, 0, keepdims=True)
        square_row = jnp.sum(squares, 0, keepdims=True) + jnp.sum(sq, 0, keepdims=True)
        row = iota((16, wide), 0)
        kind = row % 3
        v = jnp.where(
            kind == 0,
            sum_row,
            jnp.where(kind == 1, square_row, lens[:, cols].astype(F32)),
        )
        hi, mid, low = split3(v)
        piece = jnp.where(
            row < 3,
            hi.astype(F32),
            jnp.where(row < 6, mid.astype(F32), jnp.where(row < 9, low.astype(F32), 0.0)),
        ).astype(BF16)
        hot = (iota((SERIES, wide), 0) == series[:, cols]).astype(BF16)
        t = mm(piece, hot, NT)
        table[0:3, :] += t[0:3] + t[3:6] + t[6:9]


def coarse_kernel(p_in, lens, series, table, x_top, x_low, offs, abscol,
                  pooled_out, th_out, look_out, wc, offs_p, looker):
    cols = p_in.shape[1]

    @pl.when(pl.program_id(0) == 0)
    def _():
        perm = perm_of(abscol)
        half = HID // 2
        wc[0:half, :] = x_top[...]
        wc[half:HID, :] = x_low[...]
        for at in (C_M0, C_M1):
            wc[:, at : at + HID] = mm(wc[:, at : at + HID], perm, NT).astype(BF16)
        offs_p[...] = mm_exact2(perm, offs[0:HID, :])
        count = jnp.maximum(table[2:3, :], 1.0)
        centre = table[0:1, :] / count
        spread = jnp.sqrt(table[1:2, :] / count + 1e-05)
        inverse = 1.0 / spread
        shifted = centre / spread
        row = iota((16, SERIES), 0)
        v = jnp.where(row < 3, inverse, shifted)
        hi, mid, low = split3(v)
        kind = row % 3
        looker[...] = jnp.where(
            row < 6,
            jnp.where(
                kind == 0,
                hi.astype(F32),
                jnp.where(kind == 1, mid.astype(F32), low.astype(F32)),
            ),
            0.0,
        ).astype(BF16)

    hot = (iota((SERIES, cols), 0) == series[...]).astype(BF16)
    got = mm(looker[...], hot)
    inv = got[0:1] + got[1:2] + got[2:3]
    cinv = got[3:4] + got[4:5] + got[5:6]
    look_out[...] = jnp.where(iota((8, cols), 0) == 0, inv, cinv)
    group = iota((HID, cols), 0)
    begin = LOOKBACK - lens[...]
    share = jnp.clip(group * 8 + 8 - begin, 0, 8).astype(F32) * 0.125
    pooled = jnp.where(group < LP, p_in[...] * inv - cinv * share, 0.0).astype(BF16)
    pooled_out[...] = pooled
    v = activate(mm(wc[:, C_IN : C_IN + HID], pooled) + offs_p[:, 0:1])[0]
    v = activate(mm(wc[:, C_M0:C_M1], v.astype(BF16)) + offs_p[:, 1:2])[0]
    v = activate(mm(wc[:, C_M1:C_OUT], v.astype(BF16)) + offs_p[:, 2:3])[0]
    theta = mm(wc[:, C_OUT:C_ALL], v.astype(BF16), TN) + offs[0:256, 3:4]
    theta = theta * (1.0 / 48.0)
    hi = theta.astype(BF16).astype(F32)
    at = iota((256, cols), 0)
    c_hi, c_mid, c_low = split3(cinv)
    with_shift = jnp.where(
        at == CINV_AT,
        c_hi.astype(F32),
        jnp.where(
            at == CINV_AT + 1,
            c_mid.astype(F32),
            jnp.where(at == CINV_AT + 2, c_low.astype(F32), hi),
        ),
    )
    th_out[...] = with_shift.astype(BF16)


def fold_lanes(x):
    total = x[:, 0:128]
    for at in range(128, x.shape[1], 128):
        total = total + x[:, at : at + 128]
    return total


def hidden_rows(acc, perm):
    lane = iota((HID, 128), 1)
    v = jnp.zeros((HID, 128), F32)
    for k in range(3):
        v = jnp.where(lane == k, jnp.sum(acc[k], 1, keepdims=True), v)
    return mm_exact(v, perm, TN)[0:8]


def last_row(acc):
    v = jnp.broadcast_to(jnp.sum(acc, 1, keepdims=True), acc.shape)
    return jnp.transpose(v, (1, 0))[0:8]


def perm_of(abscol):
    return (iota((HID, HID), 1) == abscol[...]).astype(BF16)


def fine_kernel(hist, later, flags, look, lens, th, w1, x_top, x_low, btab_t, ftab, ftab_t, offs, abscol,
                res, dz1, dz1_p, fore, small, keep, send,
                acc, acc4, acc_loss, dz4, total, wr, offs_p, perm):
    cols = hist.shape[1]
    step = pl.program_id(0)

    @pl.when(step == 0)
    def _():
        acc[...] = jnp.zeros_like(acc)
        acc4[...] = jnp.zeros_like(acc4)
        acc_loss[...] = jnp.zeros_like(acc_loss)
        perm[...] = perm_of(abscol)
        wr[0 : HID // 2, :] = x_top[...]
        wr[HID // 2 : HID, :] = x_low[...]
        wr[:, R_M3:R_OUT] = mm(wr[:, R_M3:R_OUT], perm[...], NT).astype(BF16)
        offs_p[...] = mm_exact2(perm[...], offs[0:HID, :])
        total[...] = jnp.zeros_like(total)
        dz4[OUTLOOK:O_PAD, :] = jnp.zeros((O_PAD - OUTLOOK, cols), BF16)

    inv = look[0:1, :]
    cinv = look[1:2, :]
    begin = LOOKBACK - lens[...]
    th_hi = th[...]
    res[LOOKBACK:T_PAD, :] = jnp.zeros((T_PAD - LOOKBACK, cols), BF16)
    h1 = offs[0:HID, 0:1]
    for at in range(0, T_LIVE, 1024):
        end = min(at + 1024, T_LIVE)
        live = min(end, LOOKBACK)
        shift = mm(btab_t[at:live, :], th_hi)
        for lo in range(at, live, 512):
            width = min(512, live - lo)
            r = hist[lo : lo + width, :] * inv - shift[lo - at : lo - at + width]
            res[lo : lo + width, :] = mask_rows(r, lo, begin).astype(BF16)
        h1 = h1 + mm(w1[:, at:end], res[at:end, :])
    v1, u1 = activate(h1)
    b1 = v1.astype(BF16)
    h2 = mm(wr[:, R_M2:R_M3], b1) + offs_p[:, 1:2]
    v2, u2 = activate(h2)
    b2 = v2.astype(BF16)
    h3 = mm(wr[:, R_M3:R_OUT], b2) + offs_p[:, 2:3]
    v3, u3 = activate(h3)
    b3 = v3.astype(BF16)
    est = mm(wr[:, R_OUT:R_ALL], b3, TN) + mm(ftab_t[...], th_hi) + offs[:, 3:4]
    counted = flags[...].astype(F32)
    err = (est[0:OUTLOOK] - (later[...] * inv - cinv)) * counted
    acc_loss[0:1, :] += jnp.sum(err * err, 0, keepdims=True)
    acc_loss[1:2, :] += jnp.sum(counted, 0, keepdims=True)
    d4 = (2.0 * err).astype(BF16)
    acc4[0:OUTLOOK, :] += fold_lanes(d4.astype(F32))
    dz4[0:OUTLOOK, :] = d4
    d4 = dz4[...]
    fore[...] = jnp.zeros_like(fore)
    fore[FORE_ROWS, :] = mm(ftab[FORE_ROWS, :], d4) * (1.0 / 48.0)

    def back(upstream, slope, row):
        d = (upstream * slope).astype(BF16)
        acc[row] += fold_lanes(d.astype(F32))
        return d

    d3 = back(mm(wr[:, R_OUT:R_ALL], d4), slope_once(h3, u3, v3), 2)
    total[:, R_OUT:R_ALL] += mm(b3, d4, NT)
    d2 = back(mm(wr[:, R_M3:R_OUT], d3, TN), slope_twice(h2, u2, v2), 1)
    total[:, R_M3:R_OUT] += mm(d3, b2, NT)
    d1 = back(mm(wr[:, R_M2:R_M3], d2, TN), slope_twice(h1, u1, v1), 0)
    dz1[...] = d1
    dz1_p[...] = mm(perm[...], d1).astype(BF16)
    total[:, R_M2:R_M3] += mm(d2, b1, NT)

    @pl.when(step == pl.num_programs(0) - 1)
    def _():
        small[...] = last_row(acc4[...])
        loss = jnp.sum(acc_loss[0:1, :], 1, keepdims=True)
        tally = jnp.sum(acc_loss[1:2, :], 1, keepdims=True)
        row = iota((8, O_PAD), 0)
        small[...] = jnp.where(
            row == 3,
            small[...],
            jnp.where(row == 4, loss, jnp.where(row == 5, tally, 0.0)),
        )
        half = HID // 2
        for cols_k in (slice(R_M2, R_M3), slice(R_M3, R_OUT), slice(R_OUT, R_ALL)):
            g = total[:, cols_k]
            if cols_k.start == R_M3:
                g = natural_columns(g, perm[...])
            keep[:, cols_k] = g[0:half]
            send[:, cols_k] = g[half:HID].astype(BF16)
        small[0:3, 0:HID] = hidden_rows(acc, perm[...])[0:3]
        small[0:1, 0:HID] = last_row(acc[0])[0:1]


def natural_columns(g, perm):
    half = HID // 2
    hi = g.astype(BF16)
    low = (g - hi.astype(F32)).astype(BF16)
    out = mm(hi, perm)
    return jnp.concatenate([out[0:half] + mm(low[0:half], perm), out[half:HID]], 0)


def fine_in_grad_kernel(dz1, res, rest_keep, rest_send, keep, send):
    step = pl.program_id(0)
    tile = keep.shape[1]
    whole = T_PAD // tile
    half = HID // 2

    def product(width):
        for lo in range(0, width, 512):
            end = min(lo + 512, width)
            g = jnp.transpose(mm(res[lo:end, :], dz1[...], NT), (1, 0))
            keep[:, lo:end] = g[0:half]
            send[:, lo:end] = g[half:HID].astype(BF16)

    @pl.when(step < whole)
    def _():
        product(tile)

    for k in range(whole, F_ALL // tile):

        @pl.when(step == k)
        def _():
            edge = max(T_PAD - k * tile, 0)
            if edge:
                product(edge)
            begin = k * tile + edge - T_PAD
            keep[:, edge:tile] = rest_keep[:, begin : begin + tile - edge]
            send[:, edge:tile] = rest_send[:, begin : begin + tile - edge]


def back_kernel(first, final, *refs):
    dz1f, fore, lens, pooled, w1, btab, wc, abscol, offs_p = refs[:9]
    outs = refs[9 if first else 10 : -4]
    small = outs[-1]
    acc, acc4, total, back_grad = refs[-4:]
    cols = dz1f.shape[1]
    step = pl.program_id(0)

    @pl.when(step == 0)
    def _():
        acc[...] = jnp.zeros_like(acc)
        acc4[...] = jnp.zeros_like(acc4)
        total[...] = jnp.zeros_like(total) if first else refs[9][...]

    begin = LOOKBACK - lens[...]
    d1f = dz1f[...]
    back_grad[...] = jnp.zeros_like(back_grad)
    for at in range(0, T_LIVE, T_LIVE // 2):
        wide = mm(w1[:, at : at + T_LIVE // 2], d1f, TN)
        for lo in range(at, at + T_LIVE // 2, 512):
            width = min(512, at + T_LIVE // 2 - lo)
            d = mask_rows(wide[lo - at : lo - at + width], lo, begin).astype(BF16)
            first_knot = max(lo // RATIO - 1, 0) // 8 * 8
            last_knot = min(-(-(lo + width + RATIO) // RATIO), BACK)
            last_knot = -(-last_knot // 8) * 8
            knots = slice(first_knot, last_knot)
            back_grad[knots, :] += mm(btab[knots, lo : lo + width], d)
    row = iota((256, cols), 0)
    d4 = (jnp.where(row < BACK, back_grad[...] * (-2.0 / 48.0), 0.0) + fore[...]).astype(BF16)
    acc4[...] += fold_lanes(d4.astype(F32))

    def ahead(w, entering, k):
        h = mm(w, entering) + offs_p[:, k : k + 1]
        value, u = activate(h)
        return h, u, value, value.astype(BF16)

    p = pooled[...]
    h1, u1, v1, b1 = ahead(wc[:, C_IN : C_IN + HID], p, 0)
    h2, u2, v2, b2 = ahead(wc[:, C_M0:C_M1], b1, 1)
    h3, u3, v3, b3 = ahead(wc[:, C_M1:C_OUT], b2, 2)

    def back(upstream, slope, row):
        d = (upstream * slope).astype(BF16)
        acc[row] += fold_lanes(d.astype(F32))
        return d

    d3 = back(mm(wc[:, C_OUT:C_ALL], d4), slope_once(h3, u3, v3), 2)
    total[:, C_OUT:C_ALL] += mm(b3, d4, NT)
    d2 = back(mm(wc[:, C_M1:C_OUT], d3, TN), slope_twice(h2, u2, v2), 1)
    total[:, C_M1:C_OUT] += mm(d3, b2, NT)
    d1 = back(mm(wc[:, C_M0:C_M1], d2, TN), slope_twice(h1, u1, v1), 0)
    total[:, C_M0:C_M1] += mm(d2, b1, NT)
    total[:, C_IN:C_M0] += mm(d1, p, NT)

    @pl.when(step == pl.num_programs(0) - 1)
    def _():
        perm = perm_of(abscol)
        small[...] = jnp.zeros_like(small)
        small[0:3, :] = hidden_rows(acc, perm)[0:3]
        small[3:4, 0:256] = last_row(acc4[...])[0:1]
        if not final:
            outs[0][...] = total[...]
            return
        half = HID // 2
        for a, b in zip((C_IN, C_M0, C_M1, C_OUT), (C_M0, C_M1, C_OUT, C_ALL)):
            g = total[:, a:b]
            if a in (C_M0, C_M1):
                g = natural_columns(g, perm)
            outs[0][:, a:b] = g[0:half]
            outs[1][:, a:b] = g[half:HID].astype(BF16)


def adam_math(weight, mean_old, square_old, grad):
    mean_new = beta_first * mean_old + (1.0 - beta_first) * grad
    square_new = beta_second * square_old + (1.0 - beta_second) * grad * grad
    fix = (1.0 - beta_second**STEP) ** 0.5
    gain = learn_rate * fix / (1.0 - beta_first**STEP)
    weight_new = weight * (1.0 - learn_rate * weight_decay) - gain * mean_new / (
        jnp.sqrt(square_new) + adam_epsilon * fix
    )
    return weight_new, mean_new, square_new


def adam_kernel(dp, small, relrow, *refs):
    pieces, refs = refs[: 2 * dp], refs[2 * dp :]
    ins, biases, outs, bias_outs = refs[:15], refs[15:18], refs[18:33], refs[33:36]
    loss, tally, norm, grads, bias_grad = refs[36:]
    part = pieces[0].shape[0]
    share = dp * part
    order = [0, *range(2, dp + 1), 1, *range(dp + 1, 2 * dp)]
    for k, index in enumerate(order):
        piece = pieces[index]
        at, row = (0, k) if k < dp else (F_ALL, k - dp)
        grads[row * part : (row + 1) * part, at : at + piece.shape[1]] = piece[...].astype(F32)
    place = (iota((share, share), 1) == relrow[...]).astype(BF16)

    count = small[5:6, 0:1]
    sums = small[0:4, :]
    bias_square = jnp.sum(jnp.sum(sums * sums, 0, keepdims=True), 1, keepdims=True)
    grad_norm = jnp.sqrt(small[6:7, 0:1] + bias_square) / count
    s = clip_level / jnp.maximum(grad_norm, clip_level) / count
    loss[...] = small[4:5, 0:1]
    tally[...] = count
    norm[...] = grad_norm
    for k in range(3):
        bias_grad[:, k * HID : (k + 1) * HID] = small[k : k + 1, O_PAD : O_PAD + HID]
        bias_grad[:, (k + 3) * HID : (k + 4) * HID] = small[k : k + 1, 0:HID]
    last = 6 * HID + BACK + FORE
    bias_grad[:, 6 * HID : last] = small[3:4, O_PAD : O_PAD + BACK + FORE]
    bias_grad[:, last : last + OUTLOOK] = small[3:4, 0:OUTLOOK]
    for out, value in zip(
        bias_outs, adam_math(*(x[...] for x in biases), bias_grad[...] * s)
    ):
        out[...] = value

    def step(i, at, width, index):
        g = grads[:, at : at + width]
        hi = g.astype(BF16)
        low = (g - hi.astype(F32)).astype(BF16)
        grad = (mm(place, hi, TN) + mm(place, low, TN)) * s
        old = [ins[i + 5 * k][index] for k in range(3)]
        for k, value in enumerate(adam_math(*old, grad)):
            outs[i + 5 * k][index] = value

    every = slice(None)
    step(0, F_ALL + C_IN, LP, (every, every))
    step(1, F_ALL + C_M0, HID, 0)
    step(1, F_ALL + C_M1, HID, 1)
    step(1, T_PAD + R_M2, HID, 2)
    step(1, T_PAD + R_M3, HID, 3)
    step(2, F_ALL + C_OUT, BACK + FORE, (every, every))
    step(4, T_PAD + R_OUT, OUTLOOK, (every, every))
    for lo in range(0, LOOKBACK, 512):
        width = min(512, LOOKBACK - lo)
        step(3, lo, width, (every, slice(lo, lo + width)))


def interp_table(count, length, first_row, rows, cols):
    spots = np.clip((np.arange(length) + 0.5) * (count / length) - 0.5, 0.0, count - 1.0)
    table = np.maximum(0.0, 1.0 - np.abs(spots[None, :] - np.arange(count)[:, None]))
    out = np.zeros((rows, cols), np.float32)
    out[first_row : first_row + count, :length] = np.round(table * 48.0)
    return out


def assemble_kernel(plan, count, *refs):
    ins, outs = refs[:count], refs[count:]
    for which, begin, at, size, out in plan:
        outs[out][at : at + size, :] = ins[which][begin : begin + size, :]


def assemble(*outs):
    if any(n % 16 or b % 16 for out in outs for _, b, n in out):
        return [
            jnp.concatenate([x[b : b + n] for x, b, n in out], 0) for out in outs
        ]
    ins, plan, shapes = [], [], []
    for k, out in enumerate(outs):
        at = 0
        for x, begin, size in out:
            which = next((i for i, y in enumerate(ins) if y is x), len(ins))
            if which == len(ins):
                ins.append(x)
            plan.append((which, begin, at, size, k))
            at += size
        shapes.append(jax.ShapeDtypeStruct((at, out[0][0].shape[1]), out[0][0].dtype))
    def blocks(arrays):
        return [pl.BlockSpec(x.shape, lambda i: (0, 0)) for x in arrays]

    return pl.pallas_call(
        functools.partial(assemble_kernel, tuple(plan), len(ins)),
        grid=(1,),
        out_shape=tuple(shapes),
        in_specs=blocks(ins),
        out_specs=tuple(blocks(shapes)),
        compiler_params=vmem(63),
        cost_estimate=cost(1),
        name="assemble",
    )(*ins)


def add_rows(pairs, plan):
    sums = [keep + got.astype(F32) for keep, got in pairs]
    return [
        sums[which][begin : begin + size].astype(kind) for which, begin, size, kind in plan
    ]


def spec(shape, index):
    return pl.BlockSpec(shape, index)


def fixed(shape):
    return pl.BlockSpec(shape, lambda i: (0,) * len(shape), pipeline_mode=pl.Buffered(1))


def body(
    history, later_observed, lengths, counted_flags, series,
    coarse_in, middle, rough_final_matrix, fine_in, sharp_final_matrix, offset_vectors,
    coarse_in_mean, middle_mean, rough_final_first, fine_in_mean, sharp_final_first, biases_mean,
    coarse_in_square, middle_square, rough_final_second, fine_in_square, sharp_final_second,
    biases_square,
):
    dp, fsdp = lax.axis_size("dp"), lax.axis_size("fsdp")
    d_here, f_here = lax.axis_index("dp"), lax.axis_index("fsdp")
    rows = history.shape[0]
    share = HID // fsdp
    part = share // dp

    def exchange(x, bit_dp, bit_fsdp):
        return swap(x, dp, fsdp, bit_dp, bit_fsdp)

    def join(p, q):
        return jnp.concatenate([p, q], 0)

    here = f_here * share + d_here * part
    order = row_order(dp, fsdp)
    abscol = (jnp.asarray(order, jnp.int32) ^ here).reshape(HID, 1)
    together = lax.optimization_barrier

    def by_hidden(cin, mid, cout, fin, fout):
        return (cin.T, mid.transpose(0, 2, 1), cout, fin.T, fout)

    def one_step(arrays):
        return [
            pl.BlockSpec(x.shape, lambda i, n=len(x.shape): (0,) * n) for x in arrays
        ]

    shard_now = by_hidden(
        coarse_in, middle, rough_final_matrix, fine_in, sharp_final_matrix
    )

    x_part, w1_part = pl.pallas_call(
        pack_kernel,
        out_shape=(
            jax.ShapeDtypeStruct((part, C_ALL + R_ALL), BF16),
            jax.ShapeDtypeStruct((share, T_PAD), BF16),
        ),
        grid=(1,),
        in_specs=[pl.BlockSpec(memory_space=pltpu.SMEM)] + one_step(shard_now),
        out_specs=(
            pl.BlockSpec((part, C_ALL + R_ALL), lambda i: (0, 0)),
            pl.BlockSpec((share, T_PAD), lambda i: (0, 0)),
        ),
        compiler_params=vmem(63),
        cost_estimate=cost(1),
        name="pack_weights",
    )(d_here.reshape(1), *shard_now)

    hist = history.T
    lens = lengths.reshape(1, rows)
    series_row = series.reshape(1, rows)
    side = rows // 2
    calls = (1, 1, 2)

    def stats(which, lens_row, pool):
        count = 2
        unit = rows // (128 * count * sum(calls))
        steps = calls[which] * unit
        at = sum(calls[:which]) * unit

        def hist_spec(q):
            return spec((LOOKBACK, 128), lambda i: (0, (at + i) * count + q))

        def row_spec():
            return spec((1, 128 * count), lambda i: (0, at + i))

        return pl.pallas_call(
            functools.partial(stats_kernel, count),
            grid=(steps,),
            out_shape=(
                jax.ShapeDtypeStruct((HID, rows), F32),
                jax.ShapeDtypeStruct((8, SERIES), F32),
            ),
            in_specs=[hist_spec(q) for q in range(count)]
            + [row_spec(), row_spec()]
            + [pl.BlockSpec(memory_space=pl.ANY) for _ in pool],
            out_specs=(
                spec((HID, 128 * count), lambda i: (0, at + i)),
                pl.BlockSpec((8, SERIES), lambda i: (0, 0)),
            ),
            compiler_params=vmem(63),
            cost_estimate=cost(6),
            input_output_aliases={count + 2: 0} if pool else {},
            name="window_stats",
        )(*[hist] * count, lens_row, series_row, *pool)

    up, down = bits_of(dp), bits_of(dp)[::-1]
    near, *far = bits_of(fsdp)
    moves = [(0, bit) for bit in reversed(far)] + list(zip(down, up)) + [(0, near)]

    def cut_rows(x):
        half = x.shape[0] // 2
        return x[:half], x[half:]

    def add_over(table, steps):
        for bit_dp, bit_fsdp in steps:
            table = table + exchange(table, bit_dp, bit_fsdp)
        return table

    x = [x_part]
    pools, tables, table = [], [], None
    sums = [(0, bit) for bit in bits_of(fsdp)] + [(bit, 0) for bit in up]
    sums = [sums[1:3] + sums[:1], sums[3:]]
    for k, move in enumerate(moves[:-1]):
        along_dp = k >= len(far)
        if along_dp and len(x) == 1:
            x = list(cut_rows(x[0]))
        got = [exchange(h, b, 0) for h, b in zip(x, move)] if along_dp else [exchange(x[0], *move)]
        if k < len(calls):
            lens_row, *x = together((lens, *x))
            pool, this = stats(k, lens_row, pools[-1:])
            pools.append(pool)
            *got, this = together((*got, this))
            tables.append(this)
        elif sums:
            if table is None:
                table = sum(tables[1:], tables[0])
            table = add_over(table, sums.pop(0))
            *got, table = together((*got, table))
        if k == 0:
            w1_part, *got = together((w1_part, *got))
            w1 = lax.all_gather(w1_part, "fsdp", axis=0, tiled=True)
        if k < len(moves) - 2:
            x = [join(h, g) for h, g in zip(x, got)]
    x_top = jnp.concatenate([h for pair in zip(x, got) for h in pair], 0)
    x_low = exchange(x_top, *moves[-1])
    for steps in sums:
        table = add_over(table, steps)

    hidden = offset_vectors[: 6 * HID].reshape(6, HID)
    rough_bias = offset_vectors[6 * HID : 6 * HID + BACK + FORE]
    sharp_bias = offset_vectors[6 * HID + BACK + FORE :]

    def bias_cols(three, last, width):
        out = jnp.pad(three, ((0, 0), (0, width - HID)))
        out = join(out, jnp.pad(last, (0, width - last.shape[0]))[None])
        return jnp.pad(out, ((0, 4), (0, 0))).T

    coarse_offs = bias_cols(0.5 * hidden[:3], rough_bias, HID)
    fine_offs = bias_cols(0.5 * hidden[3:], sharp_bias, O_PAD)

    r = 512
    tiles = rows // r

    def col_spec(height, begin=0, last=tiles - 1):
        return spec((height, r), lambda i: (0, jnp.minimum(begin + i, last)))

    wide_r = 2 * r if rows % (2 * r) == 0 else r

    def wide_spec(height):
        return spec((height, wide_r), lambda i: (0, i))

    half_block = pl.BlockSpec(
        (HID // 2, C_ALL), lambda i: (0, 0), pipeline_mode=pl.Buffered(1)
    )
    pooled, th, look, wc, offs_p = pl.pallas_call(
        coarse_kernel,
        grid=(rows // wide_r,),
        out_shape=(
            jax.ShapeDtypeStruct((HID, rows), BF16),
            jax.ShapeDtypeStruct((256, rows), BF16),
            jax.ShapeDtypeStruct((8, rows), F32),
            jax.ShapeDtypeStruct((HID, C_ALL), BF16),
            jax.ShapeDtypeStruct((HID, 8), F32),
        ),
        in_specs=[
            wide_spec(HID),
            wide_spec(1),
            wide_spec(1),
            fixed((8, SERIES)),
            half_block,
            half_block,
            fixed((HID, 8)),
            fixed((HID, 1)),
        ],
        out_specs=(
            wide_spec(HID),
            wide_spec(256),
            wide_spec(8),
            pl.BlockSpec((HID, C_ALL), lambda i: (0, 0)),
            pl.BlockSpec((HID, 8), lambda i: (0, 0)),
        ),
        scratch_shapes=[pltpu.VMEM((16, SERIES), BF16)],
        compiler_params=vmem(63),
        cost_estimate=cost(10),
        name="coarse_forward",
    )(
        pools[-1], lens, series_row, table, x_top, x_low, coarse_offs, abscol,
    )
    back_table = interp_table(BACK, LOOKBACK, 0, 256, T_PAD)
    btab = jnp.asarray(back_table, BF16)
    back_table[CINV_AT : CINV_AT + 3, :LOOKBACK] = 1.0
    btab_t = jnp.asarray(back_table.T, BF16)
    fore_table = interp_table(FORE, OUTLOOK, BACK, 256, O_PAD)
    ftab = jnp.asarray(fore_table, BF16)
    ftab_t = jnp.asarray(fore_table.T, BF16)

    tall = jax.ShapeDtypeStruct((HID, rows), BF16)
    r_shapes = (
        jax.ShapeDtypeStruct((HID // 2, R_ALL), F32),
        jax.ShapeDtypeStruct((HID // 2, R_ALL), BF16),
    )
    rest_block = pl.BlockSpec(
        (HID // 2, R_ALL), lambda i: (0, 1), pipeline_mode=pl.Buffered(1)
    )
    res, dz1, dz1_p, fore, f_small, r_keep, r_send = pl.pallas_call(
        fine_kernel,
        grid=(tiles,),
        out_shape=(
            jax.ShapeDtypeStruct((T_PAD, rows), BF16),
            tall,
            tall,
            jax.ShapeDtypeStruct((256, rows), F32),
            jax.ShapeDtypeStruct((8, O_PAD), F32),
            *r_shapes,
        ),
        in_specs=[
            col_spec(LOOKBACK),
            col_spec(OUTLOOK),
            col_spec(OUTLOOK),
            col_spec(8),
            col_spec(1),
            col_spec(256),
            fixed((HID, T_PAD)),
            rest_block,
            rest_block,
            fixed((T_PAD, 256)),
            fixed((256, O_PAD)),
            fixed((O_PAD, 256)),
            fixed((O_PAD, 8)),
            fixed((HID, 1)),
        ],
        out_specs=(
            col_spec(T_PAD),
            col_spec(HID),
            col_spec(HID),
            col_spec(256),
            pl.BlockSpec((8, O_PAD), lambda i: (0, 0)),
            *[pl.BlockSpec((HID // 2, R_ALL), lambda i: (0, 0))] * 2,
        ),
        scratch_shapes=[
            pltpu.VMEM((3, HID, 128), F32),
            pltpu.VMEM((O_PAD, 128), F32),
            pltpu.VMEM((8, r), F32),
            pltpu.VMEM((O_PAD, r), BF16),
            pltpu.VMEM((HID, R_ALL), F32),
            pltpu.VMEM((HID, R_ALL), BF16),
            pltpu.VMEM((HID, 8), F32),
            pltpu.VMEM((HID, HID), BF16),
        ],
        compiler_params=vmem(63),
        cost_estimate=cost(40),
        name="fine_block",
    )(
        hist, later_observed.T, counted_flags.T, look, lens, th,
        w1, x_top, x_low, btab_t, ftab, ftab_t, fine_offs, abscol,
    )

    wide = F_ALL // 4
    res_last = -(-T_PAD // wide) - 1

    f_keep, f_send = pl.pallas_call(
        fine_in_grad_kernel,
        grid=(F_ALL // wide,),
        out_shape=tuple(
            jax.ShapeDtypeStruct((HID // 2, F_ALL), kind) for kind in (F32, BF16)
        ),
        in_specs=[
            fixed((HID, rows)),
            spec((wide, rows), lambda i: (jnp.minimum(i, res_last), 0)),
            fixed((HID // 2, R_ALL)),
            fixed((HID // 2, R_ALL)),
        ],
        out_specs=tuple([spec((HID // 2, wide), lambda i: (0, i))] * 2),
        compiler_params=vmem(54),
        cost_estimate=cost(12),
        name="fine_in_grad",
    )(dz1_p, res, r_keep, r_send)

    def backward(at, steps, fore, before):
        first = not before
        final = at + steps == tiles
        half = HID // 2
        shapes = (
            [jax.ShapeDtypeStruct((HID, C_ALL), F32)]
            if not final
            else [jax.ShapeDtypeStruct((half, C_ALL), t) for t in (F32, BF16)]
        ) + [jax.ShapeDtypeStruct((8, HID), F32)]

        def rows_of(height):
            return col_spec(height, at)

        return pl.pallas_call(
            functools.partial(back_kernel, first, final),
            grid=(steps,),
            out_shape=tuple(shapes),
            in_specs=[
                rows_of(HID),
                rows_of(256),
                rows_of(1),
                rows_of(HID),
                fixed((HID, T_PAD)),
                fixed((256, T_PAD)),
                fixed((HID, C_ALL)),
                fixed((HID, 1)),
                fixed((HID, 8)),
            ]
            + [fixed(x.shape) for x in before],
            out_specs=tuple(pl.BlockSpec(s.shape, lambda i: (0, 0)) for s in shapes),
            scratch_shapes=[
                pltpu.VMEM((3, HID, 128), F32),
                pltpu.VMEM((256, 128), F32),
                pltpu.VMEM((HID, C_ALL), F32),
                pltpu.VMEM((256, r), F32),
            ],
            compiler_params=vmem(36),
            cost_estimate=cost(17),
            name="coarse_backward",
        )(dz1, fore, lens, pooled, w1, btab, wc, abscol, offs_p, *before)

    legs = [(0, near)] + list(zip(up, down)) + [(0, bit) for bit in far]

    def split(j):
        return 1 <= j <= len(up)

    def sum_and_cut(pairs, j):
        n = pairs[0][0].shape[0]
        if j + 1 == len(legs):
            plan = [(0, 0, n, F32)]
        elif not split(j + 1):
            plan = [(0, 0, n, F32), (1, 0, n, BF16)] if len(pairs) == 2 else [
                (0, 0, n // 2, F32), (0, n // 2, n // 2, BF16)
            ]
        else:
            size = n // 2 if len(pairs) == 2 else n // 4
            plan = []
            for k in range(2):
                which, begin = (k, 0) if len(pairs) == 2 else (0, 2 * k * size)
                plan += [(which, begin, size, F32), (which, begin + size, size, BF16)]
        flat = add_rows(pairs, plan)
        return [tuple(flat[k : k + 2]) for k in range(0, len(flat), 2)]

    def travel(state, j):
        if split(j):
            return [exchange(send, bit, 0) for (_, send), bit in zip(state, legs[j])]
        return [exchange(state[0][1], *legs[j])]

    def kept(state, got):
        return [(pair[0], g) for pair, g in zip(state, got)]

    def beside(got, *others):
        return together((*got, *others))[: len(got)]

    def hold(state, value):
        return together((value, *(x for pair in state for x in pair)))[0]

    state, got = [(f_keep, f_send)], [exchange(f_send, 0, near)]
    quarter = max(tiles // 4, 1)
    smalls, c_part, at = [], (), 0
    for j, count in enumerate((quarter, tiles - 2 * quarter, quarter)):
        if j:
            got = travel(state, j)
        *c_part, this = backward(at, count, hold(state, fore), tuple(c_part))
        smalls.append(this)
        at += count
        both = together((*got, *c_part))
        got, c_part = both[: len(got)], both[len(got) :]
        state = sum_and_cut(kept(state, got), j)
    f_state, f_leg = state, 3
    c_keep, c_send = c_part
    c_small = sum(smalls[1:], smalls[0])

    def advance(f_state, f_got, f_leg):
        f_state = sum_and_cut(kept(f_state, f_got), f_leg)
        f_leg += 1
        return f_state, travel(f_state, f_leg) if f_leg < len(legs) else None, f_leg

    def share_out(part):
        return [part] + [exchange(part, d, 0) for d in range(1, dp)]

    c_got = exchange(c_send, 0, near)
    f_got = travel(f_state, f_leg)
    c_state = sum_and_cut([(c_keep, c_got)], 0)
    f_all = None
    for j in range(1, len(legs)):
        got = travel(c_state, j)
        c_state = sum_and_cut(kept(c_state, got), j)
        if f_got is not None and j != 2:
            f_state, f_got, f_leg = advance(f_state, beside(f_got, *c_state[0]), f_leg)
            if f_got is None:
                gf_part = f_state[0][0]
                f_all = share_out(gf_part.astype(BF16))
        elif f_got is None:
            f_all = beside(f_all, *c_state[0])
    while f_got is not None:
        f_state, f_got, f_leg = advance(f_state, f_got, f_leg)
    if f_all is None:
        gf_part = f_state[0][0]
        f_all = share_out(gf_part.astype(BF16))
    gc_part = c_state[0][0]
    c_all = share_out(gc_part)

    rel = np.concatenate([np.arange(part) ^ (d * part) for d in range(dp)])
    relrow = (jnp.asarray(rel, jnp.int32) ^ (d_here * part)).reshape(share, 1)

    squares = jnp.sum(gf_part * gf_part) + jnp.sum(gc_part * gc_part)
    small = jnp.concatenate([f_small, c_small], 1)
    small = jnp.where(
        (iota(small.shape, 0) == 6) & (iota(small.shape, 1) == 0), squares, small
    )
    small = add_over(small, [(bit, 0) for bit in up] + [(0, near)])
    *c_all, small = together((*c_all, small))
    small = add_over(small, [(0, bit) for bit in far])
    pieces = [f_all[0], c_all[0], *f_all[1:], *c_all[1:]]
    shards = (
        *shard_now,
        *by_hidden(
            coarse_in_mean, middle_mean, rough_final_first, fine_in_mean, sharp_final_first
        ),
        *by_hidden(
            coarse_in_square, middle_square, rough_final_second, fine_in_square,
            sharp_final_second,
        ),
    )
    biases = [x.reshape(1, -1) for x in (offset_vectors, biases_mean, biases_square)]
    given = (small, relrow, *pieces, *shards, *biases)
    results = tuple(jax.ShapeDtypeStruct(x.shape, F32) for x in (*shards, *biases)) + (
        jax.ShapeDtypeStruct((1, 1), F32),
    ) * 3
    new = pl.pallas_call(
        functools.partial(adam_kernel, dp),
        out_shape=results,
        grid=(1,),
        in_specs=one_step(given),
        out_specs=tuple(one_step(results)),
        scratch_shapes=[
            pltpu.VMEM((share, F_ALL + C_ALL), F32),
            pltpu.VMEM(biases[0].shape, F32),
        ],
        compiler_params=vmem(63),
        cost_estimate=cost(6),
        name="adam",
    )(*given)
    return (
        *(x.reshape(()) for x in new[18:21]),
        *by_hidden(*new[0:5]), new[15].reshape(-1),
        *by_hidden(*new[5:10]), new[16].reshape(-1),
        *by_hidden(*new[10:15]), new[17].reshape(-1),
    )


def solution(mesh):
    rows2 = P(("dp", "fsdp"), None)
    rows1 = P(("dp", "fsdp"))
    weights = (P(None, "fsdp"), P(None, None, "fsdp"), P("fsdp", None), P(None, "fsdp"), P("fsdp", None), P())
    in_specs = (rows2, rows2, rows1, rows2, rows1) + weights * 3
    out_specs = (P(), P(), P()) + weights * 3
    return jax.shard_map(body, mesh=mesh, in_specs=in_specs, out_specs=out_specs, check_vma=False)
```
